128 devices in a mesh: dp: 2 (over y_lo), row: 2 (over y_hi), col: 32 (over z, x, core).
Axes of the slice: x: 4, y: 4 (y_hi: 2, y_lo: 2; y = y_hi * 2 + y_lo), z: 4, core: 2. Of those that a mesh axis runs over, the one named last changes fastest.
Arguments:
- expanded: bfloat16 [4, 64, 32, 32, 1024], P('dp', ('row', 'col')), may hold values from -6 to 6
- skip: bfloat16 [4, 64, 32, 32, 256], P('dp', ('row', 'col')), may hold values from -6 to 6
- cotangent: bfloat16 [4, 64, 32, 32, 256], P('dp', ('row', 'col')), may hold values from -6 to 6
- depth_kernel: float32 [3, 3, 1024], replicated, may hold values from -2 to 2
- w_proj: bfloat16 [1024, 256], replicated, may hold values from -0.1875 to 0.1875
- norm_gain: float32 [256], replicated, may hold values from 0.5 to 1.5
- w_qkv: bfloat16 [256, 768], replicated, may hold values from -1 to 1
- w_out: bfloat16 [256, 256], replicated, may hold values from -0.375 to 0.375
Outputs:
- grad_expanded: bfloat16 [4, 64, 32, 32, 1024], P('dp', ('row', 'col'))
- grad_skip: bfloat16 [4, 64, 32, 32, 256], P('dp', ('row', 'col'))
- grad_kernel: float32 [3, 3, 1024], replicated
- grad_proj: float32 [1024, 256], replicated
- grad_wqkv: float32 [256, 768], replicated
- grad_out: float32 [256, 256], replicated
- grad_gain: float32 [256], replicated
The draws below stay inside these ranges and needn't reach their ends.
All inputs are finite; a program needn't handle non-finite values.
Results may differ from the reference program's by a relative error of at most 0.023.
The reference program's roundings to bfloat16 on the way count: a program that leaves them out, or rounds other values in their place, can miss the bound.
Values may be sent and summed in bfloat16 or wider, within the bound.
A program may use at most 192 MiB of HBM per device.

```python
import math
import jax
import jax.numpy as jnp
from jax import lax

WIDTH = 256
EXPAND = 1024
HEADS = 8
GRID = 8
TILE_ROWS = 32
TILE_COLS = 32
TILES = 64
ROW_TILES = 8
BATCH = 4
ROWS = 256
COLS = 256


def draw_w_qkv(key, part):
    key = jax.random.fold_in(key, 11)
    matrix = jax.random.truncated_normal(key, -4.0, 4.0, (WIDTH, 3 * WIDTH), jnp.float32) / math.sqrt(WIDTH)
    return matrix.astype(jnp.bfloat16)


def shard_levels(key, shape, pieces, least, high):
    def one(dim, blocks):
        steps = jax.random.uniform(jax.random.fold_in(jax.random.fold_in(key, 6), dim), (blocks,), jnp.float32, least / len(pieces), high / len(pieces))
        return jnp.repeat(jnp.exp(steps), shape[dim] // blocks).reshape((-1,) + (1,) * (len(shape) - dim - 1))

    factor_of = one(*pieces[0])
    for cut in pieces[1:]:
        factor_of = factor_of * one(*cut)
    return factor_of


def normal_values(stream_key, shape, deviation, most, cuts=(), dtype=jnp.bfloat16):
    gain = shard_levels(stream_key, shape, cuts, -0.22, 0.18) if cuts else 1.0
    values = jax.random.normal(stream_key, shape, jnp.float32) * deviation * gain
    return jnp.minimum(jnp.maximum(values, -most), most).astype(dtype)


def setup_inputs(seed: int = 0) -> dict:
    keys = jax.random.split(jax.random.key(seed), 9)
    return {
        "expanded": normal_values(keys[0], (BATCH, TILES, TILE_ROWS, TILE_COLS, EXPAND), 1.0, 6.0, ((0, 2), (1, 64))),
        "skip": normal_values(keys[1], (BATCH, TILES, TILE_ROWS, TILE_COLS, WIDTH), 1.0, 6.0, ((0, 2), (1, 64))),
        "cotangent": normal_values(keys[2], (BATCH, TILES, TILE_ROWS, TILE_COLS, WIDTH), 1.0, 6.0, ((0, 2), (1, 64))),
        "depth_kernel": normal_values(keys[3], (3, 3, EXPAND), 9 ** -0.5, 2.0, (), jnp.float32),
        "w_proj": normal_values(keys[4], (EXPAND, WIDTH), EXPAND ** -0.5, 0.1875),
        "norm_gain": jnp.clip(1.0 + 0.1 * jax.random.normal(keys[5], (WIDTH,), jnp.float32), 0.5, 1.5),
        "w_qkv": draw_w_qkv(jax.random.fold_in(keys[8], 71), 0),
        "w_out": normal_values(keys[7], (WIDTH, WIDTH), WIDTH ** -0.5, 0.375),
    }


def contract(pattern, left_op, right_op):
    return jnp.einsum(pattern, left_op.astype(jnp.float32), right_op.astype(jnp.float32))

def transposed_dot(left_op, right_op):
    return lax.dot_general(left_op.astype(jnp.float32), right_op.astype(jnp.float32), (((0,), (0,)), ((), ())))

def smooth(inside):
    return jax.nn.gelu(inside, approximate=True)

def depthwise(padded, kernel, n_rows, n_cols):
    summed = jnp.zeros(padded.shape[:-3] + (n_rows, n_cols, padded.shape[-1]), jnp.float32)
    for row_off in range(3):
        for col_off in range(3):
            summed = summed + kernel[row_off, col_off] * padded[..., row_off:row_off + n_rows, col_off:col_off + n_cols, :].astype(jnp.float32)
    return summed

def depthwise_back(padded_grad, kernel, n_rows, n_cols):
    summed = jnp.zeros(padded_grad.shape[:-3] + (n_rows, n_cols, padded_grad.shape[-1]), jnp.float32)
    for row_off in range(3):
        for col_off in range(3):
            summed = summed + kernel[row_off, col_off] * padded_grad[..., 2 - row_off:2 - row_off + n_rows, 2 - col_off:2 - col_off + n_cols, :].astype(jnp.float32)
    return summed

def kernel_grad(grad_pre, padded, n_rows, n_cols):
    grad_float = grad_pre.astype(jnp.float32)
    lead_axes = tuple(range(grad_float.ndim - 1))
    stacked = []
    for row_off in range(3):
        row_terms = []
        for col_off in range(3):
            window = padded[..., row_off:row_off + n_rows, col_off:col_off + n_cols, :].astype(jnp.float32)
            row_terms.append(lax.optimization_barrier(jnp.sum(grad_float * window, axis=lead_axes)))
        stacked.append(jnp.stack(row_terms))
    return jnp.stack(stacked)

def attend_back(mixture, cotangent, norm_gain, w_qkv, w_out, n_heads):
    groups, length, model_dim = mixture.shape
    head_size = model_dim // n_heads
    score_scale = 1.0 / math.sqrt(head_size)
    mix_float = mixture.astype(jnp.float32)
    inverse = lax.rsqrt(lax.optimization_barrier(jnp.mean(mix_float * mix_float, axis=-1, keepdims=True)) + 1e-06)
    normed = (mix_float * inverse * norm_gain).astype(jnp.bfloat16)
    flat_norm = normed.reshape(groups * length, model_dim)
    proj_qkv = jnp.dot(flat_norm, w_qkv, preferred_element_type=jnp.float32).astype(jnp.bfloat16)
    proj_qkv = proj_qkv.reshape(groups, length, 3, n_heads, head_size)
    queries = proj_qkv[:, :, 0]
    key_rows = proj_qkv[:, :, 1]
    values = proj_qkv[:, :, 2]
    scores = contract('gqhd,gkhd->ghqk', queries, key_rows) * score_scale
    attn_probs = jax.nn.softmax(scores, axis=-1)
    weights_bf = attn_probs.astype(jnp.bfloat16)
    attended = contract('ghqk,gkhd->gqhd', weights_bf, values).astype(jnp.bfloat16)
    attended = attended.reshape(groups * length, model_dim)
    flat_cot = cotangent.reshape(groups * length, model_dim)
    grad_out = transposed_dot(attended, flat_cot)
    grad_att = jnp.dot(flat_cot, w_out.T, preferred_element_type=jnp.float32).astype(jnp.bfloat16)
    grad_att = grad_att.reshape(groups, length, n_heads, head_size)
    grad_values = contract('ghqk,gqhd->gkhd', weights_bf, grad_att)
    grad_probs = contract('gqhd,gkhd->ghqk', grad_att, values)
    grad_scores = attn_probs * (grad_probs - lax.optimization_barrier(jnp.sum(grad_probs * attn_probs, axis=-1, keepdims=True))) * score_scale
    grad_scores = grad_scores.astype(jnp.bfloat16)
    grad_query = contract('ghqk,gkhd->gqhd', grad_scores, key_rows)
    grad_keys = contract('ghqk,gqhd->gkhd', grad_scores, queries)
    grad_qkv = jnp.stack([grad_query, grad_keys, grad_values], axis=2).astype(jnp.bfloat16)
    grad_qkv = grad_qkv.reshape(groups * length, 3 * model_dim)
    grad_wqkv = transposed_dot(flat_norm, grad_qkv)
    grad_normed = jnp.dot(grad_qkv, w_qkv.T, preferred_element_type=jnp.float32).reshape(groups, length, model_dim)
    grad_gain = lax.optimization_barrier(jnp.sum(grad_normed * mix_float * inverse, axis=(0, 1)))
    scaled = grad_normed * norm_gain
    grad_mix = inverse * scaled - mix_float * inverse * inverse * inverse * lax.optimization_barrier(jnp.mean(scaled * mix_float, axis=-1, keepdims=True))
    summed = (cotangent.astype(jnp.float32) + grad_mix).astype(jnp.bfloat16)
    return (summed, grad_wqkv, grad_out, grad_gain)

def reference(expanded, skip, cotangent, depth_kernel, w_proj, norm_gain, w_qkv, w_out):
    span_a = ROWS // GRID
    span_b = COLS // GRID

    def to_picture(tiled):
        channels = tiled.shape[-1]
        tiled = tiled.reshape(ROW_TILES, GRID, TILE_ROWS, TILE_COLS, channels).transpose(0, 2, 1, 3, 4)
        return tiled.reshape(ROWS, COLS, channels)

    def to_tiles(picture):
        channels = picture.shape[-1]
        picture = picture.reshape(ROW_TILES, TILE_ROWS, GRID, TILE_COLS, channels).transpose(0, 2, 1, 3, 4)
        return picture.reshape(TILES, TILE_ROWS, TILE_COLS, channels)

    def to_groups(tensor):
        channels = tensor.shape[-1]
        tensor = tensor.reshape(GRID, span_a, GRID, span_b, channels).transpose(1, 3, 0, 2, 4)
        return tensor.reshape(span_a * span_b, GRID * GRID, channels)

    def from_groups(tensor):
        channels = tensor.shape[-1]
        tensor = tensor.reshape(span_a, span_b, GRID, GRID, channels).transpose(2, 0, 3, 1, 4)
        return tensor.reshape(ROWS, COLS, channels)

    def per_picture(running, slices_in):
        picture = to_picture(slices_in[0])
        skip_in = to_picture(slices_in[1])
        grad_in = to_picture(slices_in[2])
        padded = jnp.pad(picture, ((1, 1), (1, 1), (0, 0)))
        pre_act = depthwise(padded, depth_kernel, ROWS, COLS)
        activated = smooth(pre_act).astype(jnp.bfloat16)
        flat_act = activated.reshape(ROWS * COLS, EXPAND)
        mixture = (skip_in.astype(jnp.float32) + jnp.dot(flat_act, w_proj, preferred_element_type=jnp.float32).reshape(ROWS, COLS, WIDTH)).astype(jnp.bfloat16)
        summed, g_qkv, g_out, g_gain = attend_back(to_groups(mixture), to_groups(grad_in), norm_gain, w_qkv, w_out, HEADS)
        grad_skip = from_groups(summed)
        flat_grad = grad_skip.reshape(ROWS * COLS, WIDTH)
        g_proj = transposed_dot(flat_act, flat_grad)
        grad_act = jnp.dot(flat_grad, w_proj.T, preferred_element_type=jnp.float32).reshape(ROWS, COLS, EXPAND)
        _, pullback = jax.vjp(smooth, pre_act)
        grad_pre = pullback(grad_act)[0].astype(jnp.bfloat16)
        g_kernel = kernel_grad(grad_pre, padded, ROWS, COLS)
        grad_padded = jnp.pad(grad_pre, ((1, 1), (1, 1), (0, 0)))
        grad_picture = depthwise_back(grad_padded, depth_kernel, ROWS, COLS).astype(jnp.bfloat16)
        running = (running[0] + g_kernel, running[1] + g_proj, running[2] + g_qkv, running[3] + g_out, running[4] + g_gain)
        return (running, (to_tiles(grad_picture), to_tiles(grad_skip)))
    zeros_init = (jnp.zeros((3, 3, EXPAND), jnp.float32), jnp.zeros((EXPAND, WIDTH), jnp.float32), jnp.zeros((WIDTH, 3 * WIDTH), jnp.float32), jnp.zeros((WIDTH, WIDTH), jnp.float32), jnp.zeros((WIDTH,), jnp.float32))
    summed_grads, outputs = lax.scan(per_picture, zeros_init, (expanded, skip, cotangent))
    grad_expanded, grad_skip = outputs
    factor = 1.0 / math.sqrt(BATCH * ROWS * COLS)
    return (grad_expanded, grad_skip, summed_grads[0] * factor, summed_grads[1] * factor, summed_grads[2] * factor, summed_grads[3] * factor, summed_grads[4] * factor)
```

```python
import math

import jax
import jax.numpy as jnp
import numpy as np
from jax import lax
from jax.experimental import pallas as pl
from jax.experimental.pallas import tpu as pltpu
from jax.sharding import PartitionSpec as P

GRID = 8
TILES = 64
ROWS = 32
COLS = 32
LANES = 128
WIDTH = 256
EXPAND = 1024
LANE_BLOCKS = EXPAND // LANES
BAND = 4
BANDS = ROWS // BAND
BAND_CELLS = BAND * COLS
BAND_TILES = TILES // BANDS
F32 = jnp.float32
BF16 = jnp.bfloat16
MESH_ID = pl.DeviceIdType.MESH
GELU_1 = math.sqrt(2.0 / math.pi)
GELU_3 = GELU_1 * 0.044715


def dot(a, b):
    return lax.dot_general(a, b, (((1,), (0,)), ((), ())), preferred_element_type=F32)


def dot_t(a, b):
    return lax.dot_general(a, b, (((1,), (1,)), ((), ())), preferred_element_type=F32)


def dot_tl(a, b):
    return lax.dot_general(a, b, (((0,), (0,)), ((), ())), preferred_element_type=F32)


def tile_id(tile):
    return {"row": tile // 32, "col": lax.rem(tile, 32)}


def my_tile():
    return lax.axis_index("row") * 32 + lax.axis_index("col")


def neighbours(me):
    tile_row, tile_col = me // GRID, lax.rem(me, GRID)
    found = {}
    for down in (-1, 0, 1):
        for right in (-1, 0, 1):
            if (down, right) != (0, 0):
                found[down, right] = lax.rem(tile_row + down + GRID, GRID) * GRID + lax.rem(
                    tile_col + right + GRID, GRID
                )
    return found


SIDES = ((0, -1), (0, 1))
ENDS = ((-1, 0), (1, 0))
CORNERS = ((-1, -1), (-1, 1), (1, -1), (1, 1))
AROUND = SIDES + ENDS + CORNERS


def rim_copies(me, grid_ref, sides_out, sides_in, corners_out, corners_in, send_sem, recv_sem):
    around = neighbours(me)
    copies = []
    for n, (down, right) in enumerate(AROUND):
        if down == 0:
            source = sides_out.at[(right + 1) // 2]
            target = sides_in.at[(1 - right) // 2]
        elif right == 0:
            source = grid_ref.at[:, 1 if down < 0 else ROWS]
            target = grid_ref.at[:, ROWS + 1 if down < 0 else 0]
        else:
            place = CORNERS.index((down, right))
            source = corners_out.at[place]
            target = corners_in.at[3 - place]
        copies.append(
            pltpu.make_async_remote_copy(
                src_ref=source,
                dst_ref=target,
                send_sem=send_sem.at[n],
                recv_sem=recv_sem.at[n],
                device_id=tile_id(around[down, right]),
                device_id_type=MESH_ID,
            )
        )
    return copies


def collect_sides(grid_ref, sides_out, corners_out):
    for side in range(2):
        for picture in range(2):
            for start in range(0, ROWS, 16):
                window = grid_ref[picture, 1 + start : 17 + start, 16 * side : 16 * side + 16, :]
                column = window.astype(F32)[:, 15 * side, :]
                sides_out[side, picture, start : start + 16, :] = column.astype(BF16)
    for place, (down, right) in enumerate(CORNERS):
        edge = 0 if down < 0 else 16
        row = 0 if down < 0 else 15
        both = [
            sides_out[(right + 1) // 2, picture, edge : edge + 16, :].astype(F32)[row : row + 1]
            for picture in range(2)
        ]
        filler = jnp.zeros((14, EXPAND), F32)
        corners_out[place] = jnp.concatenate(both + [filler], axis=0).astype(BF16)


def clear_outside(me, grid_ref, sides_in, corners_in):
    tile_row, tile_col = me // GRID, lax.rem(me, GRID)
    for side, last in ((0, 0), (1, GRID - 1)):

        @pl.when(tile_col == last)
        def _():
            sides_in[side] = jnp.zeros(sides_in.shape[1:], BF16)
            corners_in[side] = jnp.zeros(corners_in.shape[1:], BF16)
            corners_in[2 + side] = jnp.zeros(corners_in.shape[1:], BF16)

    for end, last in ((0, 0), (1, GRID - 1)):

        @pl.when(tile_row == last)
        def _():
            grid_ref[:, (ROWS + 1) * end] = jnp.zeros((2, COLS, EXPAND), BF16)
            corners_in[2 * end] = jnp.zeros(corners_in.shape[1:], BF16)
            corners_in[2 * end + 1] = jnp.zeros(corners_in.shape[1:], BF16)


def column_stack(sides_in, corners_in, columns):
    for side in range(2):
        for picture in range(2):
            columns[side, picture, 0:8] = jnp.concatenate(
                [jnp.zeros((7, EXPAND), F32), corners_in[side].astype(F32)[picture : picture + 1]], axis=0
            )
            columns[side, picture, 8 : 8 + ROWS] = sides_in[side, picture].astype(F32)
            columns[side, picture, 40:48] = jnp.concatenate(
                [corners_in[2 + side].astype(F32)[picture : picture + 1], jnp.zeros((7, EXPAND), F32)], axis=0
            )


def column_terms(columns, weights, col_offs, terms):
    for side in range(2):
        for picture in range(2):
            total = None
            for row_off in range(3):
                term = (
                    weights(row_off, col_offs[side])
                    * columns[side, picture, 7 + row_off : 7 + row_off + ROWS, :]
                )
                total = term if total is None else total + term
            for band in range(BANDS):
                terms[side, picture, band, 0:BAND] = total[BAND * band : BAND * band + BAND]


def convolve(rows, weights, left, right):
    spot = lax.broadcasted_iota(jnp.int32, (BAND, COLS, LANES), 1)
    parts = []
    for col_off in range(3):
        total = None
        for row_off in range(3):
            term = weights[3 * row_off + col_off][None, :, :] * rows[row_off : row_off + BAND]
            total = term if total is None else total + term
        parts.append(total)
    from_left = jnp.where(spot == 0, left[:, None, :], pltpu.roll(parts[0], 1, 1))
    from_right = jnp.where(spot == COLS - 1, right[:, None, :], pltpu.roll(parts[2], COLS - 1, 1))
    return parts[1] + from_left + from_right


def forward_kernel(
    x_hbm, skip_ref, cot_hbm, kern_ref, wproj_ref,
    act_hbm, dg_hbm, got_mix, got_cot, ends_out, columns_out,
    grid, sides_out, sides_in, corners_out, corners_in, columns, terms, act, dg, mix,
    load_sem, rim_send, rim_recv, cot_send, cot_recv, mix_send, mix_recv, own_sem, store_sem,
):
    me = my_tile()
    load = pltpu.make_async_copy(x_hbm, grid.at[:, pl.ds(1, ROWS)], load_sem)
    load.start()
    barrier = pltpu.get_barrier_semaphore()

    def greet(i, carry):
        pl.semaphore_signal(
            barrier, inc=1, device_id=tile_id(lax.rem(me + i, TILES)), device_id_type=MESH_ID
        )
        return carry

    lax.fori_loop(1, TILES, greet, 0)
    load.wait()
    collect_sides(grid, sides_out, corners_out)
    pl.semaphore_wait(barrier, TILES - 1)
    rim = rim_copies(me, grid, sides_out, sides_in, corners_out, corners_in, rim_send, rim_recv)
    for copy in rim:
        copy.start()

    def cot_copy(target, slot):
        return pltpu.make_async_remote_copy(
            src_ref=cot_hbm.at[:, pl.ds(pl.multiple_of(target * 16, 16), 16), :],
            dst_ref=got_cot.at[:, pl.ds(pl.multiple_of(slot * 16, 16), 16), :],
            send_sem=cot_send.at[target],
            recv_sem=cot_recv.at[slot],
            device_id=tile_id(target),
            device_id_type=MESH_ID,
        )

    def mix_copy(target, slot):
        return pltpu.make_async_remote_copy(
            src_ref=mix.at[:, pl.ds(pl.multiple_of(target * 16, 16), 16), :],
            dst_ref=got_mix.at[:, pl.ds(pl.multiple_of(slot * 16, 16), 16), :],
            send_sem=mix_send.at[target],
            recv_sem=mix_recv.at[slot],
            device_id=tile_id(target),
            device_id_type=MESH_ID,
        )

    def send_cot(i, carry):
        cot_copy(lax.rem(me + i, TILES), me).start()
        return carry

    lax.fori_loop(1, TILES, send_cot, 0)
    own = pl.ds(pl.multiple_of(me * 16, 16), 16)
    own_cot = pltpu.make_async_copy(cot_hbm.at[:, own, :], got_cot.at[:, own, :], own_sem.at[0])
    own_cot.start()
    for copy in rim:
        copy.wait_recv()
    for copy in rim:
        copy.wait_send()
    clear_outside(me, grid, sides_in, corners_in)
    column_stack(sides_in, corners_in, columns)
    column_terms(
        columns, lambda a, c: kern_ref[3 * a + c : 3 * a + c + 1, :], (0, 2), terms
    )
    ends = pltpu.make_async_copy(grid.at[:, 0], ends_out.at[0], own_sem.at[1])
    ends.start()
    ends_low = pltpu.make_async_copy(grid.at[:, ROWS + 1], ends_out.at[1], own_sem.at[2])
    ends_low.start()
    cols = pltpu.make_async_copy(columns, columns_out, own_sem.at[3])
    cols.start()

    def band_copies(band):
        cells = pl.ds(pl.multiple_of(band * BAND_CELLS, BAND_CELLS), BAND_CELLS)
        return (
            pltpu.make_async_copy(act.at[:, cells, :], act_hbm.at[:, cells, :], store_sem.at[0, band]),
            pltpu.make_async_copy(dg.at[:, cells, :], dg_hbm.at[:, cells, :], store_sem.at[1, band]),
        )

    def do_band(step, carry):
        band = lax.rem(step + me // GRID, BANDS)
        first = band * BAND
        cells = pl.ds(pl.multiple_of(band * BAND_CELLS, BAND_CELLS), BAND_CELLS)

        def do_block(index, inner):
            picture, block = index // LANE_BLOCKS, lax.rem(index, LANE_BLOCKS)
            lanes = pl.ds(pl.multiple_of(block * LANES, LANES), LANES)
            rows = grid[picture, pl.ds(first, BAND + 2), :, lanes].astype(F32)
            weights = [kern_ref[n : n + 1, lanes] for n in range(9)]
            pre = convolve(
                rows,
                weights,
                terms[0, picture, band, 0:BAND, lanes],
                terms[1, picture, band, 0:BAND, lanes],
            )
            square = pre * pre
            tanh = jnp.tanh(pre * (GELU_1 + GELU_3 * square))
            half = 0.5 * pre
            activated = half + half * tanh
            slope = (0.5 + 0.5 * tanh) + half * (1.0 - tanh * tanh) * (GELU_1 + (3.0 * GELU_3) * square)
            act[picture, cells, lanes] = activated.astype(BF16).reshape(BAND_CELLS, LANES)
            dg[picture, cells, lanes] = slope.astype(BF16).reshape(BAND_CELLS, LANES)
            return inner

        lax.fori_loop(0, 2 * LANE_BLOCKS, do_block, 0)
        flat = act[:, cells, :].reshape(2 * BAND_CELLS, EXPAND)
        projected = dot(flat, wproj_ref[...]).reshape(2, BAND_CELLS, WIDTH)
        mix[:, cells, :] = (skip_ref[:, cells, :].astype(F32) + projected).astype(BF16)

        def send_mix(i, inner):
            target = band * BAND_TILES + i

            @pl.when(target != me)
            def _():
                mix_copy(target, me).start()

            @pl.when(target == me)
            def _():
                pltpu.make_async_copy(mix.at[:, own, :], got_mix.at[:, own, :], own_sem.at[4]).start()

            return inner

        lax.fori_loop(0, BAND_TILES, send_mix, 0)
        for copy in band_copies(band):
            copy.start()
        return carry

    lax.fori_loop(0, BANDS, do_band, 0)
    for band in range(BANDS):
        for copy in band_copies(band):
            copy.wait()
    own_cot.wait()
    ends.wait()
    ends_low.wait()
    cols.wait()
    pltpu.make_async_copy(mix.at[:, own, :], got_mix.at[:, own, :], own_sem.at[4]).wait()

    def finish(i, carry):
        peer = lax.rem(me + i, TILES)
        cot_copy(peer, peer).wait_recv()
        mix_copy(peer, peer).wait_recv()
        cot_copy(peer, peer).wait_send()
        mix_copy(peer, peer).wait_send()
        return carry

    lax.fori_loop(1, TILES, finish, 0)


def forward(x, skip, cot, kern, wproj):
    vmem = pl.BlockSpec(memory_space=pltpu.VMEM)
    anywhere = pl.BlockSpec(memory_space=pl.ANY)
    cells = ROWS * COLS
    dma = pltpu.SemaphoreType.DMA
    return pl.pallas_call(
        forward_kernel,
        out_shape=(
            jax.ShapeDtypeStruct((2, cells, EXPAND), BF16),
            jax.ShapeDtypeStruct((2, cells, EXPAND), BF16),
            jax.ShapeDtypeStruct((2, cells, WIDTH), BF16),
            jax.ShapeDtypeStruct((2, cells, WIDTH), BF16),
            jax.ShapeDtypeStruct((2, 2, COLS, EXPAND), BF16),
            jax.ShapeDtypeStruct((2, 2, 48, EXPAND), F32),
        ),
        in_specs=[anywhere, vmem, anywhere, vmem, vmem],
        out_specs=(anywhere,) * 6,
        scratch_shapes=[
            pltpu.VMEM((2, ROWS + 2, COLS, EXPAND), BF16),
            pltpu.VMEM((2, 2, ROWS, EXPAND), BF16),
            pltpu.VMEM((2, 2, ROWS, EXPAND), BF16),
            pltpu.VMEM((4, 16, EXPAND), BF16),
            pltpu.VMEM((4, 16, EXPAND), BF16),
            pltpu.VMEM((2, 2, 48, EXPAND), F32),
            pltpu.VMEM((2, 2, BANDS, 8, EXPAND), F32),
            pltpu.VMEM((2, cells, EXPAND), BF16),
            pltpu.VMEM((2, cells, EXPAND), BF16),
            pltpu.VMEM((2, cells, WIDTH), BF16),
            dma,
            dma((8,)),
            dma((8,)),
            dma((TILES,)),
            dma((TILES,)),
            dma((TILES,)),
            dma((TILES,)),
            dma((5,)),
            dma((2, BANDS)),
        ],
        compiler_params=pltpu.CompilerParams(
            collective_id=0, has_side_effects=True, vmem_limit_bytes=56 * 2**20
        ),
        name="forward",
    )(x, skip, cot, kern, wproj)


def attention_kernel(
    mix_ref, cot_ref, gain_ref, wqkv_ref, wout_ref, perm_ref, mask_ref,
    back_ref, gw_ref, go_ref, gg_ref, mix_s, cot_s,
):
    scale = 1.0 / math.sqrt(32.0)
    perm = perm_ref[...]
    for s in range(8):
        for src, dst in ((mix_ref, mix_s), (cot_ref, cot_s)):
            rows = src[:, 128 * s : 128 * s + 128, :].reshape(256, 256)
            dst[:, 8 * s : 8 * s + 8, :] = dot(perm, rows).reshape(32, 8, 256)
    gw_ref[...] = jnp.zeros_like(gw_ref)
    go_ref[...] = jnp.zeros_like(go_ref)
    gg_ref[...] = jnp.zeros_like(gg_ref)
    gain = gain_ref[...]
    lane = lax.broadcasted_iota(jnp.int32, (64, 128), 1) // 32

    def pick(full):
        halves = []
        for half in range(2):
            cols = slice(128 * half, 128 * half + 128)
            acc = full[64 * (4 * half) : 64 * (4 * half) + 64, cols]
            for h in range(1, 4):
                hh = 4 * half + h
                acc = jnp.where(lane == h, full[64 * hh : 64 * hh + 64, cols], acc)
            halves.append(acc)
        return jnp.concatenate(halves, axis=1)

    def block(b, carry):
        g0 = b * 4
        mix = mix_s[pl.ds(g0, 4)].reshape(256, 256)
        cot_f = cot_s[pl.ds(g0, 4)].reshape(256, 256)
        cot = cot_f.astype(BF16)
        inv = lax.rsqrt(jnp.mean(mix * mix, axis=-1, keepdims=True) + 1e-6)
        normed = (mix * inv * gain).astype(BF16)
        qkv = dot(normed, wqkv_ref[...]).astype(BF16)
        gatt = dot_t(cot, wout_ref[...]).astype(BF16)
        att, gqs, gks, gvs = [], [], [], []
        for i in range(4):
            r = slice(64 * i, 64 * i + 64)
            q, k, v = qkv[r, 0:256], qkv[r, 256:512], qkv[r, 512:768]
            do = gatt[r]
            qexp = jnp.concatenate([q] * 8, axis=0) * mask_ref[...]
            doexp = jnp.concatenate([do] * 8, axis=0) * mask_ref[...]
            st = dot_t(k, qexp) * scale
            e = jnp.exp(st - jnp.max(st, axis=0, keepdims=True))
            p = e * (1.0 / jnp.sum(e, axis=0, keepdims=True))
            pb = p.astype(BF16)
            dp = dot_t(v, doexp)
            dsum = jnp.sum(dp * p, axis=0, keepdims=True)
            ds = (p * (dp - dsum) * scale).astype(BF16)
            att.append(pick(dot_tl(pb, v)).astype(BF16))
            gqs.append(pick(dot_tl(ds, k)).astype(BF16))
            gks.append(dot(ds, qexp).astype(BF16))
            gvs.append(dot(pb, doexp).astype(BF16))
        attended = jnp.concatenate(att, axis=0)
        gqkv = [jnp.concatenate(x, axis=0) for x in (gqs, gks, gvs)]
        go_ref[...] += dot_tl(attended, cot)
        gn = jnp.zeros((256, 256), F32)
        normed_t = normed.T
        for j in range(3):
            gw_ref[256 * j : 256 * j + 256] += dot(normed_t, gqkv[j])
            gn = gn + dot_t(gqkv[j], wqkv_ref[:, 256 * j : 256 * j + 256])
        mi = mix * inv
        gg_ref[...] += jnp.sum(gn * mi, axis=0, keepdims=True)
        scaled = gn * gain
        mean = jnp.mean(scaled * mix, axis=-1, keepdims=True)
        out = cot_f + inv * scaled - mi * (inv * inv * mean)
        cot_s[pl.ds(g0, 4)] = out.reshape(4, 64, 256)
        return carry

    lax.fori_loop(0, 8, block, 0)
    for s in range(8):
        rows = cot_s[:, 8 * s : 8 * s + 8, :].reshape(256, 256).astype(BF16)
        back_ref[:, 128 * s : 128 * s + 128, :] = dot_tl(perm, rows).astype(BF16).reshape(2, 128, 256)


def consts():
    perm = np.zeros((256, 256), np.float32)
    for g in range(32):
        for s in range(8):
            perm[g * 8 + s, (g // 16) * 128 + s * 16 + g % 16] = 1
    mask = np.kron(np.eye(8), np.ones((64, 32))).astype(np.float32)
    return jnp.asarray(perm, BF16), jnp.asarray(mask, BF16)


def attention(got_mix, got_cot, gain, wqkv, wout):
    perm, mask = consts()
    v = pl.BlockSpec(memory_space=pltpu.VMEM)
    return pl.pallas_call(
        attention_kernel,
        out_shape=(
            jax.ShapeDtypeStruct((2, 1024, 256), BF16),
            jax.ShapeDtypeStruct((768, 256), F32),
            jax.ShapeDtypeStruct((256, 256), F32),
            jax.ShapeDtypeStruct((1, 256), F32),
        ),
        in_specs=[v] * 7,
        out_specs=(v,) * 4,
        scratch_shapes=[pltpu.VMEM((32, 64, 256), F32), pltpu.VMEM((32, 64, 256), F32)],
        compiler_params=pltpu.CompilerParams(vmem_limit_bytes=48 * 2**20),
        name="attention",
    )(got_mix, got_cot, gain.reshape(1, 256), wqkv, wout, perm, mask)


HEADS = 8


def passed_along(block, axis, distance):
    devices = range(lax.axis_size(axis))
    route = [(i - distance, i) for i in devices if i - distance in devices]
    return lax.ppermute(block, axis, route)


def contract(pattern, left_op, right_op):
    return jnp.einsum(pattern, left_op, right_op, preferred_element_type=jnp.float32)


def transposed_dot(left_op, right_op):
    return lax.dot_general(
        left_op, right_op, (((0,), (0,)), ((), ())), preferred_element_type=jnp.float32
    )


def smooth(inside):
    return jax.nn.gelu(inside, approximate=True)


def depthwise(padded, kernel, n_rows, n_cols):
    summed = jnp.zeros(padded.shape[:-3] + (n_rows, n_cols, padded.shape[-1]), jnp.float32)
    for row_off in range(3):
        for col_off in range(3):
            summed = summed + kernel[row_off, col_off] * padded[
                ..., row_off : row_off + n_rows, col_off : col_off + n_cols, :
            ].astype(jnp.float32)
    return summed


def depthwise_back(padded_grad, kernel, n_rows, n_cols):
    summed = jnp.zeros(
        padded_grad.shape[:-3] + (n_rows, n_cols, padded_grad.shape[-1]), jnp.float32
    )
    for row_off in range(3):
        for col_off in range(3):
            summed = summed + kernel[row_off, col_off] * padded_grad[
                ..., 2 - row_off : 2 - row_off + n_rows, 2 - col_off : 2 - col_off + n_cols, :
            ].astype(jnp.float32)
    return summed


def kernel_grad(grad_pre, padded, n_rows, n_cols):
    grad_float = grad_pre.astype(jnp.float32)
    lead_axes = tuple(range(grad_float.ndim - 1))
    stacked = []
    for row_off in range(3):
        row_terms = []
        for col_off in range(3):
            window = padded[..., row_off : row_off + n_rows, col_off : col_off + n_cols, :].astype(
                jnp.float32
            )
            row_terms.append(jnp.sum(grad_float * window, axis=lead_axes))
        stacked.append(jnp.stack(row_terms))
    return jnp.stack(stacked)


def attend_back(mixture, cotangent, norm_gain, w_qkv, w_out, n_heads):
    groups, length, model_dim = mixture.shape
    head_size = model_dim // n_heads
    score_scale = 1.0 / math.sqrt(head_size)
    mix_float = mixture.astype(jnp.float32)
    inverse = lax.rsqrt(jnp.mean(mix_float * mix_float, axis=-1, keepdims=True) + 1e-06)
    normed = (mix_float * inverse * norm_gain).astype(jnp.bfloat16)
    flat_norm = normed.reshape(groups * length, model_dim)
    proj_qkv = jnp.dot(flat_norm, w_qkv, preferred_element_type=jnp.float32).astype(jnp.bfloat16)
    proj_qkv = proj_qkv.reshape(groups, length, 3, n_heads, head_size)
    queries = proj_qkv[:, :, 0]
    key_rows = proj_qkv[:, :, 1]
    values = proj_qkv[:, :, 2]
    scores = contract("gqhd,gkhd->ghqk", queries, key_rows) * score_scale
    attn_probs = jax.nn.softmax(scores, axis=-1)
    weights_bf = attn_probs.astype(jnp.bfloat16)
    attended = contract("ghqk,gkhd->gqhd", weights_bf, values).astype(jnp.bfloat16)
    attended = attended.reshape(groups * length, model_dim)
    flat_cot = cotangent.reshape(groups * length, model_dim)
    grad_out = transposed_dot(attended, flat_cot)
    grad_att = jnp.dot(flat_cot, w_out.T, preferred_element_type=jnp.float32).astype(jnp.bfloat16)
    grad_att = grad_att.reshape(groups, length, n_heads, head_size)
    grad_values = contract("ghqk,gqhd->gkhd", weights_bf, grad_att)
    grad_probs = contract("gqhd,gkhd->ghqk", grad_att, values)
    grad_scores = (
        attn_probs
        * (grad_probs - jnp.sum(grad_probs * attn_probs, axis=-1, keepdims=True))
        * score_scale
    )
    grad_scores = grad_scores.astype(jnp.bfloat16)
    grad_query = contract("ghqk,gkhd->gqhd", grad_scores, key_rows)
    grad_keys = contract("ghqk,gqhd->gkhd", grad_scores, queries)
    grad_qkv = jnp.stack([grad_query, grad_keys, grad_values], axis=2).astype(jnp.bfloat16)
    grad_qkv = grad_qkv.reshape(groups * length, 3 * model_dim)
    grad_wqkv = transposed_dot(flat_norm, grad_qkv)
    grad_normed = jnp.dot(grad_qkv, w_qkv.T, preferred_element_type=jnp.float32).reshape(
        groups, length, model_dim
    )
    grad_gain = jnp.sum(grad_normed * mix_float * inverse, axis=(0, 1))
    scaled = grad_normed * norm_gain
    grad_mix = inverse * scaled - mix_float * inverse * inverse * inverse * jnp.mean(
        scaled * mix_float, axis=-1, keepdims=True
    )
    summed = (cotangent.astype(jnp.float32) + grad_mix).astype(jnp.bfloat16)
    return (summed, grad_wqkv, grad_out, grad_gain)


def pad_tile(tile, width):
    tile_col = lax.axis_index(("row", "col")) % GRID
    from_left = passed_along(tile[:, :, -width:], ("row", "col"), 1)
    from_right = passed_along(tile[:, :, :width], ("row", "col"), -1)
    from_left = jnp.where(tile_col == 0, jnp.zeros_like(from_left), from_left)
    from_right = jnp.where(tile_col == GRID - 1, jnp.zeros_like(from_right), from_right)
    sided = jnp.concatenate([from_left, tile, from_right], axis=2)
    from_above = passed_along(sided[:, -width:], ("row", "col"), GRID)
    from_below = passed_along(sided[:, :width], ("row", "col"), -GRID)
    return jnp.concatenate([from_above, sided, from_below], axis=1)


def to_targets(tile, n_tiles, per_tile, group_part):
    pictures, rows_here, cols_here, channels = tile.shape
    tile = tile.reshape(pictures, per_tile, n_tiles, group_part, channels)
    tile = tile.transpose(2, 0, 1, 3, 4)
    return tile.reshape(n_tiles, 1, pictures, per_tile, group_part, channels)


def received_to_groups(tensor, row_tiles, per_tile, group_part):
    pictures = tensor.shape[2]
    channels = tensor.shape[-1]
    tensor = tensor.reshape(row_tiles, GRID, pictures, per_tile, group_part, channels)
    tensor = tensor.transpose(2, 4, 0, 3, 1, 5)
    return tensor.reshape(pictures * group_part, GRID * GRID, channels)


def groups_to_targets(tensor, pictures, row_tiles, per_tile, group_part):
    channels = tensor.shape[-1]
    tensor = tensor.reshape(pictures, group_part, row_tiles, per_tile, GRID, channels)
    tensor = tensor.transpose(2, 4, 0, 3, 1, 5)
    return tensor.reshape(row_tiles * GRID, 1, pictures, per_tile, group_part, channels)


def returned_to_tile(tensor, n_tiles, rows_here, cols_here):
    pictures, per_tile, group_part, channels = tensor.shape[2:]
    tensor = tensor.reshape(n_tiles, pictures, per_tile, group_part, channels).transpose(
        1, 2, 0, 3, 4
    )
    return tensor.reshape(pictures, rows_here, cols_here, channels)


def on_device(expanded, skip, cotangent, depth_kernel, w_proj, norm_gain, w_qkv, w_out):
    expanded = expanded[:, 0]
    skip = skip[:, 0]
    cotangent = cotangent[:, 0]
    pictures, rows_here, cols_here, expand_dim = expanded.shape
    model_dim = skip.shape[3]
    n_row = lax.axis_size("row")
    n_col = lax.axis_size("col")
    n_tiles = n_row * n_col
    row_tiles = n_tiles // GRID
    span_a = rows_here * row_tiles // GRID
    per_tile = GRID // row_tiles
    group_part = span_a * cols_here // n_tiles
    token_count = pictures * lax.axis_size("dp") * rows_here * cols_here * n_tiles
    factor = 1.0 / math.sqrt(token_count)
    kern = depth_kernel.reshape(9, expand_dim)
    cells = rows_here * cols_here
    act, slope, got_mix, got_cot, ends, columns = forward(
        expanded, skip.reshape(pictures, cells, model_dim), cotangent.reshape(pictures, cells, model_dim), kern, w_proj
    )
    flat_act = act.reshape(-1, expand_dim)
    back, grad_wqkv, grad_out, grad_gain = attention(got_mix, got_cot, norm_gain, w_qkv, w_out)
    grad_wqkv = jnp.concatenate([grad_wqkv[256 * j : 256 * j + 256] for j in range(3)], axis=1)
    grad_gain = grad_gain[0]
    left = columns[0, :, 7:41, None].astype(jnp.bfloat16)
    right = columns[1, :, 7:41, None].astype(jnp.bfloat16)
    tall = jnp.concatenate([ends[0][:, None], expanded, ends[1][:, None]], axis=1)
    padded = jnp.concatenate([left, tall, right], axis=2)
    back_parts = back.reshape(pictures, 64, 16, model_dim).transpose(1, 0, 2, 3)[:, None, :, None]
    returned = lax.all_to_all(back_parts, ("row", "col"), split_axis=0, concat_axis=1, tiled=True)
    grad_skip = returned_to_tile(returned, n_tiles, rows_here, cols_here)
    flat_grad = grad_skip.reshape(-1, model_dim)
    grad_proj = transposed_dot(flat_act, flat_grad)
    grad_act = jnp.dot(flat_grad, w_proj.T, preferred_element_type=jnp.float32)
    grad_act = grad_act.reshape(pictures, rows_here, cols_here, expand_dim)
    grad_pre = (grad_act * slope.reshape(grad_act.shape).astype(jnp.float32)).astype(jnp.bfloat16)
    grad_pre_pad = pad_tile(grad_pre, 1)
    grad_kernel = kernel_grad(grad_pre, padded, rows_here, cols_here)
    grad_expanded = depthwise_back(grad_pre_pad, depth_kernel, rows_here, cols_here).astype(
        jnp.bfloat16
    )
    grad_kernel, grad_proj, grad_wqkv, grad_out, grad_gain = lax.psum(
        (grad_kernel, grad_proj, grad_wqkv, grad_out, grad_gain), ("dp", "row", "col")
    )
    return (
        grad_expanded[:, None],
        grad_skip[:, None],
        grad_kernel * factor,
        grad_proj * factor,
        grad_wqkv * factor,
        grad_out * factor,
        grad_gain * factor,
    )


def solution(mesh):
    placed = (
        P("dp", ("row", "col"), None, None, None),
        P("dp", ("row", "col"), None, None, None),
        P("dp", ("row", "col"), None, None, None),
        P(),
        P(),
        P(),
        P(),
        P(),
    )
    return jax.shard_map(
        on_device,
        mesh=mesh,
        in_specs=placed,
        out_specs=(
            P("dp", ("row", "col"), None, None, None),
            P("dp", ("row", "col"), None, None, None),
            P(),
            P(),
            P(),
            P(),
            P(),
        ),
        check_vma=False,
    )
```

```python
import math

import jax
import jax.numpy as jnp
import numpy as np
from jax import lax
from jax.experimental import pallas as pl
from jax.experimental.pallas import tpu as pltpu
from jax.sharding import PartitionSpec as P

GRID = 8
TILES = 64
ROWS = 32
COLS = 32
LANES = 128
WIDTH = 256
EXPAND = 1024
LANE_BLOCKS = EXPAND // LANES
BAND = 4
BANDS = ROWS // BAND
BAND_CELLS = BAND * COLS
BAND_TILES = TILES // BANDS
F32 = jnp.float32
BF16 = jnp.bfloat16
MESH_ID = pl.DeviceIdType.MESH
GELU_1 = math.sqrt(2.0 / math.pi)
GELU_3 = GELU_1 * 0.044715


def dot(a, b):
    return lax.dot_general(a, b, (((1,), (0,)), ((), ())), preferred_element_type=F32)


def dot_t(a, b):
    return lax.dot_general(a, b, (((1,), (1,)), ((), ())), preferred_element_type=F32)


def dot_tl(a, b):
    return lax.dot_general(a, b, (((0,), (0,)), ((), ())), preferred_element_type=F32)


def tile_id(tile):
    return {"row": tile // 32, "col": lax.rem(tile, 32)}


def my_tile():
    return lax.axis_index("row") * 32 + lax.axis_index("col")


def neighbours(me):
    tile_row, tile_col = me // GRID, lax.rem(me, GRID)
    found = {}
    for down in (-1, 0, 1):
        for right in (-1, 0, 1):
            if (down, right) != (0, 0):
                found[down, right] = lax.rem(tile_row + down + GRID, GRID) * GRID + lax.rem(
                    tile_col + right + GRID, GRID
                )
    return found


SIDES = ((0, -1), (0, 1))
ENDS = ((-1, 0), (1, 0))
CORNERS = ((-1, -1), (-1, 1), (1, -1), (1, 1))
AROUND = SIDES + ENDS + CORNERS


def rim_copies(me, grid_ref, sides_out, sides_in, corners_out, corners_in, send_sem, recv_sem):
    around = neighbours(me)
    copies = []
    for n, (down, right) in enumerate(AROUND):
        if down == 0:
            source = sides_out.at[(right + 1) // 2]
            target = sides_in.at[(1 - right) // 2]
        elif right == 0:
            source = grid_ref.at[:, 1 if down < 0 else ROWS]
            target = grid_ref.at[:, ROWS + 1 if down < 0 else 0]
        else:
            place = CORNERS.index((down, right))
            source = corners_out.at[place]
            target = corners_in.at[3 - place]
        copies.append(
            pltpu.make_async_remote_copy(
                src_ref=source,
                dst_ref=target,
                send_sem=send_sem.at[n],
                recv_sem=recv_sem.at[n],
                device_id=tile_id(around[down, right]),
                device_id_type=MESH_ID,
            )
        )
    return copies


def collect_sides(grid_ref, sides_out, corners_out):
    for side in range(2):
        for picture in range(2):
            for start in range(0, ROWS, 16):
                window = grid_ref[picture, 1 + start : 17 + start, 16 * side : 16 * side + 16, :]
                column = window.astype(F32)[:, 15 * side, :]
                sides_out[side, picture, start : start + 16, :] = column.astype(BF16)
    for place, (down, right) in enumerate(CORNERS):
        edge = 0 if down < 0 else 16
        row = 0 if down < 0 else 15
        both = [
            sides_out[(right + 1) // 2, picture, edge : edge + 16, :].astype(F32)[row : row + 1]
            for picture in range(2)
        ]
        filler = jnp.zeros((14, EXPAND), F32)
        corners_out[place] = jnp.concatenate(both + [filler], axis=0).astype(BF16)


def clear_outside(me, grid_ref, sides_in, corners_in):
    tile_row, tile_col = me // GRID, lax.rem(me, GRID)
    for side, last in ((0, 0), (1, GRID - 1)):

        @pl.when(tile_col == last)
        def _():
            sides_in[side] = jnp.zeros(sides_in.shape[1:], BF16)
            corners_in[side] = jnp.zeros(corners_in.shape[1:], BF16)
            corners_in[2 + side] = jnp.zeros(corners_in.shape[1:], BF16)

    for end, last in ((0, 0), (1, GRID - 1)):

        @pl.when(tile_row == last)
        def _():
            grid_ref[:, (ROWS + 1) * end] = jnp.zeros((2, COLS, EXPAND), BF16)
            corners_in[2 * end] = jnp.zeros(corners_in.shape[1:], BF16)
            corners_in[2 * end + 1] = jnp.zeros(corners_in.shape[1:], BF16)


def column_stack(sides_in, corners_in, columns):
    for side in range(2):
        for picture in range(2):
            columns[side, picture, 0:8] = jnp.concatenate(
                [jnp.zeros((7, EXPAND), F32), corners_in[side].astype(F32)[picture : picture + 1]], axis=0
            )
            columns[side, picture, 8 : 8 + ROWS] = sides_in[side, picture].astype(F32)
            columns[side, picture, 40:48] = jnp.concatenate(
                [corners_in[2 + side].astype(F32)[picture : picture + 1], jnp.zeros((7, EXPAND), F32)], axis=0
            )


def column_terms(columns, weights, col_offs, terms):
    for side in range(2):
        for picture in range(2):
            total = None
            for row_off in range(3):
                term = (
                    weights(row_off, col_offs[side])
                    * columns[side, picture, 7 + row_off : 7 + row_off + ROWS, :]
                )
                total = term if total is None else total + term
            for band in range(BANDS):
                terms[side, picture, band, 0:BAND] = total[BAND * band : BAND * band + BAND]


def convolve(rows, weights, left, right):
    spot = lax.broadcasted_iota(jnp.int32, (BAND, COLS, LANES), 1)
    parts = []
    for col_off in range(3):
        total = None
        for row_off in range(3):
            term = weights[3 * row_off + col_off][None, :, :] * rows[row_off : row_off + BAND]
            total = term if total is None else total + term
        parts.append(total)
    from_left = jnp.where(spot == 0, left[:, None, :], pltpu.roll(parts[0], 1, 1))
    from_right = jnp.where(spot == COLS - 1, right[:, None, :], pltpu.roll(parts[2], COLS - 1, 1))
    return parts[1] + from_left + from_right


def forward_kernel(
    x_hbm, skip_ref, cot_hbm, kern_ref, wproj_ref,
    act_hbm, dg_hbm, got_mix, got_cot, ends_out, columns_out,
    grid, sides_out, sides_in, corners_out, corners_in, columns, terms, act, dg, mix,
    load_sem, rim_send, rim_recv, cot_send, cot_recv, mix_send, mix_recv, own_sem, store_sem,
):
    me = my_tile()
    load = pltpu.make_async_copy(x_hbm, grid.at[:, pl.ds(1, ROWS)], load_sem)
    load.start()
    barrier = pltpu.get_barrier_semaphore()

    def greet(i, carry):
        pl.semaphore_signal(
            barrier, inc=1, device_id=tile_id(lax.rem(me + i, TILES)), device_id_type=MESH_ID
        )
        return carry

    lax.fori_loop(1, TILES, greet, 0)
    load.wait()
    collect_sides(grid, sides_out, corners_out)
    pl.semaphore_wait(barrier, TILES - 1)
    rim = rim_copies(me, grid, sides_out, sides_in, corners_out, corners_in, rim_send, rim_recv)
    for copy in rim:
        copy.start()

    def cot_copy(target, slot):
        return pltpu.make_async_remote_copy(
            src_ref=cot_hbm.at[:, pl.ds(pl.multiple_of(target * 16, 16), 16), :],
            dst_ref=got_cot.at[:, pl.ds(pl.multiple_of(slot * 16, 16), 16), :],
            send_sem=cot_send.at[target],
            recv_sem=cot_recv.at[slot],
            device_id=tile_id(target),
            device_id_type=MESH_ID,
        )

    def mix_copy(target, slot):
        return pltpu.make_async_remote_copy(
            src_ref=mix.at[:, pl.ds(pl.multiple_of(target * 16, 16), 16), :],
            dst_ref=got_mix.at[:, pl.ds(pl.multiple_of(slot * 16, 16), 16), :],
            send_sem=mix_send.at[target],
            recv_sem=mix_recv.at[slot],
            device_id=tile_id(target),
            device_id_type=MESH_ID,
        )

    def send_cot(i, carry):
        cot_copy(lax.rem(me + i, TILES), me).start()
        return carry

    lax.fori_loop(1, TILES, send_cot, 0)
    own = pl.ds(pl.multiple_of(me * 16, 16), 16)
    own_cot = pltpu.make_async_copy(cot_hbm.at[:, own, :], got_cot.at[:, own, :], own_sem.at[0])
    own_cot.start()
    for copy in rim:
        copy.wait_recv()
    for copy in rim:
        copy.wait_send()
    clear_outside(me, grid, sides_in, corners_in)
    column_stack(sides_in, corners_in, columns)
    column_terms(
        columns, lambda a, c: kern_ref[3 * a + c : 3 * a + c + 1, :], (0, 2), terms
    )
    ends = pltpu.make_async_copy(grid.at[:, 0], ends_out.at[0], own_sem.at[1])
    ends.start()
    ends_low = pltpu.make_async_copy(grid.at[:, ROWS + 1], ends_out.at[1], own_sem.at[2])
    ends_low.start()
    cols = pltpu.make_async_copy(columns, columns_out, own_sem.at[3])
    cols.start()

    def band_copies(band):
        cells = pl.ds(pl.multiple_of(band * BAND_CELLS, BAND_CELLS), BAND_CELLS)
        return (
            pltpu.make_async_copy(act.at[:, cells, :], act_hbm.at[:, cells, :], store_sem.at[0, band]),
            pltpu.make_async_copy(dg.at[:, cells, :], dg_hbm.at[:, cells, :], store_sem.at[1, band]),
        )

    def do_band(step, carry):
        band = lax.rem(step + me // GRID, BANDS)
        first = band * BAND
        cells = pl.ds(pl.multiple_of(band * BAND_CELLS, BAND_CELLS), BAND_CELLS)

        def do_block(index, inner):
            picture, block = index // LANE_BLOCKS, lax.rem(index, LANE_BLOCKS)
            lanes = pl.ds(pl.multiple_of(block * LANES, LANES), LANES)
            rows = grid[picture, pl.ds(first, BAND + 2), :, lanes].astype(F32)
            weights = [kern_ref[n : n + 1, lanes] for n in range(9)]
            pre = convolve(
                rows,
                weights,
                terms[0, picture, band, 0:BAND, lanes],
                terms[1, picture, band, 0:BAND, lanes],
            )
            square = pre * pre
            tanh = jnp.tanh(pre * (GELU_1 + GELU_3 * square))
            half = 0.5 * pre
            activated = half + half * tanh
            slope = (0.5 + 0.5 * tanh) + half * (1.0 - tanh * tanh) * (GELU_1 + (3.0 * GELU_3) * square)
            act[picture, cells, lanes] = activated.astype(BF16).reshape(BAND_CELLS, LANES)
            dg[picture, cells, lanes] = slope.astype(BF16).reshape(BAND_CELLS, LANES)
            return inner

        lax.fori_loop(0, 2 * LANE_BLOCKS, do_block, 0)
        flat = act[:, cells, :].reshape(2 * BAND_CELLS, EXPAND)
        projected = dot(flat, wproj_ref[...]).reshape(2, BAND_CELLS, WIDTH)
        mix[:, cells, :] = (skip_ref[:, cells, :].astype(F32) + projected).astype(BF16)

        def send_mix(i, inner):
            target = band * BAND_TILES + i

            @pl.when(target != me)
            def _():
                mix_copy(target, me).start()

            @pl.when(target == me)
            def _():
                pltpu.make_async_copy(mix.at[:, own, :], got_mix.at[:, own, :], own_sem.at[4]).start()

            return inner

        lax.fori_loop(0, BAND_TILES, send_mix, 0)
        for copy in band_copies(band):
            copy.start()
        return carry

    lax.fori_loop(0, BANDS, do_band, 0)
    for band in range(BANDS):
        for copy in band_copies(band):
            copy.wait()
    own_cot.wait()
    ends.wait()
    ends_low.wait()
    cols.wait()
    pltpu.make_async_copy(mix.at[:, own, :], got_mix.at[:, own, :], own_sem.at[4]).wait()

    def finish(i, carry):
        peer = lax.rem(me + i, TILES)
        cot_copy(peer, peer).wait_recv()
        mix_copy(peer, peer).wait_recv()
        cot_copy(peer, peer).wait_send()
        mix_copy(peer, peer).wait_send()
        return carry

    lax.fori_loop(1, TILES, finish, 0)


def forward(x, skip, cot, kern, wproj):
    vmem = pl.BlockSpec(memory_space=pltpu.VMEM)
    anywhere = pl.BlockSpec(memory_space=pl.ANY)
    cells = ROWS * COLS
    dma = pltpu.SemaphoreType.DMA
    return pl.pallas_call(
        forward_kernel,
        out_shape=(
            jax.ShapeDtypeStruct((2, cells, EXPAND), BF16),
            jax.ShapeDtypeStruct((2, cells, EXPAND), BF16),
            jax.ShapeDtypeStruct((2, cells, WIDTH), BF16),
            jax.ShapeDtypeStruct((2, cells, WIDTH), BF16),
            jax.ShapeDtypeStruct((2, 2, COLS, EXPAND), BF16),
            jax.ShapeDtypeStruct((2, 2, 48, EXPAND), F32),
        ),
        in_specs=[anywhere, vmem, anywhere, vmem, vmem],
        out_specs=(anywhere,) * 6,
        scratch_shapes=[
            pltpu.VMEM((2, ROWS + 2, COLS, EXPAND), BF16),
            pltpu.VMEM((2, 2, ROWS, EXPAND), BF16),
            pltpu.VMEM((2, 2, ROWS, EXPAND), BF16),
            pltpu.VMEM((4, 16, EXPAND), BF16),
            pltpu.VMEM((4, 16, EXPAND), BF16),
            pltpu.VMEM((2, 2, 48, EXPAND), F32),
            pltpu.VMEM((2, 2, BANDS, 8, EXPAND), F32),
            pltpu.VMEM((2, cells, EXPAND), BF16),
            pltpu.VMEM((2, cells, EXPAND), BF16),
            pltpu.VMEM((2, cells, WIDTH), BF16),
            dma,
            dma((8,)),
            dma((8,)),
            dma((TILES,)),
            dma((TILES,)),
            dma((TILES,)),
            dma((TILES,)),
            dma((5,)),
            dma((2, BANDS)),
        ],
        compiler_params=pltpu.CompilerParams(
            collective_id=0, has_side_effects=True, vmem_limit_bytes=56 * 2**20
        ),
        name="forward",
    )(x, skip, cot, kern, wproj)


def attention_kernel(
    mix_ref, cot_ref, gain_ref, wqkv_ref, wout_ref, perm_ref, mask_ref,
    back_ref, gw_ref, go_ref, gg_ref, mix_s, cot_s,
):
    scale = 1.0 / math.sqrt(32.0)
    perm = perm_ref[...]
    for s in range(8):
        for src, dst in ((mix_ref, mix_s), (cot_ref, cot_s)):
            rows = src[:, 128 * s : 128 * s + 128, :].reshape(256, 256)
            dst[:, 8 * s : 8 * s + 8, :] = dot(perm, rows).reshape(32, 8, 256)
    gw_ref[...] = jnp.zeros_like(gw_ref)
    go_ref[...] = jnp.zeros_like(go_ref)
    gg_ref[...] = jnp.zeros_like(gg_ref)
    gain = gain_ref[...]
    lane = lax.broadcasted_iota(jnp.int32, (64, 128), 1) // 32

    def pick(full):
        halves = []
        for half in range(2):
            cols = slice(128 * half, 128 * half + 128)
            acc = full[64 * (4 * half) : 64 * (4 * half) + 64, cols]
            for h in range(1, 4):
                hh = 4 * half + h
                acc = jnp.where(lane == h, full[64 * hh : 64 * hh + 64, cols], acc)
            halves.append(acc)
        return jnp.concatenate(halves, axis=1)

    def block(b, carry):
        g0 = b * 4
        mix = mix_s[pl.ds(g0, 4)].reshape(256, 256)
        cot_f = cot_s[pl.ds(g0, 4)].reshape(256, 256)
        cot = cot_f.astype(BF16)
        inv = lax.rsqrt(jnp.mean(mix * mix, axis=-1, keepdims=True) + 1e-6)
        normed = (mix * inv * gain).astype(BF16)
        qkv = dot(normed, wqkv_ref[...]).astype(BF16)
        gatt = dot_t(cot, wout_ref[...]).astype(BF16)
        att, gqs, gks, gvs = [], [], [], []
        for i in range(4):
            r = slice(64 * i, 64 * i + 64)
            q, k, v = qkv[r, 0:256], qkv[r, 256:512], qkv[r, 512:768]
            do = gatt[r]
            qexp = jnp.concatenate([q] * 8, axis=0) * mask_ref[...]
            doexp = jnp.concatenate([do] * 8, axis=0) * mask_ref[...]
            st = dot_t(k, qexp) * scale
            e = jnp.exp(st - jnp.max(st, axis=0, keepdims=True))
            p = e * (1.0 / jnp.sum(e, axis=0, keepdims=True))
            pb = p.astype(BF16)
            dp = dot_t(v, doexp)
            dsum = jnp.sum(dp * p, axis=0, keepdims=True)
            ds = (p * (dp - dsum) * scale).astype(BF16)
            att.append(pick(dot_tl(pb, v)).astype(BF16))
            gqs.append(pick(dot_tl(ds, k)).astype(BF16))
            gks.append(dot(ds, qexp).astype(BF16))
            gvs.append(dot(pb, doexp).astype(BF16))
        attended = jnp.concatenate(att, axis=0)
        gqkv = [jnp.concatenate(x, axis=0) for x in (gqs, gks, gvs)]
        go_ref[...] += dot_tl(attended, cot)
        gn = jnp.zeros((256, 256), F32)
        normed_t = normed.T
        for j in range(3):
            gw_ref[256 * j : 256 * j + 256] += dot(normed_t, gqkv[j])
            gn = gn + dot_t(gqkv[j], wqkv_ref[:, 256 * j : 256 * j + 256])
        mi = mix * inv
        gg_ref[...] += jnp.sum(gn * mi, axis=0, keepdims=True)
        scaled = gn * gain
        mean = jnp.mean(scaled * mix, axis=-1, keepdims=True)
        out = cot_f + inv * scaled - mi * (inv * inv * mean)
        cot_s[pl.ds(g0, 4)] = out.reshape(4, 64, 256)
        return carry

    lax.fori_loop(0, 8, block, 0)
    for s in range(8):
        rows = cot_s[:, 8 * s : 8 * s + 8, :].reshape(256, 256).astype(BF16)
        back_ref[:, 128 * s : 128 * s + 128, :] = dot_tl(perm, rows).astype(BF16).reshape(2, 128, 256)


def consts():
    perm = np.zeros((256, 256), np.float32)
    for g in range(32):
        for s in range(8):
            perm[g * 8 + s, (g // 16) * 128 + s * 16 + g % 16] = 1
    mask = np.kron(np.eye(8), np.ones((64, 32))).astype(np.float32)
    return jnp.asarray(perm, BF16), jnp.asarray(mask, BF16)


def attention(got_mix, got_cot, gain, wqkv, wout):
    perm, mask = consts()
    v = pl.BlockSpec(memory_space=pltpu.VMEM)
    return pl.pallas_call(
        attention_kernel,
        out_shape=(
            jax.ShapeDtypeStruct((2, 1024, 256), BF16),
            jax.ShapeDtypeStruct((768, 256), F32),
            jax.ShapeDtypeStruct((256, 256), F32),
            jax.ShapeDtypeStruct((1, 256), F32),
        ),
        in_specs=[v] * 7,
        out_specs=(v,) * 4,
        scratch_shapes=[pltpu.VMEM((32, 64, 256), F32), pltpu.VMEM((32, 64, 256), F32)],
        compiler_params=pltpu.CompilerParams(vmem_limit_bytes=48 * 2**20),
        name="attention",
    )(got_mix, got_cot, gain.reshape(1, 256), wqkv, wout, perm, mask)


def owner_id(j, m):
    return {"dp": j // 4, "row": lax.rem(j // 2, 2), "col": m * 2 + lax.rem(j, 2)}


def backward_kernel(
    back_hbm, act_hbm, dg_hbm, x_hbm, ends_hbm, columns_hbm, kern_ref, wproj_ref, gw_ref, go_ref, gg_ref,
    ge_hbm, gs_hbm, gkern_out, gproj_out, gwqkv_out, gout_out, ggain_out,
    gs, act, dg, xgrid, ggrid, xcols, gcols, sides_out, sides_in, corners_out, corners_in, terms, gproj_t, gkern,
    part_out, part_in, small_out, small_in, whole,
    load_sem, back_send, back_recv, own_sem, rim_send, rim_recv, store_sem,
    first_send, first_recv, extra_send, extra_recv, second_send, second_recv,
    share_send, share_recv, last_send, last_recv, scale,
):
    me = my_tile()
    tile_row, tile_col = me // GRID, lax.rem(me, GRID)
    dp = lax.axis_index("dp")
    core = lax.rem(lax.axis_index("col"), 2)
    j = dp * 4 + lax.axis_index("row") * 2 + core
    m = lax.axis_index("col") // 2
    loads = [
        pltpu.make_async_copy(dg_hbm, dg, load_sem.at[0]),
        pltpu.make_async_copy(act_hbm, act, load_sem.at[1]),
        pltpu.make_async_copy(x_hbm, xgrid.at[:, pl.ds(1, ROWS)], load_sem.at[2]),
        pltpu.make_async_copy(ends_hbm.at[0], xgrid.at[:, 0], load_sem.at[3]),
        pltpu.make_async_copy(ends_hbm.at[1], xgrid.at[:, ROWS + 1], load_sem.at[4]),
        pltpu.make_async_copy(columns_hbm, xcols, load_sem.at[5]),
    ]
    for copy in loads:
        copy.start()
    barrier = pltpu.get_barrier_semaphore()

    def greet(i, carry):
        pl.semaphore_signal(
            barrier, inc=1, device_id=tile_id(lax.rem(me + i, TILES)), device_id_type=MESH_ID
        )
        return carry

    lax.fori_loop(1, TILES, greet, 0)
    for n in range(4):
        pl.semaphore_signal(
            barrier, inc=1, device_id=owner_id((1 - dp) * 4 + n, m), device_id_type=MESH_ID
        )
    for n in range(4):
        part_out[4 + n, 0:256] = (gw_ref[256 * n : 256 * n + 256] if n < 3 else go_ref[...]).astype(BF16)
    pl.semaphore_wait(barrier, TILES + 3)

    def back_copy(target, slot):
        return pltpu.make_async_remote_copy(
            src_ref=back_hbm.at[:, pl.ds(pl.multiple_of(target * 16, 16), 16), :],
            dst_ref=gs.at[:, pl.ds(pl.multiple_of(slot * 16, 16), 16), :],
            send_sem=back_send.at[target],
            recv_sem=back_recv.at[slot],
            device_id=tile_id(target),
            device_id_type=MESH_ID,
        )

    def send_back(i, carry):
        target = lax.rem(tile_row + GRID - i // GRID, GRID) * GRID + lax.rem(
            tile_col + GRID - lax.rem(i, GRID), GRID
        )
        back_copy(target, me).start()
        return carry

    lax.fori_loop(1, TILES, send_back, 0)
    own = pl.ds(pl.multiple_of(me * 16, 16), 16)
    own_copy = pltpu.make_async_copy(back_hbm.at[:, own, :], gs.at[:, own, :], own_sem.at[0])
    own_copy.start()

    def first_copy(owner, slot):
        return pltpu.make_async_remote_copy(
            src_ref=part_out.at[owner, pl.ds(0, 256)],
            dst_ref=part_in.at[slot, pl.ds(0, 256)],
            send_sem=first_send.at[owner],
            recv_sem=first_recv.at[slot],
            device_id=owner_id(owner, m),
            device_id_type=MESH_ID,
        )

    def extra_copy(owner, slot):
        return pltpu.make_async_remote_copy(
            src_ref=part_out.at[owner, pl.ds(256, 16)],
            dst_ref=part_in.at[slot, pl.ds(256, 16)],
            send_sem=extra_send.at[owner],
            recv_sem=extra_recv.at[slot],
            device_id=owner_id(owner, m),
            device_id_type=MESH_ID,
        )

    def second_copy(owner, slot):
        return pltpu.make_async_remote_copy(
            src_ref=small_out.at[owner],
            dst_ref=small_in.at[slot],
            send_sem=second_send.at[owner],
            recv_sem=second_recv.at[slot],
            device_id=owner_id(j, owner),
            device_id_type=MESH_ID,
        )

    def share_copy(other, slot):
        rows = pl.ds(pl.multiple_of(slot * 16, 16), 16)
        return pltpu.make_async_remote_copy(
            src_ref=whole.at[j, pl.ds(pl.multiple_of(m * 16, 16), 16)],
            dst_ref=whole.at[j, rows],
            send_sem=share_send.at[other],
            recv_sem=share_recv.at[slot],
            device_id=owner_id(j, other),
            device_id_type=MESH_ID,
        )

    def last_copy(other, slot):
        return pltpu.make_async_remote_copy(
            src_ref=whole.at[j],
            dst_ref=whole.at[slot],
            send_sem=last_send.at[other],
            recv_sem=last_recv.at[slot],
            device_id=owner_id(other, m),
            device_id_type=MESH_ID,
        )

    def to_eight(copy, begin, end):
        for n in range(begin, end):

            @pl.when(j != n)
            def _():
                copy(n, j).start()

    def around(count, mine, action):
        def one(i, carry):
            action(lax.rem(mine + i, count))
            return carry

        lax.fori_loop(1, count, one, 0)

    to_eight(first_copy, 4, 8)
    gproj_t[...] = jnp.zeros_like(gproj_t)
    loads[0].wait()
    loads[1].wait()
    own_copy.wait()

    def do_band(step, carry):
        band = lax.rem(step + tile_row, BANDS)
        cells = pl.ds(pl.multiple_of(band * BAND_CELLS, BAND_CELLS), BAND_CELLS)

        def arrived(i, inner):
            source = band * BAND_TILES + i

            @pl.when(source != me)
            def _():
                back_copy(source, source).wait_recv()

            return inner

        lax.fori_loop(0, BAND_TILES, arrived, 0)
        flat = gs[:, cells, :].reshape(2 * BAND_CELLS, WIDTH)
        flat_t = flat.T
        for n in range(4):
            lanes = slice(256 * n, 256 * n + 256)
            grad_act = dot_t(flat, wproj_ref[lanes, :])
            slope = dg[:, cells, lanes].astype(F32).reshape(2 * BAND_CELLS, 256)
            grad_pre = (grad_act * slope).astype(BF16)
            ggrid[:, pl.ds(1 + band * BAND, BAND), :, lanes] = grad_pre.reshape(2, BAND, COLS, 256)
            gproj_t[:, lanes] += dot(flat_t, act[:, cells, lanes].reshape(2 * BAND_CELLS, 256))
        return carry

    lax.fori_loop(0, BANDS, do_band, 0)
    gs_store = pltpu.make_async_copy(gs, gs_hbm, own_sem.at[1])
    gs_store.start()
    collect_sides(ggrid, sides_out, corners_out)
    rim = rim_copies(me, ggrid, sides_out, sides_in, corners_out, corners_in, rim_send, rim_recv)
    for copy in rim:
        copy.start()
    for n in range(4):
        part_out[n, 0:256] = gproj_t[:, 256 * n : 256 * n + 256].T.astype(BF16)
    to_eight(first_copy, 0, 4)
    for copy in loads[2:]:
        copy.wait()

    spot = lax.broadcasted_iota(jnp.int32, (BAND, COLS, LANES), 1)

    def kernel_block(block, carry):
        lanes = pl.ds(pl.multiple_of(block * LANES, LANES), LANES)

        def one(index, sums):
            picture, band = index // BANDS, lax.rem(index, BANDS)
            grads = ggrid[picture, pl.ds(1 + band * BAND, BAND), :, lanes].astype(F32)
            rows = xgrid[picture, pl.ds(band * BAND, BAND + 2), :, lanes].astype(F32)
            shifted = (
                jnp.where(spot == COLS - 1, 0.0, pltpu.roll(grads, COLS - 1, 1)),
                grads,
                jnp.where(spot == 0, 0.0, pltpu.roll(grads, 1, 1)),
            )
            new = []
            for row_off in range(3):
                for col_off in range(3):
                    product = shifted[col_off] * rows[row_off : row_off + BAND]
                    product = product.reshape(BAND * 4, 8, LANES).sum(axis=0)
                    new.append(sums[3 * row_off + col_off] + product)
            return tuple(new)

        sums = lax.fori_loop(
            0, 2 * BANDS, one, tuple(jnp.zeros((8, LANES), F32) for _ in range(9))
        )
        for n in range(9):
            gkern[n : n + 1, lanes] = jnp.sum(sums[n], axis=0, keepdims=True)
        return carry

    lax.fori_loop(0, LANE_BLOCKS, kernel_block, 0)
    for row_off in range(3):
        for side in range(2):
            n = 3 * row_off + 2 * side
            for picture in range(2):
                beside = xcols[side, picture, 7 + row_off : 7 + row_off + ROWS, :]
                gkern[n : n + 1, :] += jnp.sum(
                    sides_out[side, picture].astype(F32) * beside, axis=0, keepdims=True
                )
    for n in range(8):
        if n < 4:
            rows = [gkern[0:9, 256 * n : 256 * n + 256], jnp.zeros((7, 256), F32)]
        elif n == 4:
            rows = [gg_ref[...], jnp.zeros((15, 256), F32)]
        else:
            rows = [jnp.zeros((16, 256), F32)]
        part_out[n, 256:272] = jnp.concatenate(rows, axis=0).astype(BF16)
    to_eight(extra_copy, 0, 8)

    for copy in rim:
        copy.wait_recv()
    for copy in rim:
        copy.wait_send()
    clear_outside(me, ggrid, sides_in, corners_in)
    column_stack(sides_in, corners_in, gcols)
    column_terms(
        gcols, lambda a, c: kern_ref[8 - 3 * a - c : 9 - 3 * a - c, :], (0, 2), terms
    )

    def band_copy(band):
        cells = pl.ds(pl.multiple_of(band * BAND_CELLS, BAND_CELLS), BAND_CELLS)
        return pltpu.make_async_copy(dg.at[:, cells, :], ge_hbm.at[:, cells, :], store_sem.at[band])

    def last_band(band, carry):
        first = band * BAND
        cells = pl.ds(pl.multiple_of(band * BAND_CELLS, BAND_CELLS), BAND_CELLS)

        def do_block(index, inner):
            picture, block = index // LANE_BLOCKS, lax.rem(index, LANE_BLOCKS)
            lanes = pl.ds(pl.multiple_of(block * LANES, LANES), LANES)
            rows = ggrid[picture, pl.ds(first, BAND + 2), :, lanes].astype(F32)
            weights = [kern_ref[8 - n : 9 - n, lanes] for n in range(9)]
            total = convolve(
                rows,
                weights,
                terms[0, picture, band, 0:BAND, lanes],
                terms[1, picture, band, 0:BAND, lanes],
            )
            dg[picture, cells, lanes] = total.astype(BF16).reshape(BAND_CELLS, LANES)
            return inner

        lax.fori_loop(0, 2 * LANE_BLOCKS, do_block, 0)
        band_copy(band).start()
        return carry

    lax.fori_loop(0, 3, last_band, 0)

    around(8, j, lambda p: first_copy(p, p).wait_recv())
    around(8, j, lambda p: extra_copy(p, p).wait_recv())
    part_in[j] = part_out[j]
    total = part_in[0].astype(F32)
    for n in range(1, 8):
        total = total + part_in[n].astype(F32)
    total = total.astype(BF16)
    for n in range(16):
        small_out[n, 0:16] = total[16 * n : 16 * n + 16]
        small_out[n, 16:32] = total[256:272]
    around(16, m, lambda p: second_copy(p, m).start())

    lax.fori_loop(3, 6, last_band, 0)

    around(16, m, lambda p: second_copy(p, p).wait_recv())
    small_in[m] = small_out[m]
    total = small_in[0].astype(F32)
    for n in range(1, 16):
        total = total + small_in[n].astype(F32)
    total = total.astype(BF16)
    whole[j, pl.ds(pl.multiple_of(m * 16, 16), 16)] = total[0:16]
    whole[j, 256:272] = total[16:32]
    around(16, m, lambda p: share_copy(p, m).start())

    lax.fori_loop(6, BANDS, last_band, 0)

    around(16, m, lambda p: share_copy(p, p).wait_recv())
    around(16, m, lambda p: share_copy(p, p).wait_send())
    around(8, j, lambda p: last_copy(p, j).start())
    around(8, j, lambda p: first_copy(p, p).wait_send())
    around(8, j, lambda p: extra_copy(p, p).wait_send())
    around(16, m, lambda p: second_copy(p, p).wait_send())
    around(TILES, me, lambda p: back_copy(p, p).wait_send())
    gs_store.wait()
    for band in range(BANDS):
        band_copy(band).wait()
    around(8, j, lambda p: last_copy(p, p).wait_recv())
    around(8, j, lambda p: last_copy(p, p).wait_send())
    for n in range(8):
        block = whole[n, 0:256].astype(F32) * scale
        if n < 4:
            gproj_out[256 * n : 256 * n + 256, :] = block
            gkern_out[:, 256 * n : 256 * n + 256] = whole[n, 256:272].astype(F32)[0:9] * scale
        elif n < 7:
            gwqkv_out[:, 256 * (n - 4) : 256 * (n - 4) + 256] = block
        else:
            gout_out[...] = block
    ggain_out[...] = whole[4, 256:272].astype(F32)[0:1] * scale


def backward(back, act, slope, x, ends, columns, kern, wproj, gw, go, gg, scale):
    vmem = pl.BlockSpec(memory_space=pltpu.VMEM)
    anywhere = pl.BlockSpec(memory_space=pl.ANY)
    cells = ROWS * COLS
    dma = pltpu.SemaphoreType.DMA

    def kernel(*refs):
        backward_kernel(*refs, scale)

    return pl.pallas_call(
        kernel,
        out_shape=(
            jax.ShapeDtypeStruct((2, cells, EXPAND), BF16),
            jax.ShapeDtypeStruct((2, cells, WIDTH), BF16),
            jax.ShapeDtypeStruct((9, EXPAND), F32),
            jax.ShapeDtypeStruct((EXPAND, WIDTH), F32),
            jax.ShapeDtypeStruct((WIDTH, 3 * WIDTH), F32),
            jax.ShapeDtypeStruct((WIDTH, WIDTH), F32),
            jax.ShapeDtypeStruct((1, WIDTH), F32),
        ),
        in_specs=[anywhere] * 6 + [vmem] * 5,
        out_specs=(anywhere,) * 2 + (vmem,) * 5,
        scratch_shapes=[
            pltpu.VMEM((2, cells, WIDTH), BF16),
            pltpu.VMEM((2, cells, EXPAND), BF16),
            pltpu.VMEM((2, cells, EXPAND), BF16),
            pltpu.VMEM((2, ROWS + 2, COLS, EXPAND), BF16),
            pltpu.VMEM((2, ROWS + 2, COLS, EXPAND), BF16),
            pltpu.VMEM((2, 2, 48, EXPAND), F32),
            pltpu.VMEM((2, 2, 48, EXPAND), F32),
            pltpu.VMEM((2, 2, ROWS, EXPAND), BF16),
            pltpu.VMEM((2, 2, ROWS, EXPAND), BF16),
            pltpu.VMEM((4, 16, EXPAND), BF16),
            pltpu.VMEM((4, 16, EXPAND), BF16),
            pltpu.VMEM((2, 2, BANDS, 8, EXPAND), F32),
            pltpu.VMEM((WIDTH, EXPAND), F32),
            pltpu.VMEM((16, EXPAND), F32),
            pltpu.VMEM((8, 272, 256), BF16),
            pltpu.VMEM((8, 272, 256), BF16),
            pltpu.VMEM((16, 32, 256), BF16),
            pltpu.VMEM((16, 32, 256), BF16),
            pltpu.VMEM((8, 272, 256), BF16),
            dma((6,)),
            dma((TILES,)),
            dma((TILES,)),
            dma((2,)),
            dma((8,)),
            dma((8,)),
            dma((BANDS,)),
            dma((8,)),
            dma((8,)),
            dma((8,)),
            dma((8,)),
            dma((16,)),
            dma((16,)),
            dma((16,)),
            dma((16,)),
            dma((8,)),
            dma((8,)),
        ],
        compiler_params=pltpu.CompilerParams(
            collective_id=1, has_side_effects=True, vmem_limit_bytes=56 * 2**20
        ),
        name="backward",
    )(back, act, slope, x, ends, columns, kern, wproj, gw, go, gg)


def on_device(expanded, skip, cotangent, depth_kernel, w_proj, norm_gain, w_qkv, w_out):
    cells = ROWS * COLS
    kern = depth_kernel.reshape(9, EXPAND)
    x = expanded[:, 0]
    act, slope, got_mix, got_cot, ends, columns = forward(
        x, skip.reshape(2, cells, WIDTH), cotangent.reshape(2, cells, WIDTH), kern, w_proj
    )
    back, grad_wqkv, grad_out, grad_gain = attention(got_mix, got_cot, norm_gain, w_qkv, w_out)
    scale = 1.0 / math.sqrt(2 * lax.axis_size("dp") * TILES * cells)
    ge, gs, gkern, gproj, gwqkv, gout, ggain = backward(
        back, act, slope, x, ends, columns, kern, w_proj, grad_wqkv, grad_out, grad_gain, scale
    )
    return (
        ge.reshape(2, 1, ROWS, COLS, EXPAND),
        gs.reshape(2, 1, ROWS, COLS, WIDTH),
        gkern.reshape(3, 3, EXPAND),
        gproj,
        gwqkv,
        gout,
        ggain.reshape(WIDTH),
    )


def solution(mesh):
    tiled = P("dp", ("row", "col"), None, None, None)
    return jax.shard_map(
        on_device,
        mesh=mesh,
        in_specs=(tiled, tiled, tiled, P(), P(), P(), P(), P()),
        out_specs=(tiled, tiled, P(), P(), P(), P(), P()),
        check_vma=False,
    )
```

```python
import math

import jax
import jax.numpy as jnp
import numpy as np
from jax import lax
from jax.experimental import pallas as pl
from jax.experimental.pallas import tpu as pltpu
from jax.sharding import PartitionSpec as P

GRID = 8
TILES = 64
ROWS = 32
COLS = 32
CELLS = ROWS * COLS
LANES = 128
WIDTH = 256
EXPAND = 1024
LANE_BLOCKS = EXPAND // LANES
STRIP = 4
STRIPS = ROWS // STRIP
STRIP_CELLS = STRIP * COLS
BAND = 8
BANDS = ROWS // BAND
BAND_CELLS = BAND * COLS
BAND_TILES = TILES // BANDS
SHARE = CELLS // TILES
F32 = jnp.float32
BF16 = jnp.bfloat16
MESH_ID = pl.DeviceIdType.MESH
GELU_1 = math.sqrt(2.0 / math.pi)
GELU_3 = GELU_1 * 0.044715
SIDES = ((0, -1), (0, 1))
ENDS = ((-1, 0), (1, 0))
CORNERS = ((-1, -1), (-1, 1), (1, -1), (1, 1))
AROUND = SIDES + ENDS + CORNERS


def dot(a, b):
    return lax.dot_general(a, b, (((1,), (0,)), ((), ())), preferred_element_type=F32)


def dot_t(a, b):
    return lax.dot_general(a, b, (((1,), (1,)), ((), ())), preferred_element_type=F32)


def dot_tl(a, b):
    return lax.dot_general(a, b, (((0,), (0,)), ((), ())), preferred_element_type=F32)


def tile_id(tile):
    return {"row": tile // 32, "col": lax.rem(tile, 32)}


def times(start, count, size=None):
    return pl.ds(pl.multiple_of(start * count, count), size or count)


def loop(begin, end, body):
    def one(i, carry):
        body(i)
        return carry

    lax.fori_loop(begin, end, one, 0)


def neighbours(me):
    tile_row, tile_col = me // GRID, lax.rem(me, GRID)
    return {
        (down, right): lax.rem(tile_row + down + GRID, GRID) * GRID + lax.rem(tile_col + right + GRID, GRID)
        for down in (-1, 0, 1)
        for right in (-1, 0, 1)
        if (down, right) != (0, 0)
    }


def rim_copies(me, picture, turn, grid_ref, sides_out, sides_in, corners_out, corners_in, send_sem, recv_sem):
    around = neighbours(me)
    copies = []
    for n, (down, right) in enumerate(AROUND):
        if down == 0:
            source = sides_out.at[(right + 1) // 2, picture]
            target = sides_in.at[(1 - right) // 2, picture]
        elif right == 0:
            source = grid_ref.at[picture, 1 if down < 0 else ROWS]
            target = grid_ref.at[picture, ROWS + 1 if down < 0 else 0]
        else:
            place = CORNERS.index((down, right))
            source = corners_out.at[picture, place]
            target = corners_in.at[picture, 3 - place]
        copies.append(
            pltpu.make_async_remote_copy(
                src_ref=source,
                dst_ref=target,
                send_sem=send_sem.at[turn, picture, n],
                recv_sem=recv_sem.at[turn, picture, n],
                device_id=tile_id(around[down, right]),
                device_id_type=MESH_ID,
            )
        )
    return copies


def collect_sides(picture, grid_ref, sides_out, corners_out):
    for side in range(2):
        for start in range(0, ROWS, 16):
            window = grid_ref[picture, 1 + start : 17 + start, 16 * side : 16 * side + 16, :]
            column = window.astype(F32)[:, 15 * side, :]
            sides_out[side, picture, start : start + 16, :] = column.astype(BF16)
    for place, (down, right) in enumerate(CORNERS):
        edge = 0 if down < 0 else 16
        row = 0 if down < 0 else 15
        one = sides_out[(right + 1) // 2, picture, edge : edge + 16, :].astype(F32)[row : row + 1]
        corners_out[picture, place] = jnp.concatenate([one, jnp.zeros((15, EXPAND), F32)], axis=0).astype(BF16)


def clear_outside(me, picture, grid_ref, sides_in, corners_in):
    tile_row, tile_col = me // GRID, lax.rem(me, GRID)
    none = jnp.zeros((16, EXPAND), BF16)
    for side, last in ((0, 0), (1, GRID - 1)):

        @pl.when(tile_col == last)
        def _():
            sides_in[side, picture] = jnp.zeros((ROWS, EXPAND), BF16)
            corners_in[picture, side] = none
            corners_in[picture, 2 + side] = none

    for end, last in ((0, 0), (1, GRID - 1)):

        @pl.when(tile_row == last)
        def _():
            grid_ref[picture, (ROWS + 1) * end] = jnp.zeros((COLS, EXPAND), BF16)
            corners_in[picture, 2 * end] = none
            corners_in[picture, 2 * end + 1] = none


def column_stack(picture, sides_in, corners_in, columns):
    blank = jnp.zeros((7, EXPAND), F32)
    for side in range(2):
        above = corners_in[picture, side].astype(F32)[0:1]
        below = corners_in[picture, 2 + side].astype(F32)[0:1]
        columns[side, picture, 0:8] = jnp.concatenate([blank, above], axis=0)
        columns[side, picture, 8 : 8 + ROWS] = sides_in[side, picture].astype(F32)
        columns[side, picture, 40:48] = jnp.concatenate([below, blank], axis=0)


def column_terms(picture, columns, weights, terms):
    for side in range(2):
        total = None
        for row_off in range(3):
            term = weights(row_off, 2 * side) * columns[side, picture, 7 + row_off : 7 + row_off + ROWS, :]
            total = term if total is None else total + term
        for strip in range(STRIPS):
            terms[side, picture, strip, 0:STRIP] = total[STRIP * strip : STRIP * strip + STRIP]


def convolve(rows, weights, left, right):
    spot = lax.broadcasted_iota(jnp.int32, (STRIP, COLS, LANES), 1)
    parts = []
    for col_off in range(3):
        total = None
        for row_off in range(3):
            term = weights[3 * row_off + col_off][None, :, :] * rows[row_off : row_off + STRIP]
            total = term if total is None else total + term
        parts.append(total)
    from_left = jnp.where(spot == 0, left[:, None, :], pltpu.roll(parts[0], 1, 1))
    from_right = jnp.where(spot == COLS - 1, right[:, None, :], pltpu.roll(parts[2], COLS - 1, 1))
    return parts[1] + from_left + from_right


def pick_heads(full, lane):
    halves = []
    for half in range(2):
        cols = slice(128 * half, 128 * half + 128)
        kept = full[256 * half : 256 * half + 64, cols]
        for h in range(1, 4):
            start = 256 * half + 64 * h
            kept = jnp.where(lane == h, full[start : start + 64, cols], kept)
        halves.append(kept)
    return jnp.concatenate(halves, axis=1)


def attend(mix, cot, gain, wqkv_ref, wout_ref, mask_ref, gw_ref, go_ref, gg_ref):
    scale = 1.0 / math.sqrt(32.0)
    lane = lax.broadcasted_iota(jnp.int32, (64, 128), 1) // 32
    mix = mix.astype(F32)
    inv = lax.rsqrt(jnp.mean(mix * mix, axis=-1, keepdims=True) + 1e-6)
    mi = mix * inv
    normed = (mi * gain).astype(BF16)
    qkv = dot(normed, wqkv_ref[...]).astype(BF16)
    gatt = dot_t(cot, wout_ref[...]).astype(BF16)
    att, gqs, gks, gvs = [], [], [], []
    for i in range(4):
        r = slice(64 * i, 64 * i + 64)
        q, k, v = qkv[r, 0:256], qkv[r, 256:512], qkv[r, 512:768]
        qexp = jnp.concatenate([q] * 8, axis=0) * mask_ref[...]
        doexp = jnp.concatenate([gatt[r]] * 8, axis=0) * mask_ref[...]
        st = dot_t(k, qexp) * scale
        e = jnp.exp(st - jnp.max(st, axis=0, keepdims=True))
        p = e * (1.0 / jnp.sum(e, axis=0, keepdims=True))
        pb = p.astype(BF16)
        dp = dot_t(v, doexp)
        ds = (p * (dp - jnp.sum(dp * p, axis=0, keepdims=True)) * scale).astype(BF16)
        att.append(pick_heads(dot_tl(pb, v), lane).astype(BF16))
        gqs.append(pick_heads(dot_tl(ds, k), lane).astype(BF16))
        gks.append(dot(ds, qexp).astype(BF16))
        gvs.append(dot(pb, doexp).astype(BF16))
    gqkv = [jnp.concatenate(x, axis=0) for x in (gqs, gks, gvs)]
    go_ref[...] += dot_tl(jnp.concatenate(att, axis=0), cot)
    normed_t = normed.T
    gn = jnp.zeros((256, 256), F32)
    for n in range(3):
        gw_ref[256 * n : 256 * n + 256] += dot(normed_t, gqkv[n])
        gn = gn + dot_t(gqkv[n], wqkv_ref[:, 256 * n : 256 * n + 256])
    gg_ref[...] += jnp.sum(gn * mi, axis=0, keepdims=True)
    scaled = gn * gain
    mean = jnp.mean(scaled * mix, axis=-1, keepdims=True)
    return (cot.astype(F32) + inv * scaled - mi * (inv * inv * mean)).astype(BF16)


def whole_kernel(
    x_hbm, skip_ref, cot_hbm, kern_ref, wproj_ref, gain_ref, wqkv_ref, wout_ref, perm_ref, mask_ref,
    ge_hbm, gs_hbm, whole_hbm, extra_out,
    xgrid, ggrid, act, dg, mix, got_mix, got_cot, mix_s, cot_s, back, gs,
    sides_out, sides_in, corners_out, corners_in, xcols, gcols, terms, gsides_out, gsides_in, gcorners_out, gcorners_in,
    gproj_t, gkern, gw_ref, go_ref, gg_ref, part_out, core_in, y_out, y_in, small_out, small_in, whole,
    ex_a, ex_b, ex_c,
    load_sem, rim_send, rim_recv, cot_send, cot_recv, mix_send, mix_recv, back_send, back_recv, own_sem, store_sem,
    core_send, core_recv, y_send, y_recv, z_send, z_recv, g_send, g_recv, gy_send, gy_recv,
    ey_send, ey_recv, ez_send, ez_recv,
):
    me = my_tile()
    tile_row, tile_col = me // GRID, lax.rem(me, GRID)
    dp, row, col = lax.axis_index("dp"), lax.axis_index("row"), lax.axis_index("col")
    core, chip = lax.rem(col, 2), col // 2
    q = dp * 2 + row
    mate = {"col": col + 1 - 2 * core}
    own = times(me, SHARE)

    def weight(n, lanes=slice(None)):
        return kern_ref[n // 3, n % 3 : n % 3 + 1, lanes]

    loads = [pltpu.make_async_copy(x_hbm.at[p], xgrid.at[p, pl.ds(1, ROWS)], load_sem.at[p]) for p in range(2)]
    for copy in loads:
        copy.start()
    barrier = pltpu.get_barrier_semaphore()

    def greet(i):
        pl.semaphore_signal(barrier, inc=1, device_id=tile_id(lax.rem(me + i, TILES)), device_id_type=MESH_ID)

    loop(1, TILES, greet)
    for n in range(2):
        pl.semaphore_signal(
            barrier, inc=1, device_id={"dp": 1 - dp, "row": n, "col": col}, device_id_type=MESH_ID
        )
    loads[0].wait()
    collect_sides(0, xgrid, sides_out, corners_out)
    pl.semaphore_wait(barrier, TILES + 1)

    def rim_of(picture, turn):
        if turn == 0:
            refs = (xgrid, sides_out, sides_in, corners_out, corners_in)
        else:
            refs = (ggrid, gsides_out, gsides_in, gcorners_out, gcorners_in)
        return rim_copies(me, picture, turn, *refs, rim_send, rim_recv)

    for copy in rim_of(0, 0):
        copy.start()
    loads[1].wait()
    collect_sides(1, xgrid, sides_out, corners_out)
    for copy in rim_of(1, 0):
        copy.start()

    def cot_copy(target, slot):
        return pltpu.make_async_remote_copy(
            src_ref=cot_hbm.at[:, times(target, SHARE), :],
            dst_ref=got_cot.at[:, times(slot, SHARE), :],
            send_sem=cot_send.at[target],
            recv_sem=cot_recv.at[slot],
            device_id=tile_id(target),
            device_id_type=MESH_ID,
        )

    def mix_copy(picture, target, slot):
        return pltpu.make_async_remote_copy(
            src_ref=mix.at[picture, times(target, SHARE), :],
            dst_ref=got_mix.at[picture, times(slot, SHARE), :],
            send_sem=mix_send.at[picture, target],
            recv_sem=mix_recv.at[picture, slot],
            device_id=tile_id(target),
            device_id_type=MESH_ID,
        )

    def back_copy(picture, target, slot):
        return pltpu.make_async_remote_copy(
            src_ref=back.at[picture, times(target, SHARE), :],
            dst_ref=gs.at[picture, times(slot, SHARE), :],
            send_sem=back_send.at[picture, target],
            recv_sem=back_recv.at[picture, slot],
            device_id=tile_id(target),
            device_id_type=MESH_ID,
        )

    loop(1, TILES, lambda i: cot_copy(lax.rem(me + i, TILES), me).start())
    own_cot = pltpu.make_async_copy(cot_hbm.at[:, own, :], got_cot.at[:, own, :], own_sem.at[0])
    own_cot.start()


    def forward_picture(picture):
        rim = rim_of(picture, 0)
        for copy in rim:
            copy.wait_recv()
        clear_outside(me, picture, xgrid, sides_in, corners_in)
        column_stack(picture, sides_in, corners_in, xcols)
        column_terms(picture, xcols, lambda a, c: weight(3 * a + c), terms)

        def do_band(step):
            band = lax.rem(step + tile_row // 2, BANDS)
            cells = times(band, BAND_CELLS)

            def do_block(index):
                strip = band * 2 + index // LANE_BLOCKS
                lanes = times(lax.rem(index, LANE_BLOCKS), LANES)
                rows = xgrid[picture, pl.ds(strip * STRIP, STRIP + 2), :, lanes].astype(F32)
                pre = convolve(
                    rows,
                    [weight(n, lanes) for n in range(9)],
                    terms[0, picture, strip, 0:STRIP, lanes],
                    terms[1, picture, strip, 0:STRIP, lanes],
                )
                square = pre * pre
                tanh = jnp.tanh(pre * (GELU_1 + GELU_3 * square))
                half = 0.5 * pre
                activated = half + half * tanh
                slope = (0.5 + 0.5 * tanh) + half * (1.0 - tanh * tanh) * (GELU_1 + (3.0 * GELU_3) * square)
                here = times(strip, STRIP_CELLS)
                act[picture, here, lanes] = activated.astype(BF16).reshape(STRIP_CELLS, LANES)
                dg[picture, here, lanes] = slope.astype(BF16).reshape(STRIP_CELLS, LANES)

            loop(0, 2 * LANE_BLOCKS, do_block)
            projected = dot(act[picture, cells, :], wproj_ref[...])
            mix[picture, cells, :] = (skip_ref[picture, cells, :].astype(F32) + projected).astype(BF16)

            def send_mix(i):
                target = band * BAND_TILES + lax.rem(me + i, BAND_TILES)

                @pl.when(target != me)
                def _():
                    mix_copy(picture, target, me).start()

            loop(0, BAND_TILES, send_mix)

        loop(0, BANDS, do_band)

    loop(0, 2, forward_picture)


    gw_ref[...] = jnp.zeros_like(gw_ref)
    go_ref[...] = jnp.zeros_like(go_ref)
    gg_ref[...] = jnp.zeros_like(gg_ref)
    gproj_t[...] = jnp.zeros_like(gproj_t)
    own_cot.wait()
    loop(1, TILES, lambda i: cot_copy(lax.rem(me + i, TILES), lax.rem(me + i, TILES)).wait_recv())

    def attend_picture(picture):
        own_mix = pltpu.make_async_copy(mix.at[picture, own, :], got_mix.at[picture, own, :], own_sem.at[1])
        own_mix.start()
        perm = perm_ref[...]
        for b in range(4):
            r = slice(256 * b, 256 * b + 256)
            cot_s[:, 16 * b : 16 * b + 16, :] = dot(perm, got_cot[picture, r, :]).astype(BF16).reshape(16, 16, 256)
        loop(1, TILES, lambda i: mix_copy(picture, lax.rem(me + i, TILES), lax.rem(me + i, TILES)).wait_recv())
        own_mix.wait()
        for b in range(4):
            r = slice(256 * b, 256 * b + 256)
            mix_s[:, 16 * b : 16 * b + 16, :] = dot(perm, got_mix[picture, r, :]).astype(BF16).reshape(16, 16, 256)

        def block(b):
            groups = pl.ds(b * 4, 4)
            out = attend(
                mix_s[groups].reshape(256, 256), cot_s[groups].reshape(256, 256), gain_ref[...],
                wqkv_ref, wout_ref, mask_ref, gw_ref, go_ref, gg_ref,
            )
            cot_s[groups] = out.reshape(4, 64, 256)

        loop(0, 4, block)
        for b in range(4):
            rows = cot_s[:, 16 * b : 16 * b + 16, :].reshape(256, 256)
            back[picture, 256 * b : 256 * b + 256] = dot(perm, rows).astype(BF16)

        def send_back(i):
            target = lax.rem(tile_row + GRID - i // GRID, GRID) * GRID + lax.rem(
                tile_col + GRID - lax.rem(i, GRID), GRID
            )
            back_copy(picture, target, me).start()

        loop(1, TILES, send_back)
        own_back = pltpu.make_async_copy(back.at[picture, own, :], gs.at[picture, own, :], own_sem.at[2])
        own_back.start()
        own_back.wait()

    loop(0, 2, attend_picture)


    def core_copy(half):
        return pltpu.make_async_remote_copy(
            src_ref=part_out.at[pl.ds(2 * half, 2), 1 - core],
            dst_ref=core_in.at[pl.ds(2 * half, 2)],
            send_sem=core_send.at[half],
            recv_sem=core_recv.at[half],
            device_id=mate,
            device_id_type=MESH_ID,
        )

    def remote(source, target, send, recv, device):
        return pltpu.make_async_remote_copy(
            src_ref=source, dst_ref=target, send_sem=send, recv_sem=recv, device_id=device, device_id_type=MESH_ID
        )

    def y_id(n):
        return {"dp": n // 2, "row": lax.rem(n, 2)}

    def z_id(n):
        return {"col": n * 2 + core}

    def y_copy(to, slot):
        return remote(y_out.at[to], y_in.at[slot], y_send.at[to], y_recv.at[slot], y_id(to))

    def z_copy(to, slot):
        return remote(small_out.at[times(to, 16)], small_in.at[slot], z_send.at[to], z_recv.at[slot], z_id(to))

    def g_copy(to, slot):
        return remote(
            whole.at[q, core, times(chip, 16)], whole.at[q, core, times(slot, 16)],
            g_send.at[to], g_recv.at[slot], z_id(to),
        )

    def gy_copy(to, slot):
        return remote(whole.at[q, core], whole.at[slot, core], gy_send.at[to], gy_recv.at[slot], y_id(to))

    def ey_copy(to, slot):
        return remote(ex_b.at[q], ex_b.at[slot], ey_send.at[to], ey_recv.at[slot], y_id(to))

    def ez_copy(to, slot):
        return remote(ex_c.at[chip], ex_c.at[slot], ez_send.at[to], ez_recv.at[slot], z_id(to))

    def others(count, mine, action):
        loop(1, count, lambda i: action(lax.rem(mine + i, count)))

    def core_sum(half):
        core_copy(half).wait_recv()
        for n in (2 * half, 2 * half + 1):
            y_out[n] = (part_out[n, core].astype(F32) + core_in[n].astype(F32)).astype(BF16)

            @pl.when(q != n)
            def _():
                y_copy(n, q).start()

    for n in range(4):
        block = gw_ref[256 * n : 256 * n + 256] if n < 3 else go_ref[...]
        part_out[2 + n // 2, n % 2] = block.astype(BF16)
    core_copy(1).start()


    spot = lax.broadcasted_iota(jnp.int32, (STRIP, COLS, LANES), 1)
    gkern[...] = jnp.zeros_like(gkern)

    def back_picture(picture):
        def do_band(step):
            band = lax.rem(step + tile_row // 2, BANDS)
            cells = times(band, BAND_CELLS)

            def arrived(i):
                source = band * BAND_TILES + i

                @pl.when(source != me)
                def _():
                    back_copy(picture, source, source).wait_recv()

            loop(0, BAND_TILES, arrived)
            flat = gs[picture, cells, :]
            flat_t = flat.T
            for n in range(4):
                lanes = slice(256 * n, 256 * n + 256)
                grad_act = dot_t(flat, wproj_ref[lanes, :])
                grad_pre = (grad_act * dg[picture, cells, lanes].astype(F32)).astype(BF16)
                ggrid[picture, pl.ds(1 + band * BAND, BAND), :, lanes] = grad_pre.reshape(BAND, COLS, 256)
                gproj_t[:, lanes] += dot(flat_t, act[picture, cells, lanes])

        loop(0, BANDS, do_band)
        collect_sides(picture, ggrid, gsides_out, gcorners_out)
        for copy in rim_of(picture, 1):
            copy.start()

        @pl.when(picture == 0)
        def _():
            core_sum(1)

        @pl.when(picture == 1)
        def _():
            for n in range(4):
                part_out[n // 2, n % 2] = gproj_t[:, 256 * n : 256 * n + 256].T.astype(BF16)
            core_copy(0).start()

        def kernel_block(block):
            lanes = times(block, LANES)

            def one(strip, sums):
                grads = ggrid[picture, pl.ds(1 + strip * STRIP, STRIP), :, lanes].astype(F32)
                rows = xgrid[picture, pl.ds(strip * STRIP, STRIP + 2), :, lanes].astype(F32)
                shifted = (
                    jnp.where(spot == COLS - 1, 0.0, pltpu.roll(grads, COLS - 1, 1)),
                    grads,
                    jnp.where(spot == 0, 0.0, pltpu.roll(grads, 1, 1)),
                )
                new = []
                for row_off in range(3):
                    for col_off in range(3):
                        product = shifted[col_off] * rows[row_off : row_off + STRIP]
                        product = product.reshape(STRIP * 4, 8, LANES).sum(axis=0)
                        new.append(sums[3 * row_off + col_off] + product)
                return tuple(new)

            sums = lax.fori_loop(0, STRIPS, one, tuple(jnp.zeros((8, LANES), F32) for _ in range(9)))
            for n in range(9):
                gkern[n : n + 1, lanes] += jnp.sum(sums[n], axis=0, keepdims=True)

        loop(0, LANE_BLOCKS // 2, kernel_block)

        @pl.when(picture == 1)
        def _():
            core_sum(0)

        loop(LANE_BLOCKS // 2, LANE_BLOCKS, kernel_block)
        for row_off in range(3):
            for side in range(2):
                n = 3 * row_off + 2 * side
                beside = xcols[side, picture, 7 + row_off : 7 + row_off + ROWS, :]
                gkern[n : n + 1, :] += jnp.sum(
                    gsides_out[side, picture].astype(F32) * beside, axis=0, keepdims=True
                )

    loop(0, 2, back_picture)
    gs_store = pltpu.make_async_copy(gs, gs_hbm, own_sem.at[3])
    gs_store.start()


    extra = [gkern[0:9, 256 * n : 256 * n + 256] for n in range(4)]
    extra = jnp.concatenate(extra + [gg_ref[...], jnp.zeros((11, 256), F32)], axis=0).astype(BF16)
    ex_a[core] = extra
    ex_core = remote(ex_a.at[core], ex_a.at[core], core_send.at[2], core_recv.at[2], mate)
    ex_core.start()

    def total_of(ref, count):
        total = ref[0].astype(F32)
        for n in range(1, count):
            total = total + ref[n].astype(F32)
        return total

    others(4, q, lambda n: y_copy(n, n).wait_recv())
    y_in[q] = y_out[q]
    small_out[...] = total_of(y_in, 4).astype(BF16)
    others(16, chip, lambda n: z_copy(n, chip).start())
    ex_core.wait_recv()
    ex_b[q] = total_of(ex_a, 2).astype(BF16)
    others(4, q, lambda n: ey_copy(n, q).start())

    def store_copy(picture, band):
        cells = times(band, BAND_CELLS)
        return pltpu.make_async_copy(dg.at[picture, cells, :], ge_hbm.at[picture, cells, :], store_sem.at[picture, band])

    def last_start(picture):
        for copy in rim_of(picture, 1):
            copy.wait_recv()
        clear_outside(me, picture, ggrid, gsides_in, gcorners_in)
        column_stack(picture, gsides_in, gcorners_in, gcols)
        column_terms(picture, gcols, lambda a, c: weight(8 - 3 * a - c), terms)

    def last_bands(picture, begin, end):
        def do_band(band):
            def do_block(index):
                strip = band * 2 + index // LANE_BLOCKS
                lanes = times(lax.rem(index, LANE_BLOCKS), LANES)
                rows = ggrid[picture, pl.ds(strip * STRIP, STRIP + 2), :, lanes].astype(F32)
                total = convolve(
                    rows,
                    [weight(8 - n, lanes) for n in range(9)],
                    terms[0, picture, strip, 0:STRIP, lanes],
                    terms[1, picture, strip, 0:STRIP, lanes],
                )
                dg[picture, times(strip, STRIP_CELLS), lanes] = total.astype(BF16).reshape(STRIP_CELLS, LANES)

            loop(0, 2 * LANE_BLOCKS, do_block)
            store_copy(picture, band).start()

        loop(begin, end, do_band)

    last_start(0)
    last_bands(0, 0, 4)

    others(16, chip, lambda n: z_copy(n, n).wait_recv())
    small_in[chip] = small_out[times(chip, 16)]
    whole[q, core, times(chip, 16)] = total_of(small_in, 16).astype(BF16)
    others(16, chip, lambda n: g_copy(n, chip).start())
    others(4, q, lambda n: ey_copy(n, n).wait_recv())
    ex_c[chip] = total_of(ex_b, 4).astype(BF16)
    others(16, chip, lambda n: ez_copy(n, chip).start())

    last_start(1)
    last_bands(1, 0, 3)

    others(16, chip, lambda n: g_copy(n, n).wait_recv())
    others(4, q, lambda n: gy_copy(n, q).start())

    last_bands(1, 3, 4)

    others(16, chip, lambda n: ez_copy(n, n).wait_recv())
    extra_out[...] = total_of(ex_c, 16)


    def sent(i):
        peer = lax.rem(me + i, TILES)
        cot_copy(peer, peer).wait_send()
        for picture in range(2):
            mix_copy(picture, peer, peer).wait_send()
            back_copy(picture, peer, peer).wait_send()

    loop(1, TILES, sent)
    for turn in range(2):
        for picture in range(2):
            for copy in rim_of(picture, turn):
                copy.wait_send()
    for half in range(2):
        core_copy(half).wait_send()
    ex_core.wait_send()
    others(4, q, lambda n: y_copy(n, n).wait_send())
    others(4, q, lambda n: ey_copy(n, n).wait_send())
    others(16, chip, lambda n: z_copy(n, n).wait_send())
    others(16, chip, lambda n: g_copy(n, n).wait_send())
    others(16, chip, lambda n: ez_copy(n, n).wait_send())
    gs_store.wait()
    for picture in range(2):
        for band in range(BANDS):
            store_copy(picture, band).wait()
    others(4, q, lambda n: gy_copy(n, n).wait_recv())
    to_mate = remote(whole.at[:, core], whole.at[:, core], core_send.at[3], core_recv.at[3], mate)
    to_mate.start()
    others(4, q, lambda n: gy_copy(n, n).wait_send())
    to_mate.wait_recv()
    to_mate.wait_send()
    whole_store = pltpu.make_async_copy(whole, whole_hbm, own_sem.at[4])
    whole_store.start()
    whole_store.wait()


def my_tile():
    return lax.axis_index("row") * 32 + lax.axis_index("col")


def constants():
    perm = np.zeros((256, 256), np.float32)
    for a in range(16):
        for b in range(16):
            perm[a * 16 + b, b * 16 + a] = 1
    mask = np.kron(np.eye(8), np.ones((64, 32))).astype(np.float32)
    return jnp.asarray(perm, BF16), jnp.asarray(mask, BF16)


def whole_call(x, skip, cot, kern, wproj, gain, wqkv, wout):
    vmem = pl.BlockSpec(memory_space=pltpu.VMEM)
    anywhere = pl.BlockSpec(memory_space=pl.ANY)
    dma = pltpu.SemaphoreType.DMA

    def bf(*shape):
        return pltpu.VMEM(shape, BF16)

    def fl(*shape):
        return pltpu.VMEM(shape, F32)

    rims = [bf(2, 2, ROWS, EXPAND), bf(2, 2, ROWS, EXPAND), bf(2, 4, 16, EXPAND), bf(2, 4, 16, EXPAND)]
    return pl.pallas_call(
        whole_kernel,
        out_shape=(
            jax.ShapeDtypeStruct((2, CELLS, EXPAND), BF16),
            jax.ShapeDtypeStruct((2, CELLS, WIDTH), BF16),
            jax.ShapeDtypeStruct((4, 2, 256, 256), BF16),
            jax.ShapeDtypeStruct((48, 256), F32),
        ),
        in_specs=[anywhere, vmem, anywhere] + [vmem] * 7,
        out_specs=(anywhere, anywhere, anywhere, vmem),
        scratch_shapes=[
            bf(2, ROWS + 2, COLS, EXPAND), bf(2, ROWS + 2, COLS, EXPAND), bf(2, CELLS, EXPAND), bf(2, CELLS, EXPAND),
            bf(2, CELLS, WIDTH), bf(2, CELLS, WIDTH), bf(2, CELLS, WIDTH), bf(16, 64, WIDTH), bf(16, 64, WIDTH),
            bf(2, CELLS, WIDTH), bf(2, CELLS, WIDTH),
        ]
        + rims
        + [fl(2, 2, 48, EXPAND), fl(2, 2, 48, EXPAND), fl(2, 2, STRIPS, 8, EXPAND)]
        + rims
        + [
            fl(WIDTH, EXPAND), fl(16, EXPAND), fl(3 * WIDTH, WIDTH), fl(WIDTH, WIDTH), fl(1, WIDTH),
            bf(4, 2, 256, 256), bf(4, 256, 256), bf(4, 256, 256), bf(4, 256, 256),
            bf(256, 256), bf(16, 16, 256), bf(4, 2, 256, 256),
            bf(2, 48, 256), bf(4, 48, 256), bf(16, 48, 256),
            dma((2,)), dma((2, 2, 8)), dma((2, 2, 8)), dma((TILES,)), dma((TILES,)),
            dma((2, TILES)), dma((2, TILES)), dma((2, TILES)), dma((2, TILES)), dma((5,)), dma((2, BANDS)),
            dma((4,)), dma((4,)), dma((4,)), dma((4,)), dma((16,)), dma((16,)), dma((16,)), dma((16,)),
            dma((4,)), dma((4,)), dma((4,)), dma((4,)), dma((16,)), dma((16,)),
        ],
        compiler_params=pltpu.CompilerParams(
            collective_id=0, has_side_effects=True, vmem_limit_bytes=56 * 2**20
        ),
        name="whole",
    )(x, skip, cot, kern, wproj, gain, wqkv, wout, *constants())


def finish_kernel(
    ge_hbm, gs_hbm, whole_ref, extra_ref, ge_out, gs_out, gkern_out, gproj_out, gwqkv_out, gout_out, ggain_out, sems, *, scale
):
    copies = []
    for picture in range(2):
        for part in range(2):
            rows = pl.ds(512 * part, 512)
            copies.append(
                pltpu.make_async_copy(
                    ge_hbm.at[picture, rows], ge_out.at[picture, rows], sems.at[2 * picture + part]
                )
            )
    copies.append(pltpu.make_async_copy(gs_hbm, gs_out, sems.at[4]))
    for copy in copies:
        copy.start()
    for n in range(8):
        block = whole_ref[n // 2, n % 2].astype(F32) * scale
        if n < 4:
            gproj_out[256 * n : 256 * n + 256, :] = block
            some = extra_ref[9 * n : 9 * n + 9, :] * scale
            for row in range(3):
                gkern_out[row, :, 256 * n : 256 * n + 256] = some[3 * row : 3 * row + 3]
        elif n < 7:
            gwqkv_out[:, 256 * (n - 4) : 256 * (n - 4) + 256] = block
        else:
            gout_out[...] = block
    ggain_out[...] = extra_ref[36:37, :] * scale
    for copy in copies:
        copy.wait()


def finish(ge, gs, whole, extra, scale):
    vmem = pl.BlockSpec(memory_space=pltpu.VMEM)
    anywhere = pl.BlockSpec(memory_space=pl.ANY)

    def kernel(*refs):
        finish_kernel(*refs, scale=scale)

    return pl.pallas_call(
        kernel,
        out_shape=(
            jax.ShapeDtypeStruct((2, CELLS, EXPAND), BF16),
            jax.ShapeDtypeStruct((2, CELLS, WIDTH), BF16),
            jax.ShapeDtypeStruct((3, 3, EXPAND), F32),
            jax.ShapeDtypeStruct((EXPAND, WIDTH), F32),
            jax.ShapeDtypeStruct((WIDTH, 3 * WIDTH), F32),
            jax.ShapeDtypeStruct((WIDTH, WIDTH), F32),
            jax.ShapeDtypeStruct((1, WIDTH), F32),
        ),
        in_specs=[anywhere, anywhere, vmem, vmem],
        out_specs=(anywhere,) * 2 + (vmem,) * 5,
        scratch_shapes=[pltpu.SemaphoreType.DMA((5,))],
        compiler_params=pltpu.CompilerParams(vmem_limit_bytes=32 * 2**20),
        name="finish",
    )(ge, gs, whole, extra)


def on_device(expanded, skip, cotangent, depth_kernel, w_proj, norm_gain, w_qkv, w_out):
    ge, gs, whole, extra = whole_call(
        expanded[:, 0],
        skip.reshape(2, CELLS, WIDTH),
        cotangent.reshape(2, CELLS, WIDTH),
        depth_kernel,
        w_proj,
        norm_gain.reshape(1, WIDTH),
        w_qkv,
        w_out,
    )
    scale = 1.0 / math.sqrt(2 * lax.axis_size("dp") * TILES * CELLS)
    ge, gs, gkern, gproj, gwqkv, gout, ggain = finish(ge, gs, whole, extra, scale)
    return (
        ge.reshape(2, 1, ROWS, COLS, EXPAND),
        gs.reshape(2, 1, ROWS, COLS, WIDTH),
        gkern,
        gproj,
        gwqkv,
        gout,
        ggain.reshape(WIDTH),
    )


def solution(mesh):
    tiled = P("dp", ("row", "col"), None, None, None)
    return jax.shard_map(
        on_device,
        mesh=mesh,
        in_specs=(tiled, tiled, tiled, P(), P(), P(), P(), P()),
        out_specs=(tiled, tiled, P(), P(), P(), P(), P()),
        check_vma=False,
    )
```

```python
import math

import jax
import jax.numpy as jnp
import numpy as np
from jax import lax
from jax.experimental import pallas as pl
from jax.experimental.pallas import tpu as pltpu
from jax.sharding import PartitionSpec as P

GRID = 8
TILES = 64
ROWS = 32
COLS = 32
CELLS = ROWS * COLS
LANES = 128
WIDTH = 256
EXPAND = 1024
LANE_BLOCKS = EXPAND // LANES
STRIP = 4
STRIPS = ROWS // STRIP
STRIP_CELLS = STRIP * COLS
BAND = 8
BANDS = ROWS // BAND
BAND_CELLS = BAND * COLS
BAND_TILES = TILES // BANDS
SHARE = CELLS // TILES
F32 = jnp.float32
BF16 = jnp.bfloat16
MESH_ID = pl.DeviceIdType.MESH
GELU_1 = math.sqrt(2.0 / math.pi)
GELU_3 = GELU_1 * 0.044715
SIDES = ((0, -1), (0, 1))
ENDS = ((-1, 0), (1, 0))
CORNERS = ((-1, -1), (-1, 1), (1, -1), (1, 1))
AROUND = SIDES + ENDS + CORNERS


def dot(a, b):
    return lax.dot_general(a, b, (((1,), (0,)), ((), ())), preferred_element_type=F32)


def dot_t(a, b):
    return lax.dot_general(a, b, (((1,), (1,)), ((), ())), preferred_element_type=F32)


def dot_tl(a, b):
    return lax.dot_general(a, b, (((0,), (0,)), ((), ())), preferred_element_type=F32)


def tile_id(tile):
    return {"row": tile // 32, "col": lax.rem(tile, 32)}


def times(start, count, size=None):
    return pl.ds(pl.multiple_of(start * count, count), size or count)


def loop(begin, end, body):
    def one(i, carry):
        body(i)
        return carry

    lax.fori_loop(begin, end, one, 0)


def neighbours(me):
    tile_row, tile_col = me // GRID, lax.rem(me, GRID)
    return {
        (down, right): lax.rem(tile_row + down + GRID, GRID) * GRID + lax.rem(tile_col + right + GRID, GRID)
        for down in (-1, 0, 1)
        for right in (-1, 0, 1)
        if (down, right) != (0, 0)
    }


def rim_copies(me, picture, turn, grid_ref, sides_out, sides_in, corners_out, corners_in, send_sem, recv_sem):
    around = neighbours(me)
    copies = []
    for n, (down, right) in enumerate(AROUND):
        if down == 0:
            source = sides_out.at[(right + 1) // 2, picture]
            target = sides_in.at[(1 - right) // 2, picture]
        elif right == 0:
            source = grid_ref.at[picture, 1 if down < 0 else ROWS]
            target = grid_ref.at[picture, ROWS + 1 if down < 0 else 0]
        else:
            place = CORNERS.index((down, right))
            source = corners_out.at[picture, place]
            target = corners_in.at[picture, 3 - place]
        copies.append(
            pltpu.make_async_remote_copy(
                src_ref=source,
                dst_ref=target,
                send_sem=send_sem.at[turn, picture, n],
                recv_sem=recv_sem.at[turn, picture, n],
                device_id=tile_id(around[down, right]),
                device_id_type=MESH_ID,
            )
        )
    return copies


def collect_sides(picture, grid_ref, sides_out, corners_out):
    for side in range(2):
        for start in range(0, ROWS, 16):
            window = grid_ref[picture, 1 + start : 17 + start, 16 * side : 16 * side + 16, :]
            column = window.astype(F32)[:, 15 * side, :]
            sides_out[side, picture, start : start + 16, :] = column.astype(BF16)
    for place, (down, right) in enumerate(CORNERS):
        edge = 0 if down < 0 else 16
        row = 0 if down < 0 else 15
        one = sides_out[(right + 1) // 2, picture, edge : edge + 16, :].astype(F32)[row : row + 1]
        corners_out[picture, place] = jnp.concatenate([one, jnp.zeros((15, EXPAND), F32)], axis=0).astype(BF16)


def clear_outside(me, picture, grid_ref, sides_in, corners_in):
    tile_row, tile_col = me // GRID, lax.rem(me, GRID)
    none = jnp.zeros((16, EXPAND), BF16)
    for side, last in ((0, 0), (1, GRID - 1)):

        @pl.when(tile_col == last)
        def _():
            sides_in[side, picture] = jnp.zeros((ROWS, EXPAND), BF16)
            corners_in[picture, side] = none
            corners_in[picture, 2 + side] = none

    for end, last in ((0, 0), (1, GRID - 1)):

        @pl.when(tile_row == last)
        def _():
            grid_ref[picture, (ROWS + 1) * end] = jnp.zeros((COLS, EXPAND), BF16)
            corners_in[picture, 2 * end] = none
            corners_in[picture, 2 * end + 1] = none


def column_stack(picture, sides_in, corners_in, columns):
    blank = jnp.zeros((7, EXPAND), F32)
    for side in range(2):
        above = corners_in[picture, side].astype(F32)[0:1]
        below = corners_in[picture, 2 + side].astype(F32)[0:1]
        columns[side, picture, 0:8] = jnp.concatenate([blank, above], axis=0)
        columns[side, picture, 8 : 8 + ROWS] = sides_in[side, picture].astype(F32)
        columns[side, picture, 40:48] = jnp.concatenate([below, blank], axis=0)


def column_terms(picture, columns, weights, terms):
    for side in range(2):
        total = None
        for row_off in range(3):
            term = weights(row_off, 2 * side) * columns[side, picture, 7 + row_off : 7 + row_off + ROWS, :]
            total = term if total is None else total + term
        for strip in range(STRIPS):
            terms[side, picture, strip, 0:STRIP] = total[STRIP * strip : STRIP * strip + STRIP]


def convolve(rows, weights, left, right):
    spot = lax.broadcasted_iota(jnp.int32, (STRIP, COLS, LANES), 1)
    parts = []
    for col_off in range(3):
        total = None
        for row_off in range(3):
            term = weights[3 * row_off + col_off][None, :, :] * rows[row_off : row_off + STRIP]
            total = term if total is None else total + term
        parts.append(total)
    from_left = jnp.where(spot == 0, left[:, None, :], pltpu.roll(parts[0], 1, 1))
    from_right = jnp.where(spot == COLS - 1, right[:, None, :], pltpu.roll(parts[2], COLS - 1, 1))
    return parts[1] + from_left + from_right


def pick_heads(full, lane):
    halves = []
    for half in range(2):
        cols = slice(128 * half, 128 * half + 128)
        kept = full[256 * half : 256 * half + 64, cols]
        for h in range(1, 4):
            start = 256 * half + 64 * h
            kept = jnp.where(lane == h, full[start : start + 64, cols], kept)
        halves.append(kept)
    return jnp.concatenate(halves, axis=1)


def attend(mix, cot, gain, wqkv_ref, wout_ref, mask_ref, gw_ref, go_ref, gg_ref):
    scale = 1.0 / math.sqrt(32.0)
    lane = lax.broadcasted_iota(jnp.int32, (64, 128), 1) // 32
    mix = mix.astype(F32)
    inv = lax.rsqrt(jnp.mean(mix * mix, axis=-1, keepdims=True) + 1e-6)
    mi = mix * inv
    normed = (mi * gain).astype(BF16)
    qkv = dot(normed, wqkv_ref[...]).astype(BF16)
    gatt = dot_t(cot, wout_ref[...]).astype(BF16)
    att, gqs, gks, gvs = [], [], [], []
    for i in range(4):
        r = slice(64 * i, 64 * i + 64)
        q, k, v = qkv[r, 0:256], qkv[r, 256:512], qkv[r, 512:768]
        qexp = jnp.concatenate([q] * 8, axis=0) * mask_ref[...]
        doexp = jnp.concatenate([gatt[r]] * 8, axis=0) * mask_ref[...]
        st = dot_t(k, qexp) * scale
        e = jnp.exp(st - jnp.max(st, axis=0, keepdims=True))
        p = e * (1.0 / jnp.sum(e, axis=0, keepdims=True))
        pb = p.astype(BF16)
        dp = dot_t(v, doexp)
        ds = (p * (dp - jnp.sum(dp * p, axis=0, keepdims=True)) * scale).astype(BF16)
        att.append(pick_heads(dot_tl(pb, v), lane).astype(BF16))
        gqs.append(pick_heads(dot_tl(ds, k), lane).astype(BF16))
        gks.append(dot(ds, qexp).astype(BF16))
        gvs.append(dot(pb, doexp).astype(BF16))
    gqkv = [jnp.concatenate(x, axis=0) for x in (gqs, gks, gvs)]
    go_ref[...] += dot_tl(jnp.concatenate(att, axis=0), cot)
    normed_t = normed.T
    gn = jnp.zeros((256, 256), F32)
    for n in range(3):
        gw_ref[256 * n : 256 * n + 256] += dot(normed_t, gqkv[n])
        gn = gn + dot_t(gqkv[n], wqkv_ref[:, 256 * n : 256 * n + 256])
    gg_ref[...] += jnp.sum(gn * mi, axis=0, keepdims=True)
    scaled = gn * gain
    mean = jnp.mean(scaled * mix, axis=-1, keepdims=True)
    return (cot.astype(F32) + inv * scaled - mi * (inv * inv * mean)).astype(BF16)


def whole_kernel(
    x_hbm, skip_ref, cot_hbm, kern_ref, wproj_ref, gain_ref, wqkv_ref, wout_ref, perm_ref, mask_ref,
    ge_hbm, gs_hbm, whole_hbm, extra_out,
    xgrid, ggrid, act, dg, mix, got_mix, got_cot, mix_s, cot_s, back, gs,
    sides_out, sides_in, corners_out, corners_in, xcols, gcols, terms, gsides_out, gsides_in, gcorners_out, gcorners_in,
    gproj_t, gkern, gw_ref, go_ref, gg_ref, part_out, core_in, y_out, y_in, small_out, small_in, whole,
    ex_a, ex_b, ex_c,
    load_sem, rim_send, rim_recv, cot_sem, mix_sem, back_send, back_recv, own_sem, store_sem,
    core_send, core_recv, y_sem, z_sem, g_sem, gy_sem, ey_sem, ez_sem,
):
    me = my_tile()
    tile_row, tile_col = me // GRID, lax.rem(me, GRID)
    dp, row, col = lax.axis_index("dp"), lax.axis_index("row"), lax.axis_index("col")
    core, chip = lax.rem(col, 2), col // 2
    q = dp * 2 + row
    mate = {"col": col + 1 - 2 * core}
    own = times(me, SHARE)

    def weight(n, lanes=slice(None)):
        return kern_ref[n // 3, n % 3 : n % 3 + 1, lanes]

    loads = [pltpu.make_async_copy(x_hbm.at[p], xgrid.at[p, pl.ds(1, ROWS)], load_sem.at[p]) for p in range(2)]
    for copy in loads:
        copy.start()
    barrier = pltpu.get_barrier_semaphore()

    def greet(i):
        pl.semaphore_signal(barrier, inc=1, device_id=tile_id(lax.rem(me + i, TILES)), device_id_type=MESH_ID)

    loop(1, TILES, greet)
    for n in range(2):
        pl.semaphore_signal(
            barrier, inc=1, device_id={"dp": 1 - dp, "row": n, "col": col}, device_id_type=MESH_ID
        )
    loads[0].wait()
    collect_sides(0, xgrid, sides_out, corners_out)
    pl.semaphore_wait(barrier, TILES + 1)

    def rim_of(picture, turn):
        if turn == 0:
            refs = (xgrid, sides_out, sides_in, corners_out, corners_in)
        else:
            refs = (ggrid, gsides_out, gsides_in, gcorners_out, gcorners_in)
        return rim_copies(me, picture, turn, *refs, rim_send, rim_recv)

    for copy in rim_of(0, 0):
        copy.start()
    loads[1].wait()
    collect_sides(1, xgrid, sides_out, corners_out)
    for copy in rim_of(1, 0):
        copy.start()

    def cot_copy(target, slot):
        return pltpu.make_async_remote_copy(
            src_ref=cot_hbm.at[:, times(target, SHARE), :],
            dst_ref=got_cot.at[:, times(slot, SHARE), :],
            send_sem=cot_sem.at[0],
            recv_sem=cot_sem.at[1],
            device_id=tile_id(target),
            device_id_type=MESH_ID,
        )

    def mix_copy(picture, target, slot):
        return pltpu.make_async_remote_copy(
            src_ref=mix.at[picture, times(target, SHARE), :],
            dst_ref=got_mix.at[picture, times(slot, SHARE), :],
            send_sem=mix_sem.at[0, picture],
            recv_sem=mix_sem.at[1, picture],
            device_id=tile_id(target),
            device_id_type=MESH_ID,
        )

    def back_copy(picture, target, slot):
        return pltpu.make_async_remote_copy(
            src_ref=back.at[picture, times(target, SHARE), :],
            dst_ref=gs.at[picture, times(slot, SHARE), :],
            send_sem=back_send.at[picture],
            recv_sem=back_recv.at[picture, slot // BAND_TILES],
            device_id=tile_id(target),
            device_id_type=MESH_ID,
        )

    def passed(view, sem):
        pltpu.make_async_copy(view, view, sem).wait()

    rest = pl.ds(0, CELLS - SHARE)
    loop(1, TILES, lambda i: cot_copy(lax.rem(me + i, TILES), me).start())
    own_cot = pltpu.make_async_copy(cot_hbm.at[:, own, :], got_cot.at[:, own, :], own_sem.at[0])
    own_cot.start()


    def forward_picture(picture):
        rim = rim_of(picture, 0)
        for copy in rim:
            copy.wait_recv()
        clear_outside(me, picture, xgrid, sides_in, corners_in)
        column_stack(picture, sides_in, corners_in, xcols)
        column_terms(picture, xcols, lambda a, c: weight(3 * a + c), terms)

        def do_band(step):
            band = lax.rem(step + tile_row // 2, BANDS)
            cells = times(band, BAND_CELLS)

            def do_block(index):
                strip = band * 2 + index // LANE_BLOCKS
                lanes = times(lax.rem(index, LANE_BLOCKS), LANES)
                rows = xgrid[picture, pl.ds(strip * STRIP, STRIP + 2), :, lanes].astype(F32)
                pre = convolve(
                    rows,
                    [weight(n, lanes) for n in range(9)],
                    terms[0, picture, strip, 0:STRIP, lanes],
                    terms[1, picture, strip, 0:STRIP, lanes],
                )
                square = pre * pre
                tanh = jnp.tanh(pre * (GELU_1 + GELU_3 * square))
                half = 0.5 * pre
                activated = half + half * tanh
                slope = (0.5 + 0.5 * tanh) + half * (1.0 - tanh * tanh) * (GELU_1 + (3.0 * GELU_3) * square)
                here = times(strip, STRIP_CELLS)
                act[picture, here, lanes] = activated.astype(BF16).reshape(STRIP_CELLS, LANES)
                dg[picture, here, lanes] = slope.astype(BF16).reshape(STRIP_CELLS, LANES)

            loop(0, 2 * LANE_BLOCKS, do_block)
            projected = dot(act[picture, cells, :], wproj_ref[...])
            mix[picture, cells, :] = (skip_ref[picture, cells, :].astype(F32) + projected).astype(BF16)

            def send_mix(i):
                mix_copy(picture, band * BAND_TILES + lax.rem(me + i, BAND_TILES), me).start()

            loop(1, BAND_TILES, send_mix)

            @pl.when(band != me // BAND_TILES)
            def _():
                send_mix(0)

        loop(0, BANDS, do_band)

    loop(0, 2, forward_picture)


    gw_ref[...] = jnp.zeros_like(gw_ref)
    go_ref[...] = jnp.zeros_like(go_ref)
    gg_ref[...] = jnp.zeros_like(gg_ref)
    gproj_t[...] = jnp.zeros_like(gproj_t)
    own_cot.wait()
    passed(got_cot.at[:, rest, :], cot_sem.at[1])

    def attend_picture(picture):
        own_mix = pltpu.make_async_copy(mix.at[picture, own, :], got_mix.at[picture, own, :], own_sem.at[1])
        own_mix.start()
        perm = perm_ref[...]
        for b in range(4):
            r = slice(256 * b, 256 * b + 256)
            cot_s[:, 16 * b : 16 * b + 16, :] = dot(perm, got_cot[picture, r, :]).astype(BF16).reshape(16, 16, 256)
        passed(got_mix.at[picture, rest, :], mix_sem.at[1, picture])
        own_mix.wait()
        for b in range(4):
            r = slice(256 * b, 256 * b + 256)
            mix_s[:, 16 * b : 16 * b + 16, :] = dot(perm, got_mix[picture, r, :]).astype(BF16).reshape(16, 16, 256)

        def block(b):
            groups = pl.ds(b * 4, 4)
            out = attend(
                mix_s[groups].reshape(256, 256), cot_s[groups].reshape(256, 256), gain_ref[...],
                wqkv_ref, wout_ref, mask_ref, gw_ref, go_ref, gg_ref,
            )
            cot_s[groups] = out.reshape(4, 64, 256)

        loop(0, 4, block)
        for b in range(4):
            rows = cot_s[:, 16 * b : 16 * b + 16, :].reshape(256, 256)
            back[picture, 256 * b : 256 * b + 256] = dot(perm, rows).astype(BF16)

        def send_back(i):
            target = lax.rem(tile_row + GRID - i // GRID, GRID) * GRID + lax.rem(
                tile_col + GRID - lax.rem(i, GRID), GRID
            )
            back_copy(picture, target, me).start()

        loop(1, TILES, send_back)
        own_back = pltpu.make_async_copy(back.at[picture, own, :], gs.at[picture, own, :], own_sem.at[2])
        own_back.start()
        own_back.wait()

    loop(0, 2, attend_picture)


    def core_copy(half):
        return pltpu.make_async_remote_copy(
            src_ref=part_out.at[half, :, 1 - core],
            dst_ref=core_in.at[half],
            send_sem=core_send.at[half],
            recv_sem=core_recv.at[half],
            device_id=mate,
            device_id_type=MESH_ID,
        )

    def remote(source, target, send, recv, device):
        return pltpu.make_async_remote_copy(
            src_ref=source, dst_ref=target, send_sem=send, recv_sem=recv, device_id=device, device_id_type=MESH_ID
        )

    def y_id(n):
        return {"dp": n // 2, "row": lax.rem(n, 2)}

    def z_id(n):
        return {"col": n * 2 + core}

    def piece(n):
        return times(n // 2, 16), times(lax.rem(n, 2), LANES)

    def y_copy(half, to):
        return remote(y_out.at[half, to], y_in.at[half, q], y_sem.at[half, 0], y_sem.at[half, 1], y_id(to))

    def z_copy(half, to):
        return remote(
            small_out.at[(half, *piece(to))], small_in.at[half, chip], z_sem.at[half, 0], z_sem.at[half, 1], z_id(to)
        )

    def g_copy(half, to):
        here = whole.at[(half, q, core, *piece(chip))]
        return remote(here, here, g_sem.at[half, 0], g_sem.at[half, 1], z_id(to))

    def gy_copy(half, to):
        here = whole.at[half, q, core]
        return remote(here, here, gy_sem.at[half, 0], gy_sem.at[half, 1], y_id(to))

    def mate_copy(half):
        here = whole.at[half, :, core]
        return remote(here, here, core_send.at[2 + half], core_recv.at[2 + half], mate)

    def others(count, mine, action):
        loop(1, count, lambda i: action(lax.rem(mine + i, count)))

    def total_of(ref, count):
        total = ref[0].astype(F32)
        for n in range(1, count):
            total = total + ref[n].astype(F32)
        return total

    def reduce_y(half):
        core_copy(half).wait_recv()
        for n in range(4):
            y_out[half, n] = (part_out[half, n, core].astype(F32) + core_in[half, n].astype(F32)).astype(BF16)
        others(4, q, lambda n: y_copy(half, n).start())

    def reduce_z(half):
        passed(y_in.at[half, pl.ds(0, 3)], y_sem.at[half, 1])
        y_in[half, q] = y_out[half, q]
        small_out[half] = total_of(y_in.at[half], 4).astype(BF16)
        others(16, chip, lambda n: z_copy(half, n).start())

    def gather_z(half):
        passed(small_in.at[half, pl.ds(0, 15)], z_sem.at[half, 1])
        small_in[half, chip] = small_out[(half, *piece(chip))]
        whole[(half, q, core, *piece(chip))] = total_of(small_in.at[half], 16).astype(BF16)
        others(16, chip, lambda n: g_copy(half, n).start())

    def gather_y(half):
        passed(small_in.at[half, pl.ds(0, 15)], g_sem.at[half, 1])
        others(4, q, lambda n: gy_copy(half, n).start())

    def gather_core(half):
        passed(y_in.at[half, pl.ds(0, 3)], gy_sem.at[half, 1])
        mate_copy(half).start()

    def reduction_sent(half):
        core_copy(half).wait_send()
        passed(y_in.at[half, pl.ds(0, 3)], y_sem.at[half, 0])
        passed(small_in.at[half, pl.ds(0, 15)], z_sem.at[half, 0])
        passed(small_in.at[half, pl.ds(0, 15)], g_sem.at[half, 0])
        passed(y_in.at[half, pl.ds(0, 3)], gy_sem.at[half, 0])

    def ey_copy(to):
        return remote(ex_b.at[q], ex_b.at[q], ey_sem.at[0], ey_sem.at[1], y_id(to))

    def ez_copy(to):
        return remote(ex_c.at[chip], ex_c.at[chip], ez_sem.at[0], ez_sem.at[1], z_id(to))

    for n in range(4):
        block = gw_ref[256 * n : 256 * n + 256] if n < 3 else go_ref[...]
        part_out[1, n] = block.astype(BF16).reshape(2, 128, 256)
    core_copy(1).start()


    spot = lax.broadcasted_iota(jnp.int32, (STRIP, COLS, LANES), 1)
    gkern[...] = jnp.zeros_like(gkern)

    def back_picture(picture):
        def do_band(step):
            band = lax.rem(step + tile_row // 2, BANDS)
            cells = times(band, BAND_CELLS)

            @pl.when(band != me // BAND_TILES)
            def _():
                passed(gs.at[picture, pl.ds(0, BAND_CELLS), :], back_recv.at[picture, band])

            @pl.when(band == me // BAND_TILES)
            def _():
                passed(gs.at[picture, pl.ds(0, BAND_CELLS - SHARE), :], back_recv.at[picture, band])

            flat = gs[picture, cells, :]
            flat_t = flat.T
            for n in range(4):
                lanes = slice(256 * n, 256 * n + 256)
                grad_act = dot_t(flat, wproj_ref[lanes, :])
                grad_pre = (grad_act * dg[picture, cells, lanes].astype(F32)).astype(BF16)
                ggrid[picture, pl.ds(1 + band * BAND, BAND), :, lanes] = grad_pre.reshape(BAND, COLS, 256)
                gproj_t[:, lanes] += dot(flat_t, act[picture, cells, lanes])

        loop(0, BANDS, do_band)
        collect_sides(picture, ggrid, gsides_out, gcorners_out)
        for copy in rim_of(picture, 1):
            copy.start()

        @pl.when(picture == 0)
        def _():
            reduce_y(1)

        @pl.when(picture == 1)
        def _():
            for n in range(4):
                part_out[0, n] = gproj_t[:, 256 * n : 256 * n + 256].T.astype(BF16).reshape(2, 128, 256)
            core_copy(0).start()
            reduce_z(1)

        def kernel_block(block):
            lanes = times(block, LANES)

            def one(strip, sums):
                grads = ggrid[picture, pl.ds(1 + strip * STRIP, STRIP), :, lanes].astype(F32)
                rows = xgrid[picture, pl.ds(strip * STRIP, STRIP + 2), :, lanes].astype(F32)
                shifted = (
                    jnp.where(spot == COLS - 1, 0.0, pltpu.roll(grads, COLS - 1, 1)),
                    grads,
                    jnp.where(spot == 0, 0.0, pltpu.roll(grads, 1, 1)),
                )
                new = []
                for row_off in range(3):
                    for col_off in range(3):
                        product = shifted[col_off] * rows[row_off : row_off + STRIP]
                        product = product.reshape(STRIP * 4, 8, LANES).sum(axis=0)
                        new.append(sums[3 * row_off + col_off] + product)
                return tuple(new)

            sums = lax.fori_loop(0, STRIPS, one, tuple(jnp.zeros((8, LANES), F32) for _ in range(9)))
            for n in range(9):
                gkern[n : n + 1, lanes] += jnp.sum(sums[n], axis=0, keepdims=True)

        loop(0, LANE_BLOCKS // 4, kernel_block)

        @pl.when(picture == 1)
        def _():
            reduce_y(0)
            gather_z(1)

        loop(LANE_BLOCKS // 4, LANE_BLOCKS, kernel_block)
        for row_off in range(3):
            for side in range(2):
                n = 3 * row_off + 2 * side
                beside = xcols[side, picture, 7 + row_off : 7 + row_off + ROWS, :]
                gkern[n : n + 1, :] += jnp.sum(
                    gsides_out[side, picture].astype(F32) * beside, axis=0, keepdims=True
                )

    loop(0, 2, back_picture)
    gs_store = pltpu.make_async_copy(gs, gs_hbm, own_sem.at[3])
    gs_store.start()


    extra = [gkern[0:9, 256 * n : 256 * n + 256] for n in range(4)]
    extra = jnp.concatenate(extra + [gg_ref[...], jnp.zeros((11, 256), F32)], axis=0).astype(BF16)
    ex_a[core] = extra
    ex_core = remote(ex_a.at[core], ex_a.at[core], core_send.at[4], core_recv.at[4], mate)
    ex_core.start()

    ex_core.wait_recv()
    ex_b[q] = total_of(ex_a, 2).astype(BF16)
    others(4, q, lambda n: ey_copy(n).start())
    reduce_z(0)
    gather_y(1)

    def store_copy(picture, band):
        cells = times(band, BAND_CELLS)
        return pltpu.make_async_copy(dg.at[picture, cells, :], ge_hbm.at[picture, cells, :], store_sem.at[picture, band])

    def last_start(picture):
        for copy in rim_of(picture, 1):
            copy.wait_recv()
        clear_outside(me, picture, ggrid, gsides_in, gcorners_in)
        column_stack(picture, gsides_in, gcorners_in, gcols)
        column_terms(picture, gcols, lambda a, c: weight(8 - 3 * a - c), terms)

    def last_bands(picture, begin, end):
        def do_band(band):
            def do_block(index):
                strip = band * 2 + index // LANE_BLOCKS
                lanes = times(lax.rem(index, LANE_BLOCKS), LANES)
                rows = ggrid[picture, pl.ds(strip * STRIP, STRIP + 2), :, lanes].astype(F32)
                total = convolve(
                    rows,
                    [weight(8 - n, lanes) for n in range(9)],
                    terms[0, picture, strip, 0:STRIP, lanes],
                    terms[1, picture, strip, 0:STRIP, lanes],
                )
                dg[picture, times(strip, STRIP_CELLS), lanes] = total.astype(BF16).reshape(STRIP_CELLS, LANES)

            loop(0, 2 * LANE_BLOCKS, do_block)
            store_copy(picture, band).start()

        loop(begin, end, do_band)

    last_start(0)
    last_bands(0, 0, 3)
    passed(ex_b.at[pl.ds(0, 3)], ey_sem.at[1])
    ex_c[chip] = total_of(ex_b, 4).astype(BF16)
    others(16, chip, lambda n: ez_copy(n).start())
    gather_z(0)
    last_bands(0, 3, 4)
    gather_core(1)
    last_start(1)
    last_bands(1, 0, 2)
    gather_y(0)
    last_bands(1, 2, 4)
    passed(ex_c.at[pl.ds(0, 15)], ez_sem.at[1])
    extra_out[...] = total_of(ex_c, 16)


    passed(got_cot.at[:, rest, :], cot_sem.at[0])
    for picture in range(2):
        passed(mix.at[picture, rest, :], mix_sem.at[0, picture])
        passed(back.at[picture, rest, :], back_send.at[picture])
    for turn in range(2):
        for picture in range(2):
            for copy in rim_of(picture, turn):
                copy.wait_send()
    ex_core.wait_send()
    passed(ex_b.at[pl.ds(0, 3)], ey_sem.at[0])
    passed(ex_c.at[pl.ds(0, 15)], ez_sem.at[0])
    gs_store.wait()
    for picture in range(2):
        for band in range(BANDS):
            store_copy(picture, band).wait()
    mate_copy(1).wait_recv()
    stores = [pltpu.make_async_copy(whole.at[half], whole_hbm.at[half], own_sem.at[4 + half]) for half in range(2)]
    stores[1].start()
    gather_core(0)
    for half in range(2):
        reduction_sent(half)
    mate_copy(0).wait_recv()
    stores[0].start()
    mate_copy(0).wait_send()
    mate_copy(1).wait_send()
    for copy in stores:
        copy.wait()


def my_tile():
    return lax.axis_index("row") * 32 + lax.axis_index("col")


def constants():
    perm = np.zeros((256, 256), np.float32)
    for a in range(16):
        for b in range(16):
            perm[a * 16 + b, b * 16 + a] = 1
    mask = np.kron(np.eye(8), np.ones((64, 32))).astype(np.float32)
    return jnp.asarray(perm, BF16), jnp.asarray(mask, BF16)


def whole_call(x, skip, cot, kern, wproj, gain, wqkv, wout):
    vmem = pl.BlockSpec(memory_space=pltpu.VMEM)
    anywhere = pl.BlockSpec(memory_space=pl.ANY)
    dma = pltpu.SemaphoreType.DMA

    def bf(*shape):
        return pltpu.VMEM(shape, BF16)

    def fl(*shape):
        return pltpu.VMEM(shape, F32)

    rims = [bf(2, 2, ROWS, EXPAND), bf(2, 2, ROWS, EXPAND), bf(2, 4, 16, EXPAND), bf(2, 4, 16, EXPAND)]
    return pl.pallas_call(
        whole_kernel,
        out_shape=(
            jax.ShapeDtypeStruct((2, CELLS, EXPAND), BF16),
            jax.ShapeDtypeStruct((2, CELLS, WIDTH), BF16),
            jax.ShapeDtypeStruct((2, 4, 2, 128, 256), BF16),
            jax.ShapeDtypeStruct((48, 256), F32),
        ),
        in_specs=[anywhere, vmem, anywhere] + [vmem] * 7,
        out_specs=(anywhere, anywhere, anywhere, vmem),
        scratch_shapes=[
            bf(2, ROWS + 2, COLS, EXPAND), bf(2, ROWS + 2, COLS, EXPAND), bf(2, CELLS, EXPAND), bf(2, CELLS, EXPAND),
            bf(2, CELLS, WIDTH), bf(2, CELLS, WIDTH), bf(2, CELLS, WIDTH), bf(16, 64, WIDTH), bf(16, 64, WIDTH),
            bf(2, CELLS, WIDTH), bf(2, CELLS, WIDTH),
        ]
        + rims
        + [fl(2, 2, 48, EXPAND), fl(2, 2, 48, EXPAND), fl(2, 2, STRIPS, 8, EXPAND)]
        + rims
        + [
            fl(WIDTH, EXPAND), fl(16, EXPAND), fl(3 * WIDTH, WIDTH), fl(WIDTH, WIDTH), fl(1, WIDTH),
            bf(2, 4, 2, 128, 256), bf(2, 4, 128, 256), bf(2, 4, 128, 256), bf(2, 4, 128, 256),
            bf(2, 128, 256), bf(2, 16, 16, LANES), bf(2, 4, 2, 128, 256),
            bf(2, 48, 256), bf(4, 48, 256), bf(16, 48, 256),
            dma((2,)), dma((2, 2, 8)), dma((2, 2, 8)), dma((2,)), dma((2, 2)), dma((2,)), dma((2, BANDS)),
            dma((6,)), dma((2, BANDS)),
            dma((5,)), dma((5,)), dma((2, 2)), dma((2, 2)), dma((2, 2)), dma((2, 2)), dma((2,)), dma((2,)),
        ],
        compiler_params=pltpu.CompilerParams(
            collective_id=0, has_side_effects=True, vmem_limit_bytes=56 * 2**20
        ),
        name="whole",
    )(x, skip, cot, kern, wproj, gain, wqkv, wout, *constants())


def finish_kernel(
    ge_hbm, gs_hbm, whole_ref, extra_ref, ge_out, gs_out, gkern_out, gproj_out, gwqkv_out, gout_out, ggain_out, sems, *, scale
):
    copies = []
    for picture in range(2):
        for part in range(2):
            rows = pl.ds(512 * part, 512)
            copies.append(
                pltpu.make_async_copy(
                    ge_hbm.at[picture, rows], ge_out.at[picture, rows], sems.at[2 * picture + part]
                )
            )
    copies.append(pltpu.make_async_copy(gs_hbm, gs_out, sems.at[4]))
    for copy in copies:
        copy.start()
    for n in range(8):
        block = whole_ref[n // 4, n % 4].reshape(256, 256).astype(F32) * scale
        if n < 4:
            gproj_out[256 * n : 256 * n + 256, :] = block
            some = extra_ref[9 * n : 9 * n + 9, :] * scale
            for row in range(3):
                gkern_out[row, :, 256 * n : 256 * n + 256] = some[3 * row : 3 * row + 3]
        elif n < 7:
            gwqkv_out[:, 256 * (n - 4) : 256 * (n - 4) + 256] = block
        else:
            gout_out[...] = block
    ggain_out[...] = extra_ref[36:37, :] * scale
    for copy in copies:
        copy.wait()


def finish(ge, gs, whole, extra, scale):
    vmem = pl.BlockSpec(memory_space=pltpu.VMEM)
    anywhere = pl.BlockSpec(memory_space=pl.ANY)

    def kernel(*refs):
        finish_kernel(*refs, scale=scale)

    return pl.pallas_call(
        kernel,
        out_shape=(
            jax.ShapeDtypeStruct((2, CELLS, EXPAND), BF16),
            jax.ShapeDtypeStruct((2, CELLS, WIDTH), BF16),
            jax.ShapeDtypeStruct((3, 3, EXPAND), F32),
            jax.ShapeDtypeStruct((EXPAND, WIDTH), F32),
            jax.ShapeDtypeStruct((WIDTH, 3 * WIDTH), F32),
            jax.ShapeDtypeStruct((WIDTH, WIDTH), F32),
            jax.ShapeDtypeStruct((1, WIDTH), F32),
        ),
        in_specs=[anywhere, anywhere, vmem, vmem],
        out_specs=(anywhere,) * 2 + (vmem,) * 5,
        scratch_shapes=[pltpu.SemaphoreType.DMA((5,))],
        compiler_params=pltpu.CompilerParams(vmem_limit_bytes=60 * 2**20),
        name="finish",
    )(ge, gs, whole, extra)


def on_device(expanded, skip, cotangent, depth_kernel, w_proj, norm_gain, w_qkv, w_out):
    ge, gs, whole, extra = whole_call(
        expanded[:, 0],
        skip.reshape(2, CELLS, WIDTH),
        cotangent.reshape(2, CELLS, WIDTH),
        depth_kernel,
        w_proj,
        norm_gain.reshape(1, WIDTH),
        w_qkv,
        w_out,
    )
    scale = 1.0 / math.sqrt(2 * lax.axis_size("dp") * TILES * CELLS)
    ge, gs, gkern, gproj, gwqkv, gout, ggain = finish(ge, gs, whole, extra, scale)
    return (
        ge.reshape(2, 1, ROWS, COLS, EXPAND),
        gs.reshape(2, 1, ROWS, COLS, WIDTH),
        gkern,
        gproj,
        gwqkv,
        gout,
        ggain.reshape(WIDTH),
    )


def solution(mesh):
    tiled = P("dp", ("row", "col"), None, None, None)
    return jax.shard_map(
        on_device,
        mesh=mesh,
        in_specs=(tiled, tiled, tiled, P(), P(), P(), P(), P()),
        out_specs=(tiled, tiled, P(), P(), P(), P(), P()),
        check_vma=False,
    )
```

```python
import math

import jax
import jax.numpy as jnp
import numpy as np
from jax import lax
from jax.experimental import pallas as pl
from jax.experimental.pallas import tpu as pltpu
from jax.sharding import PartitionSpec as P

GRID = 8
TILES = 64
ROWS = 32
COLS = 32
CELLS = ROWS * COLS
LANES = 128
WIDTH = 256
EXPAND = 1024
LANE_BLOCKS = EXPAND // LANES
STRIP = 4
STRIPS = ROWS // STRIP
STRIP_CELLS = STRIP * COLS
BAND = 8
BANDS = ROWS // BAND
BAND_CELLS = BAND * COLS
BAND_TILES = TILES // BANDS
GROUPS = 8
SHARE = CELLS // TILES
F32 = jnp.float32
BF16 = jnp.bfloat16
MESH_ID = pl.DeviceIdType.MESH
GELU_1 = math.sqrt(2.0 / math.pi)
GELU_3 = GELU_1 * 0.044715
SIDES = ((0, -1), (0, 1))
ENDS = ((-1, 0), (1, 0))
CORNERS = ((-1, -1), (-1, 1), (1, -1), (1, 1))
AROUND = SIDES + ENDS + CORNERS


def dot(a, b):
    return lax.dot_general(a, b, (((1,), (0,)), ((), ())), preferred_element_type=F32)


def dot_t(a, b):
    return lax.dot_general(a, b, (((1,), (1,)), ((), ())), preferred_element_type=F32)


def dot_tl(a, b):
    return lax.dot_general(a, b, (((0,), (0,)), ((), ())), preferred_element_type=F32)


def tile_id(tile):
    return {"row": tile // 32, "col": lax.rem(tile, 32)}


def times(start, count, size=None):
    return pl.ds(pl.multiple_of(start * count, count), size or count)


def loop(begin, end, body):
    def one(i, carry):
        body(i)
        return carry

    lax.fori_loop(begin, end, one, 0)


def neighbours(me):
    tile_row, tile_col = me // GRID, lax.rem(me, GRID)
    return {
        (down, right): lax.rem(tile_row + down + GRID, GRID) * GRID + lax.rem(tile_col + right + GRID, GRID)
        for down in (-1, 0, 1)
        for right in (-1, 0, 1)
        if (down, right) != (0, 0)
    }


def rim_copies(me, picture, turn, grid_ref, sides_out, sides_in, corners_out, corners_in, send_sem, recv_sem):
    around = neighbours(me)
    copies = []
    for n, (down, right) in enumerate(AROUND):
        if down == 0:
            source = sides_out.at[(right + 1) // 2, picture]
            target = sides_in.at[(1 - right) // 2, picture]
        elif right == 0:
            source = grid_ref.at[picture, 1 if down < 0 else ROWS]
            target = grid_ref.at[picture, ROWS + 1 if down < 0 else 0]
        else:
            place = CORNERS.index((down, right))
            source = corners_out.at[picture, place]
            target = corners_in.at[picture, 3 - place]
        copies.append(
            pltpu.make_async_remote_copy(
                src_ref=source,
                dst_ref=target,
                send_sem=send_sem.at[turn, picture, n],
                recv_sem=recv_sem.at[turn, picture, n],
                device_id=tile_id(around[down, right]),
                device_id_type=MESH_ID,
            )
        )
    return copies


def collect_sides(picture, grid_ref, sides_out, corners_out):
    for side in range(2):
        for start in range(0, ROWS, 16):
            window = grid_ref[picture, 1 + start : 17 + start, 16 * side : 16 * side + 16, :]
            column = window.astype(F32)[:, 15 * side, :]
            sides_out[side, picture, start : start + 16, :] = column.astype(BF16)
    for place, (down, right) in enumerate(CORNERS):
        edge = 0 if down < 0 else 16
        row = 0 if down < 0 else 15
        one = sides_out[(right + 1) // 2, picture, edge : edge + 16, :].astype(F32)[row : row + 1]
        corners_out[picture, place] = jnp.concatenate([one, jnp.zeros((15, EXPAND), F32)], axis=0).astype(BF16)


def clear_outside(me, picture, grid_ref, sides_in, corners_in):
    tile_row, tile_col = me // GRID, lax.rem(me, GRID)
    none = jnp.zeros((16, EXPAND), BF16)
    for side, last in ((0, 0), (1, GRID - 1)):

        @pl.when(tile_col == last)
        def _():
            sides_in[side, picture] = jnp.zeros((ROWS, EXPAND), BF16)
            corners_in[picture, side] = none
            corners_in[picture, 2 + side] = none

    for end, last in ((0, 0), (1, GRID - 1)):

        @pl.when(tile_row == last)
        def _():
            grid_ref[picture, (ROWS + 1) * end] = jnp.zeros((COLS, EXPAND), BF16)
            corners_in[picture, 2 * end] = none
            corners_in[picture, 2 * end + 1] = none


def column_stack(picture, sides_in, corners_in, columns):
    blank = jnp.zeros((7, EXPAND), F32)
    for side in range(2):
        above = corners_in[picture, side].astype(F32)[0:1]
        below = corners_in[picture, 2 + side].astype(F32)[0:1]
        columns[side, picture, 0:8] = jnp.concatenate([blank, above], axis=0)
        columns[side, picture, 8 : 8 + ROWS] = sides_in[side, picture].astype(F32)
        columns[side, picture, 40:48] = jnp.concatenate([below, blank], axis=0)


def column_terms(picture, columns, weights, terms):
    for side in range(2):
        total = None
        for row_off in range(3):
            term = weights(row_off, 2 * side) * columns[side, picture, 7 + row_off : 7 + row_off + ROWS, :]
            total = term if total is None else total + term
        for strip in range(STRIPS):
            terms[side, picture, strip, 0:STRIP] = total[STRIP * strip : STRIP * strip + STRIP]


def convolve(rows, weights, left, right):
    spot = lax.broadcasted_iota(jnp.int32, (STRIP, COLS, LANES), 1)
    parts = []
    for col_off in range(3):
        total = None
        for row_off in range(3):
            term = weights[3 * row_off + col_off][None, :, :] * rows[row_off : row_off + STRIP]
            total = term if total is None else total + term
        parts.append(total)
    from_left = jnp.where(spot == 0, left[:, None, :], pltpu.roll(parts[0], 1, 1))
    from_right = jnp.where(spot == COLS - 1, right[:, None, :], pltpu.roll(parts[2], COLS - 1, 1))
    return parts[1] + from_left + from_right


def pick_heads(full, lane):
    kept = full[0:64]
    for h in range(1, 4):
        kept = jnp.where(lane == h, full[64 * h : 64 * h + 64], kept)
    return kept


def attend(mix, cot, gain, wqkv_ref, wout_ref, mask_ref, gw_ref, go_ref, gg_ref):
    scale = 1.0 / math.sqrt(32.0)
    lane = lax.broadcasted_iota(jnp.int32, (64, 128), 1) // 32
    mix = mix.astype(F32)
    inv = lax.rsqrt(jnp.mean(mix * mix, axis=-1, keepdims=True) + 1e-6)
    mi = mix * inv
    normed = (mi * gain).astype(BF16)
    qkv = dot(normed, wqkv_ref[...]).astype(BF16)
    gatt = dot_t(cot, wout_ref[...]).astype(BF16)
    parts = [(slice(64 * i, 64 * i + 64), 128 * half) for i in range(GROUPS) for half in range(2)]
    q, k, v = ([qkv[r, first + 256 * n : first + 256 * n + 128] for r, first in parts] for n in range(3))
    qexp = [jnp.concatenate([x] * 4, axis=0) * mask_ref[...] for x in q]
    doexp = [jnp.concatenate([gatt[r, first : first + 128]] * 4, axis=0) * mask_ref[...] for r, first in parts]
    st = [dot_t(x, y) * scale for x, y in zip(k, qexp)]
    dp = [dot_t(x, y) for x, y in zip(v, doexp)]
    e = [jnp.exp(x - jnp.max(x, axis=0, keepdims=True)) for x in st]
    p = [x * (1.0 / jnp.sum(x, axis=0, keepdims=True)) for x in e]
    pb = [x.astype(BF16) for x in p]
    ds = [(x * (y - jnp.sum(y * x, axis=0, keepdims=True)) * scale).astype(BF16) for x, y in zip(p, dp)]
    att = [pick_heads(dot_tl(x, y), lane) for x, y in zip(pb, v)]
    gvs = [dot(x, y) for x, y in zip(pb, doexp)]
    gqs = [pick_heads(dot_tl(x, y), lane) for x, y in zip(ds, k)]
    gks = [dot(x, y) for x, y in zip(ds, qexp)]
    att, gqs, gks, gvs = (
        [jnp.concatenate(x[2 * i : 2 * i + 2], axis=1).astype(BF16) for i in range(GROUPS)] for x in (att, gqs, gks, gvs)
    )
    gqkv = [jnp.concatenate(x, axis=0) for x in (gqs, gks, gvs)]
    go_ref[...] += dot_tl(jnp.concatenate(att, axis=0), cot)
    normed_t = normed.T
    gn = jnp.zeros((64 * GROUPS, 256), F32)
    for n in range(3):
        gw_ref[256 * n : 256 * n + 256] += dot(normed_t, gqkv[n])
        gn = gn + dot_t(gqkv[n], wqkv_ref[:, 256 * n : 256 * n + 256])
    gg_ref[...] += jnp.sum(gn * mi, axis=0, keepdims=True)
    scaled = gn * gain
    mean = jnp.mean(scaled * mix, axis=-1, keepdims=True)
    return (cot.astype(F32) + inv * scaled - mi * (inv * inv * mean)).astype(BF16)


def whole_kernel(
    x_hbm, skip_hbm, cot_hbm, kern_ref, wproj_hbm, gain_ref, wqkv_hbm, wout_hbm, perm_hbm, mask_hbm,
    ge_hbm, gs_hbm, whole_hbm, extra_out,
    xgrid, ggrid, act, dg, mix, got_mix, got_cot, mix_s, cot_s, back, gs,
    sides_out, sides_in, corners_out, corners_in, xcols, gcols, terms, gsides_out, gsides_in, gcorners_out, gcorners_in,
    gproj_t, gkern, gw_ref, go_ref, gg_ref, part_out, core_in, y_out, y_in, small_out, small_in, whole,
    ex_a, ex_b, ex_c, skip_ref, wproj_ref, wqkv_ref, wout_ref, perm_ref, mask_ref,
    load_sem, rim_send, rim_recv, cot_sem, mix_sem, back_send, back_recv, own_sem, store_sem,
    core_send, core_recv, y_sem, z_sem, g_sem, gy_sem, ey_sem, ez_sem, operand_sem,
):
    me = my_tile()
    tile_row, tile_col = me // GRID, lax.rem(me, GRID)
    dp, row, col = lax.axis_index("dp"), lax.axis_index("row"), lax.axis_index("col")
    core, chip = lax.rem(col, 2), col // 2
    q = dp * 2 + row
    mate = {"col": col + 1 - 2 * core}
    own = times(me, SHARE)

    def weight(n, lanes=slice(None)):
        return kern_ref[n // 3, n % 3 : n % 3 + 1, lanes]

    loads = [pltpu.make_async_copy(x_hbm.at[p], xgrid.at[p, pl.ds(1, ROWS)], load_sem.at[p]) for p in range(2)]
    operands = [
        pltpu.make_async_copy(a, b, operand_sem.at[n])
        for n, (a, b) in enumerate(
            (
                (skip_hbm, skip_ref), (wproj_hbm, wproj_ref), (wqkv_hbm, wqkv_ref),
                (wout_hbm, wout_ref), (perm_hbm, perm_ref), (mask_hbm, mask_ref),
            )
        )
    ]
    for copy in loads + operands:
        copy.start()
    barrier = pltpu.get_barrier_semaphore()

    def greet(i):
        pl.semaphore_signal(barrier, inc=1, device_id=tile_id(lax.rem(me + i, TILES)), device_id_type=MESH_ID)

    loop(1, TILES, greet)
    for n in range(2):
        pl.semaphore_signal(
            barrier, inc=1, device_id={"dp": 1 - dp, "row": n, "col": col}, device_id_type=MESH_ID
        )
    loads[0].wait()
    collect_sides(0, xgrid, sides_out, corners_out)
    pl.semaphore_wait(barrier, TILES + 1)

    def rim_of(picture, turn):
        if turn == 0:
            refs = (xgrid, sides_out, sides_in, corners_out, corners_in)
        else:
            refs = (ggrid, gsides_out, gsides_in, gcorners_out, gcorners_in)
        return rim_copies(me, picture, turn, *refs, rim_send, rim_recv)

    for copy in rim_of(0, 0):
        copy.start()
    loads[1].wait()
    collect_sides(1, xgrid, sides_out, corners_out)
    for copy in rim_of(1, 0):
        copy.start()

    def cot_copy(target, slot):
        return pltpu.make_async_remote_copy(
            src_ref=cot_hbm.at[:, times(target, SHARE), :],
            dst_ref=got_cot.at[:, times(slot, SHARE), :],
            send_sem=cot_sem.at[0],
            recv_sem=cot_sem.at[1],
            device_id=tile_id(target),
            device_id_type=MESH_ID,
        )

    def mix_copy(picture, target, slot):
        return pltpu.make_async_remote_copy(
            src_ref=mix.at[picture, times(target, SHARE), :],
            dst_ref=got_mix.at[picture, times(slot, SHARE), :],
            send_sem=mix_sem.at[0, picture],
            recv_sem=mix_sem.at[1, picture],
            device_id=tile_id(target),
            device_id_type=MESH_ID,
        )

    def back_copy(picture, target, slot):
        return pltpu.make_async_remote_copy(
            src_ref=back.at[picture, times(target, SHARE), :],
            dst_ref=gs.at[picture, times(slot, SHARE), :],
            send_sem=back_send.at[picture],
            recv_sem=back_recv.at[picture, slot // BAND_TILES],
            device_id=tile_id(target),
            device_id_type=MESH_ID,
        )

    def passed(view, sem):
        pltpu.make_async_copy(view, view, sem).wait()

    rest = pl.ds(0, CELLS - SHARE)
    own_cot = pltpu.make_async_copy(cot_hbm.at[:, own, :], got_cot.at[:, own, :], own_sem.at[0])
    own_cot.start()
    for copy in operands:
        copy.wait()


    def forward_picture(picture):
        rim = rim_of(picture, 0)
        for copy in rim:
            copy.wait_recv()

        @pl.when(picture == 0)
        def _():
            loop(1, TILES, lambda i: cot_copy(lax.rem(me + i, TILES), me).start())

        clear_outside(me, picture, xgrid, sides_in, corners_in)
        column_stack(picture, sides_in, corners_in, xcols)
        column_terms(picture, xcols, lambda a, c: weight(3 * a + c), terms)

        def do_band(step):
            band = lax.rem(step + tile_row // 2, BANDS)
            cells = times(band, BAND_CELLS)

            def do_block(index):
                strip = band * 2 + index // LANE_BLOCKS
                lanes = times(lax.rem(index, LANE_BLOCKS), LANES)
                rows = xgrid[picture, pl.ds(strip * STRIP, STRIP + 2), :, lanes].astype(F32)
                pre = convolve(
                    rows,
                    [weight(n, lanes) for n in range(9)],
                    terms[0, picture, strip, 0:STRIP, lanes],
                    terms[1, picture, strip, 0:STRIP, lanes],
                )
                square = pre * pre
                tanh = jnp.tanh(pre * (GELU_1 + GELU_3 * square))
                half = 0.5 * pre
                activated = half + half * tanh
                slope = (0.5 + 0.5 * tanh) + half * (1.0 - tanh * tanh) * (GELU_1 + (3.0 * GELU_3) * square)
                here = times(strip, STRIP_CELLS)
                act[picture, here, lanes] = activated.astype(BF16).reshape(STRIP_CELLS, LANES)
                dg[picture, here, lanes] = slope.astype(BF16).reshape(STRIP_CELLS, LANES)

            loop(0, 2 * LANE_BLOCKS, do_block)
            projected = dot(act[picture, cells, :], wproj_ref[...])
            mix[picture, cells, :] = (skip_ref[picture, cells, :].astype(F32) + projected).astype(BF16)

            def send_mix(i):
                mix_copy(picture, band * BAND_TILES + lax.rem(me + i, BAND_TILES), me).start()

            loop(1, BAND_TILES, send_mix)

            @pl.when(band != me // BAND_TILES)
            def _():
                send_mix(0)

        loop(0, BANDS, do_band)

    loop(0, 2, forward_picture)


    gw_ref[...] = jnp.zeros_like(gw_ref)
    go_ref[...] = jnp.zeros_like(go_ref)
    gg_ref[...] = jnp.zeros_like(gg_ref)
    gproj_t[...] = jnp.zeros_like(gproj_t)
    own_cot.wait()
    passed(got_cot.at[:, rest, :], cot_sem.at[1])

    def attend_picture(picture):
        own_mix = pltpu.make_async_copy(mix.at[picture, own, :], got_mix.at[picture, own, :], own_sem.at[1])
        own_mix.start()
        perm = perm_ref[...]
        for b in range(4):
            r = slice(256 * b, 256 * b + 256)
            cot_s[:, 16 * b : 16 * b + 16, :] = dot(perm, got_cot[picture, r, :]).astype(BF16).reshape(16, 16, 256)
        passed(got_mix.at[picture, rest, :], mix_sem.at[1, picture])
        own_mix.wait()
        for b in range(4):
            r = slice(256 * b, 256 * b + 256)
            mix_s[:, 16 * b : 16 * b + 16, :] = dot(perm, got_mix[picture, r, :]).astype(BF16).reshape(16, 16, 256)

        def block(b):
            groups = pl.ds(b * GROUPS, GROUPS)
            out = attend(
                mix_s[groups].reshape(64 * GROUPS, 256), cot_s[groups].reshape(64 * GROUPS, 256), gain_ref[...],
                wqkv_ref, wout_ref, mask_ref, gw_ref, go_ref, gg_ref,
            )
            cot_s[groups] = out.reshape(GROUPS, 64, 256)

        loop(0, 16 // GROUPS, block)
        for b in range(4):
            rows = cot_s[:, 16 * b : 16 * b + 16, :].reshape(256, 256)
            back[picture, 256 * b : 256 * b + 256] = dot(perm, rows).astype(BF16)

        def send_back(i):
            target = lax.rem(tile_row + GRID - i // GRID, GRID) * GRID + lax.rem(
                tile_col + GRID - lax.rem(i, GRID), GRID
            )
            back_copy(picture, target, me).start()

        loop(1, TILES, send_back)
        own_back = pltpu.make_async_copy(back.at[picture, own, :], gs.at[picture, own, :], own_sem.at[2])
        own_back.start()
        own_back.wait()

    loop(0, 2, attend_picture)


    def core_copy(half):
        return pltpu.make_async_remote_copy(
            src_ref=part_out.at[half, :, 1 - core],
            dst_ref=core_in.at[half],
            send_sem=core_send.at[half],
            recv_sem=core_recv.at[half],
            device_id=mate,
            device_id_type=MESH_ID,
        )

    def remote(source, target, send, recv, device):
        return pltpu.make_async_remote_copy(
            src_ref=source, dst_ref=target, send_sem=send, recv_sem=recv, device_id=device, device_id_type=MESH_ID
        )

    def y_id(n):
        return {"dp": n // 2, "row": lax.rem(n, 2)}

    def z_id(n):
        return {"col": n * 2 + core}

    def piece(n):
        return times(n // 2, 16), times(lax.rem(n, 2), LANES)

    def y_copy(half, to):
        return remote(y_out.at[half, to], y_in.at[half, q], y_sem.at[half, 0], y_sem.at[half, 1], y_id(to))

    def z_copy(half, to):
        return remote(
            small_out.at[(half, *piece(to))], small_in.at[half, chip], z_sem.at[half, 0], z_sem.at[half, 1], z_id(to)
        )

    def g_copy(half, to):
        here = whole.at[(half, q, core, *piece(chip))]
        return remote(here, here, g_sem.at[half, 0], g_sem.at[half, 1], z_id(to))

    def gy_copy(half, to):
        here = whole.at[half, q, core]
        return remote(here, here, gy_sem.at[half, 0], gy_sem.at[half, 1], y_id(to))

    def mate_copy(half):
        here = whole.at[half, :, core]
        return remote(here, here, core_send.at[2 + half], core_recv.at[2 + half], mate)

    def others(count, mine, action):
        loop(1, count, lambda i: action(lax.rem(mine + i, count)))

    def total_of(ref, count):
        total = ref[0].astype(F32)
        for n in range(1, count):
            total = total + ref[n].astype(F32)
        return total

    def reduce_y(half):
        core_copy(half).wait_recv()
        for n in range(4):
            y_out[half, n] = (part_out[half, n, core].astype(F32) + core_in[half, n].astype(F32)).astype(BF16)
        others(4, q, lambda n: y_copy(half, n).start())

    def reduce_z(half):
        passed(y_in.at[half, pl.ds(0, 3)], y_sem.at[half, 1])
        y_in[half, q] = y_out[half, q]
        small_out[half] = total_of(y_in.at[half], 4).astype(BF16)
        others(16, chip, lambda n: z_copy(half, n).start())

    def gather_z(half):
        passed(small_in.at[half, pl.ds(0, 15)], z_sem.at[half, 1])
        small_in[half, chip] = small_out[(half, *piece(chip))]
        whole[(half, q, core, *piece(chip))] = total_of(small_in.at[half], 16).astype(BF16)
        others(16, chip, lambda n: g_copy(half, n).start())

    def gather_y(half):
        passed(small_in.at[half, pl.ds(0, 15)], g_sem.at[half, 1])
        others(4, q, lambda n: gy_copy(half, n).start())

    def gather_core(half):
        passed(y_in.at[half, pl.ds(0, 3)], gy_sem.at[half, 1])
        mate_copy(half).start()

    def reduction_sent(half):
        core_copy(half).wait_send()
        passed(y_in.at[half, pl.ds(0, 3)], y_sem.at[half, 0])
        passed(small_in.at[half, pl.ds(0, 15)], z_sem.at[half, 0])
        passed(small_in.at[half, pl.ds(0, 15)], g_sem.at[half, 0])
        passed(y_in.at[half, pl.ds(0, 3)], gy_sem.at[half, 0])

    def ey_copy(to):
        return remote(ex_b.at[q], ex_b.at[q], ey_sem.at[0], ey_sem.at[1], y_id(to))

    def ez_copy(to):
        return remote(ex_c.at[chip], ex_c.at[chip], ez_sem.at[0], ez_sem.at[1], z_id(to))

    for n in range(4):
        block = gw_ref[256 * n : 256 * n + 256] if n < 3 else go_ref[...]
        part_out[1, n] = block.astype(BF16).reshape(2, 128, 256)
    core_copy(1).start()


    spot = lax.broadcasted_iota(jnp.int32, (STRIP, COLS, LANES), 1)
    gkern[...] = jnp.zeros_like(gkern)

    def back_picture(picture):
        def do_band(step):
            band = lax.rem(step + tile_row // 2, BANDS)
            cells = times(band, BAND_CELLS)

            @pl.when(band != me // BAND_TILES)
            def _():
                passed(gs.at[picture, pl.ds(0, BAND_CELLS), :], back_recv.at[picture, band])

            @pl.when(band == me // BAND_TILES)
            def _():
                passed(gs.at[picture, pl.ds(0, BAND_CELLS - SHARE), :], back_recv.at[picture, band])

            flat = gs[picture, cells, :]
            flat_t = flat.T
            for n in range(4):
                lanes = slice(256 * n, 256 * n + 256)
                grad_act = dot_t(flat, wproj_ref[lanes, :])
                grad_pre = (grad_act * dg[picture, cells, lanes].astype(F32)).astype(BF16)
                ggrid[picture, pl.ds(1 + band * BAND, BAND), :, lanes] = grad_pre.reshape(BAND, COLS, 256)
                gproj_t[:, lanes] += dot(flat_t, act[picture, cells, lanes])

        loop(0, BANDS, do_band)
        collect_sides(picture, ggrid, gsides_out, gcorners_out)
        for copy in rim_of(picture, 1):
            copy.start()

        @pl.when(picture == 0)
        def _():
            reduce_y(1)

        @pl.when(picture == 1)
        def _():
            for n in range(4):
                part_out[0, n] = gproj_t[:, 256 * n : 256 * n + 256].T.astype(BF16).reshape(2, 128, 256)
            core_copy(0).start()
            reduce_z(1)

        def kernel_block(block):
            lanes = times(block, LANES)

            def one(strip, sums):
                grads = ggrid[picture, pl.ds(1 + strip * STRIP, STRIP), :, lanes].astype(F32)
                rows = xgrid[picture, pl.ds(strip * STRIP, STRIP + 2), :, lanes].astype(F32)
                shifted = (
                    jnp.where(spot == COLS - 1, 0.0, pltpu.roll(grads, COLS - 1, 1)),
                    grads,
                    jnp.where(spot == 0, 0.0, pltpu.roll(grads, 1, 1)),
                )
                new = []
                for row_off in range(3):
                    for col_off in range(3):
                        product = shifted[col_off] * rows[row_off : row_off + STRIP]
                        product = product.reshape(STRIP * 4, 8, LANES).sum(axis=0)
                        new.append(sums[3 * row_off + col_off] + product)
                return tuple(new)

            sums = lax.fori_loop(0, STRIPS, one, tuple(jnp.zeros((8, LANES), F32) for _ in range(9)))
            for n in range(9):
                gkern[n : n + 1, lanes] += jnp.sum(sums[n], axis=0, keepdims=True)

        loop(0, LANE_BLOCKS // 4, kernel_block)

        @pl.when(picture == 1)
        def _():
            reduce_y(0)
            gather_z(1)

        loop(LANE_BLOCKS // 4, LANE_BLOCKS, kernel_block)
        for row_off in range(3):
            for side in range(2):
                n = 3 * row_off + 2 * side
                beside = xcols[side, picture, 7 + row_off : 7 + row_off + ROWS, :]
                gkern[n : n + 1, :] += jnp.sum(
                    gsides_out[side, picture].astype(F32) * beside, axis=0, keepdims=True
                )

    loop(0, 2, back_picture)
    gs_store = pltpu.make_async_copy(gs, gs_hbm, own_sem.at[3])
    gs_store.start()


    extra = [gkern[0:9, 256 * n : 256 * n + 256] for n in range(4)]
    extra = jnp.concatenate(extra + [gg_ref[...], jnp.zeros((11, 256), F32)], axis=0).astype(BF16)
    ex_a[core] = extra
    ex_core = remote(ex_a.at[core], ex_a.at[core], core_send.at[4], core_recv.at[4], mate)
    ex_core.start()

    ex_core.wait_recv()
    ex_b[q] = total_of(ex_a, 2).astype(BF16)
    others(4, q, lambda n: ey_copy(n).start())
    reduce_z(0)
    gather_y(1)

    def store_copy(picture, band):
        cells = times(band, BAND_CELLS)
        return pltpu.make_async_copy(dg.at[picture, cells, :], ge_hbm.at[picture, cells, :], store_sem.at[picture, band])

    def last_start(picture):
        for copy in rim_of(picture, 1):
            copy.wait_recv()
        clear_outside(me, picture, ggrid, gsides_in, gcorners_in)
        column_stack(picture, gsides_in, gcorners_in, gcols)
        column_terms(picture, gcols, lambda a, c: weight(8 - 3 * a - c), terms)

    def last_bands(picture, begin, end):
        def do_band(band):
            def do_block(index):
                strip = band * 2 + index // LANE_BLOCKS
                lanes = times(lax.rem(index, LANE_BLOCKS), LANES)
                rows = ggrid[picture, pl.ds(strip * STRIP, STRIP + 2), :, lanes].astype(F32)
                total = convolve(
                    rows,
                    [weight(8 - n, lanes) for n in range(9)],
                    terms[0, picture, strip, 0:STRIP, lanes],
                    terms[1, picture, strip, 0:STRIP, lanes],
                )
                dg[picture, times(strip, STRIP_CELLS), lanes] = total.astype(BF16).reshape(STRIP_CELLS, LANES)

            loop(0, 2 * LANE_BLOCKS, do_block)
            store_copy(picture, band).start()

        loop(begin, end, do_band)

    last_start(0)
    last_bands(0, 0, 3)
    passed(ex_b.at[pl.ds(0, 3)], ey_sem.at[1])
    ex_c[chip] = total_of(ex_b, 4).astype(BF16)
    others(16, chip, lambda n: ez_copy(n).start())
    gather_z(0)
    last_bands(0, 3, 4)
    gather_core(1)
    last_start(1)
    last_bands(1, 0, 2)
    gather_y(0)
    last_bands(1, 2, 4)
    passed(ex_c.at[pl.ds(0, 15)], ez_sem.at[1])
    extra_out[...] = total_of(ex_c, 16)


    passed(got_cot.at[:, rest, :], cot_sem.at[0])
    for picture in range(2):
        passed(mix.at[picture, rest, :], mix_sem.at[0, picture])
        passed(back.at[picture, rest, :], back_send.at[picture])
    for turn in range(2):
        for picture in range(2):
            for copy in rim_of(picture, turn):
                copy.wait_send()
    ex_core.wait_send()
    passed(ex_b.at[pl.ds(0, 3)], ey_sem.at[0])
    passed(ex_c.at[pl.ds(0, 15)], ez_sem.at[0])
    gs_store.wait()
    for picture in range(2):
        for band in range(BANDS):
            store_copy(picture, band).wait()
    mate_copy(1).wait_recv()
    stores = [pltpu.make_async_copy(whole.at[half], whole_hbm.at[half], own_sem.at[4 + half]) for half in range(2)]
    stores[1].start()
    gather_core(0)
    for half in range(2):
        reduction_sent(half)
    mate_copy(0).wait_recv()
    stores[0].start()
    mate_copy(0).wait_send()
    mate_copy(1).wait_send()
    for copy in stores:
        copy.wait()


def my_tile():
    return lax.axis_index("row") * 32 + lax.axis_index("col")


def constants():
    perm = np.zeros((256, 256), np.float32)
    for a in range(16):
        for b in range(16):
            perm[a * 16 + b, b * 16 + a] = 1
    mask = np.kron(np.eye(4), np.ones((64, 32))).astype(np.float32)
    return jnp.asarray(perm, BF16), jnp.asarray(mask, BF16)


def whole_call(x, skip, cot, kern, wproj, gain, wqkv, wout):
    vmem = pl.BlockSpec(memory_space=pltpu.VMEM)
    anywhere = pl.BlockSpec(memory_space=pl.ANY)
    dma = pltpu.SemaphoreType.DMA

    def bf(*shape):
        return pltpu.VMEM(shape, BF16)

    def fl(*shape):
        return pltpu.VMEM(shape, F32)

    rims = [bf(2, 2, ROWS, EXPAND), bf(2, 2, ROWS, EXPAND), bf(2, 4, 16, EXPAND), bf(2, 4, 16, EXPAND)]
    return pl.pallas_call(
        whole_kernel,
        out_shape=(
            jax.ShapeDtypeStruct((2, CELLS, EXPAND), BF16),
            jax.ShapeDtypeStruct((2, CELLS, WIDTH), BF16),
            jax.ShapeDtypeStruct((2, 4, 2, 128, 256), BF16),
            jax.ShapeDtypeStruct((48, 256), F32),
        ),
        in_specs=[anywhere] * 3 + [vmem, anywhere, vmem] + [anywhere] * 4,
        out_specs=(anywhere, anywhere, anywhere, vmem),
        scratch_shapes=[
            bf(2, ROWS + 2, COLS, EXPAND), bf(2, ROWS + 2, COLS, EXPAND), bf(2, CELLS, EXPAND), bf(2, CELLS, EXPAND),
            bf(2, CELLS, WIDTH), bf(2, CELLS, WIDTH), bf(2, CELLS, WIDTH), bf(16, 64, WIDTH), bf(16, 64, WIDTH),
            bf(2, CELLS, WIDTH), bf(2, CELLS, WIDTH),
        ]
        + rims
        + [fl(2, 2, 48, EXPAND), fl(2, 2, 48, EXPAND), fl(2, 2, STRIPS, 8, EXPAND)]
        + rims
        + [
            fl(WIDTH, EXPAND), fl(16, EXPAND), fl(3 * WIDTH, WIDTH), fl(WIDTH, WIDTH), fl(1, WIDTH),
            bf(2, 4, 2, 128, 256), bf(2, 4, 128, 256), bf(2, 4, 128, 256), bf(2, 4, 128, 256),
            bf(2, 128, 256), bf(2, 16, 16, LANES), bf(2, 4, 2, 128, 256),
            bf(2, 48, 256), bf(4, 48, 256), bf(16, 48, 256),
            bf(2, CELLS, WIDTH), bf(EXPAND, WIDTH), bf(WIDTH, 3 * WIDTH), bf(WIDTH, WIDTH), bf(256, 256), bf(256, LANES),
            dma((2,)), dma((2, 2, 8)), dma((2, 2, 8)), dma((2,)), dma((2, 2)), dma((2,)), dma((2, BANDS)),
            dma((6,)), dma((2, BANDS)),
            dma((5,)), dma((5,)), dma((2, 2)), dma((2, 2)), dma((2, 2)), dma((2, 2)), dma((2,)), dma((2,)), dma((6,)),
        ],
        compiler_params=pltpu.CompilerParams(
            collective_id=0, has_side_effects=True, vmem_limit_bytes=56 * 2**20
        ),
        name="whole",
    )(x, skip, cot, kern, wproj, gain, wqkv, wout, *constants())


def finish_kernel(
    ge_hbm, gs_hbm, whole_hbm, extra_ref, ge_out, gs_out, gkern_out, gproj_out, gwqkv_out, gout_out, ggain_out,
    ge_held, gs_held, whole_ref, gproj, gwqkv, gout, sems, *, scale
):
    ways = [(whole_hbm, whole_ref, None)]
    for picture in range(2):
        for part in range(4):
            here = (picture, pl.ds(256 * part, 256))
            ways.append((ge_hbm.at[here], ge_held.at[here], ge_out.at[here]))
    ways.append((gs_hbm, gs_held, gs_out))
    inward = [pltpu.make_async_copy(a, b, sems.at[0, n]) for n, (a, b, _) in enumerate(ways)]
    outward = [pltpu.make_async_copy(b, c, sems.at[1, n]) for n, (_, b, c) in enumerate(ways) if n]
    results = [
        pltpu.make_async_copy(a, b, sems.at[1, len(ways) + n])
        for n, (a, b) in enumerate(((gproj, gproj_out), (gwqkv, gwqkv_out), (gout, gout_out)))
    ]
    for copy in inward:
        copy.start()
    for first, second in zip(inward[1:5], outward[:4]):
        first.wait()
        second.start()
    inward[0].wait()
    for n in range(8):
        block = whole_ref[n // 4, n % 4].reshape(256, 256).astype(F32) * scale
        if n < 4:
            gproj[256 * n : 256 * n + 256, :] = block
            some = extra_ref[9 * n : 9 * n + 9, :] * scale
            for row in range(3):
                gkern_out[row, :, 256 * n : 256 * n + 256] = some[3 * row : 3 * row + 3]
        elif n < 7:
            gwqkv[:, 256 * (n - 4) : 256 * (n - 4) + 256] = block
        else:
            gout[...] = block
    ggain_out[...] = extra_ref[36:37, :] * scale
    for copy in results:
        copy.start()
    for first, second in zip(inward[5:], outward[4:]):
        first.wait()
        second.start()
    for copy in outward + results:
        copy.wait()


def finish(ge, gs, whole, extra, scale):
    vmem = pl.BlockSpec(memory_space=pltpu.VMEM)
    anywhere = pl.BlockSpec(memory_space=pl.ANY)

    def kernel(*refs):
        finish_kernel(*refs, scale=scale)

    return pl.pallas_call(
        kernel,
        out_shape=(
            jax.ShapeDtypeStruct((2, CELLS, EXPAND), BF16),
            jax.ShapeDtypeStruct((2, CELLS, WIDTH), BF16),
            jax.ShapeDtypeStruct((3, 3, EXPAND), F32),
            jax.ShapeDtypeStruct((EXPAND, WIDTH), F32),
            jax.ShapeDtypeStruct((WIDTH, 3 * WIDTH), F32),
            jax.ShapeDtypeStruct((WIDTH, WIDTH), F32),
            jax.ShapeDtypeStruct((1, WIDTH), F32),
        ),
        in_specs=[anywhere, anywhere, anywhere, vmem],
        out_specs=(anywhere, anywhere, vmem, anywhere, anywhere, anywhere, vmem),
        scratch_shapes=[
            pltpu.VMEM((2, CELLS, EXPAND), BF16),
            pltpu.VMEM((2, CELLS, WIDTH), BF16),
            pltpu.VMEM((2, 4, 2, 128, 256), BF16),
            pltpu.VMEM((EXPAND, WIDTH), F32),
            pltpu.VMEM((WIDTH, 3 * WIDTH), F32),
            pltpu.VMEM((WIDTH, WIDTH), F32),
            pltpu.SemaphoreType.DMA((2, 13)),
        ],
        compiler_params=pltpu.CompilerParams(vmem_limit_bytes=60 * 2**20),
        name="finish",
    )(ge, gs, whole, extra)


def on_device(expanded, skip, cotangent, depth_kernel, w_proj, norm_gain, w_qkv, w_out):
    ge, gs, whole, extra = whole_call(
        expanded[:, 0],
        skip.reshape(2, CELLS, WIDTH),
        cotangent.reshape(2, CELLS, WIDTH),
        depth_kernel,
        w_proj,
        norm_gain.reshape(1, WIDTH),
        w_qkv,
        w_out,
    )
    scale = 1.0 / math.sqrt(2 * lax.axis_size("dp") * TILES * CELLS)
    ge, gs, gkern, gproj, gwqkv, gout, ggain = finish(ge, gs, whole, extra, scale)
    return (
        ge.reshape(2, 1, ROWS, COLS, EXPAND),
        gs.reshape(2, 1, ROWS, COLS, WIDTH),
        gkern,
        gproj,
        gwqkv,
        gout,
        ggain.reshape(WIDTH),
    )


def solution(mesh):
    tiled = P("dp", ("row", "col"), None, None, None)
    return jax.shard_map(
        on_device,
        mesh=mesh,
        in_specs=(tiled, tiled, tiled, P(), P(), P(), P(), P()),
        out_specs=(tiled, tiled, P(), P(), P(), P(), P()),
        check_vma=False,
    )
```

```python
import math

import jax
import jax.numpy as jnp
import numpy as np
from jax import lax
from jax.experimental import pallas as pl
from jax.experimental.pallas import tpu as pltpu
from jax.sharding import PartitionSpec as P

GRID = 8
TILES = 64
ROWS = 32
COLS = 32
CELLS = ROWS * COLS
LANES = 128
WIDTH = 256
EXPAND = 1024
LANE_BLOCKS = EXPAND // LANES
STRIP = 4
STRIPS = ROWS // STRIP
STRIP_CELLS = STRIP * COLS
BAND = 8
BANDS = ROWS // BAND
BAND_CELLS = BAND * COLS
BAND_TILES = TILES // BANDS
GROUPS = 8
SHARE = CELLS // TILES
F32 = jnp.float32
BF16 = jnp.bfloat16
MESH_ID = pl.DeviceIdType.MESH
GELU_1 = math.sqrt(2.0 / math.pi)
GELU_3 = GELU_1 * 0.044715
SIDES = ((0, -1), (0, 1))
ENDS = ((-1, 0), (1, 0))
CORNERS = ((-1, -1), (-1, 1), (1, -1), (1, 1))
AROUND = SIDES + ENDS + CORNERS


def dot(a, b):
    return lax.dot_general(a, b, (((1,), (0,)), ((), ())), preferred_element_type=F32)


def dot_t(a, b):
    return lax.dot_general(a, b, (((1,), (1,)), ((), ())), preferred_element_type=F32)


def dot_tl(a, b):
    return lax.dot_general(a, b, (((0,), (0,)), ((), ())), preferred_element_type=F32)


def tile_id(tile):
    return {"row": tile // 32, "col": lax.rem(tile, 32)}


def times(start, count, size=None):
    return pl.ds(pl.multiple_of(start * count, count), size or count)


def loop(begin, end, body):
    def one(i, carry):
        body(i)
        return carry

    lax.fori_loop(begin, end, one, 0)


def neighbours(me):
    tile_row, tile_col = me // GRID, lax.rem(me, GRID)
    return {
        (down, right): lax.rem(tile_row + down + GRID, GRID) * GRID + lax.rem(tile_col + right + GRID, GRID)
        for down in (-1, 0, 1)
        for right in (-1, 0, 1)
        if (down, right) != (0, 0)
    }


def rim_copies(me, picture, turn, grid_ref, sides_out, sides_in, corners_out, corners_in, send_sem, recv_sem):
    around = neighbours(me)
    copies = []
    for n, (down, right) in enumerate(AROUND):
        if down == 0:
            source = sides_out.at[(right + 1) // 2, picture]
            target = sides_in.at[(1 - right) // 2, picture]
        elif right == 0:
            source = grid_ref.at[picture, 1 if down < 0 else ROWS]
            target = grid_ref.at[picture, ROWS + 1 if down < 0 else 0]
        else:
            place = CORNERS.index((down, right))
            source = corners_out.at[picture, place]
            target = corners_in.at[picture, 3 - place]
        copies.append(
            pltpu.make_async_remote_copy(
                src_ref=source,
                dst_ref=target,
                send_sem=send_sem.at[turn, picture, n],
                recv_sem=recv_sem.at[turn, picture, n],
                device_id=tile_id(around[down, right]),
                device_id_type=MESH_ID,
            )
        )
    return copies


def collect_sides(picture, grid_ref, sides_out, corners_out):
    for side in range(2):
        for start in range(0, ROWS, 16):
            window = grid_ref[picture, 1 + start : 17 + start, 16 * side : 16 * side + 16, :]
            column = window.astype(F32)[:, 15 * side, :]
            sides_out[side, picture, start : start + 16, :] = column.astype(BF16)
    for place, (down, right) in enumerate(CORNERS):
        edge = 0 if down < 0 else 16
        row = 0 if down < 0 else 15
        one = sides_out[(right + 1) // 2, picture, edge : edge + 16, :].astype(F32)[row : row + 1]
        corners_out[picture, place] = jnp.concatenate([one, jnp.zeros((15, EXPAND), F32)], axis=0).astype(BF16)


def clear_outside(me, picture, grid_ref, sides_in, corners_in):
    tile_row, tile_col = me // GRID, lax.rem(me, GRID)
    none = jnp.zeros((16, EXPAND), BF16)
    for side, last in ((0, 0), (1, GRID - 1)):

        @pl.when(tile_col == last)
        def _():
            sides_in[side, picture] = jnp.zeros((ROWS, EXPAND), BF16)
            corners_in[picture, side] = none
            corners_in[picture, 2 + side] = none

    for end, last in ((0, 0), (1, GRID - 1)):

        @pl.when(tile_row == last)
        def _():
            grid_ref[picture, (ROWS + 1) * end] = jnp.zeros((COLS, EXPAND), BF16)
            corners_in[picture, 2 * end] = none
            corners_in[picture, 2 * end + 1] = none


def column_stack(picture, sides_in, corners_in, columns):
    blank = jnp.zeros((7, EXPAND), F32)
    for side in range(2):
        above = corners_in[picture, side].astype(F32)[0:1]
        below = corners_in[picture, 2 + side].astype(F32)[0:1]
        columns[side, picture, 0:8] = jnp.concatenate([blank, above], axis=0)
        columns[side, picture, 8 : 8 + ROWS] = sides_in[side, picture].astype(F32)
        columns[side, picture, 40:48] = jnp.concatenate([below, blank], axis=0)


def column_terms(picture, columns, weights, terms):
    for side in range(2):
        total = None
        for row_off in range(3):
            term = weights(row_off, 2 * side) * columns[side, picture, 7 + row_off : 7 + row_off + ROWS, :]
            total = term if total is None else total + term
        for strip in range(STRIPS):
            terms[side, picture, strip, 0:STRIP] = total[STRIP * strip : STRIP * strip + STRIP]


def convolve(rows, weights, left, right):
    spot = lax.broadcasted_iota(jnp.int32, (STRIP, COLS, LANES), 1)
    parts = []
    for col_off in range(3):
        total = None
        for row_off in range(3):
            term = weights[3 * row_off + col_off][None, :, :] * rows[row_off : row_off + STRIP]
            total = term if total is None else total + term
        parts.append(total)
    from_left = jnp.where(spot == 0, left[:, None, :], pltpu.roll(parts[0], 1, 1))
    from_right = jnp.where(spot == COLS - 1, right[:, None, :], pltpu.roll(parts[2], COLS - 1, 1))
    return parts[1] + from_left + from_right


def pick_heads(full, lane):
    kept = full[0:64]
    for h in range(1, 4):
        kept = jnp.where(lane == h, full[64 * h : 64 * h + 64], kept)
    return kept


def attend(mix, cot, gain, wqkv_ref, wout_ref, mask_ref, gw_ref, go_ref, gg_ref):
    scale = 1.0 / math.sqrt(32.0)
    lane = lax.broadcasted_iota(jnp.int32, (64, 128), 1) // 32
    mix = mix.astype(F32)
    inv = lax.rsqrt(jnp.mean(mix * mix, axis=-1, keepdims=True) + 1e-6)
    mi = mix * inv
    normed = (mi * gain).astype(BF16)
    qkv = dot(normed, wqkv_ref[...]).astype(BF16)
    gatt = dot_t(cot, wout_ref[...]).astype(BF16)
    parts = [(slice(64 * i, 64 * i + 64), 128 * half) for i in range(GROUPS) for half in range(2)]
    q, k, v = ([qkv[r, first + 256 * n : first + 256 * n + 128] for r, first in parts] for n in range(3))
    qexp = [jnp.concatenate([x] * 4, axis=0) * mask_ref[...] for x in q]
    doexp = [jnp.concatenate([gatt[r, first : first + 128]] * 4, axis=0) * mask_ref[...] for r, first in parts]
    st = [dot_t(x, y) * scale for x, y in zip(k, qexp)]
    dp = [dot_t(x, y) for x, y in zip(v, doexp)]
    e = [jnp.exp(x - jnp.max(x, axis=0, keepdims=True)) for x in st]
    p = [x * (1.0 / jnp.sum(x, axis=0, keepdims=True)) for x in e]
    pb = [x.astype(BF16) for x in p]
    ds = [(x * (y - jnp.sum(y * x, axis=0, keepdims=True)) * scale).astype(BF16) for x, y in zip(p, dp)]
    att = [pick_heads(dot_tl(x, y), lane) for x, y in zip(pb, v)]
    gvs = [dot(x, y) for x, y in zip(pb, doexp)]
    gqs = [pick_heads(dot_tl(x, y), lane) for x, y in zip(ds, k)]
    gks = [dot(x, y) for x, y in zip(ds, qexp)]
    att, gqs, gks, gvs = (
        [jnp.concatenate(x[2 * i : 2 * i + 2], axis=1).astype(BF16) for i in range(GROUPS)] for x in (att, gqs, gks, gvs)
    )
    gqkv = [jnp.concatenate(x, axis=0) for x in (gqs, gks, gvs)]
    go_ref[...] += dot_tl(jnp.concatenate(att, axis=0), cot)
    normed_t = normed.T
    gn = jnp.zeros((64 * GROUPS, 256), F32)
    for n in range(3):
        gw_ref[256 * n : 256 * n + 256] += dot(normed_t, gqkv[n])
        gn = gn + dot_t(gqkv[n], wqkv_ref[:, 256 * n : 256 * n + 256])
    gg_ref[...] += jnp.sum(gn * mi, axis=0, keepdims=True)
    scaled = gn * gain
    mean = jnp.mean(scaled * mix, axis=-1, keepdims=True)
    return (cot.astype(F32) + inv * scaled - mi * (inv * inv * mean)).astype(BF16)


def whole_kernel(
    x_hbm, skip_hbm, cot_hbm, kern_ref, wproj_hbm, gain_ref, wqkv_hbm, wout_hbm, perm_hbm, mask_hbm,
    ge_hbm, gs_hbm, whole_hbm, extra_out,
    xgrid, ggrid, act, dg, mix, got_mix, got_cot, mix_s, cot_s, back, gs,
    sides_out, sides_in, corners_out, corners_in, xcols, gcols, terms, gsides_out, gsides_in, gcorners_out, gcorners_in,
    gproj_t, gkern, gw_ref, go_ref, gg_ref, part_out, core_in, y_out, small_in, whole,
    ex_a, ex_b, ex_c, skip_ref, wproj_ref, wqkv_ref, wout_ref, perm_ref, mask_ref,
    load_sem, rim_send, rim_recv, cot_sem, mix_sem, back_send, back_recv, own_sem, store_sem,
    core_send, core_recv, scatter_sem, gather_sem, ey_sem, ez_sem, operand_sem,
):
    me = my_tile()
    tile_row, tile_col = me // GRID, lax.rem(me, GRID)
    dp, row, col = lax.axis_index("dp"), lax.axis_index("row"), lax.axis_index("col")
    core, chip = lax.rem(col, 2), col // 2
    q = dp * 2 + row
    mate = {"col": col + 1 - 2 * core}
    own = times(me, SHARE)

    def weight(n, lanes=slice(None)):
        return kern_ref[n // 3, n % 3 : n % 3 + 1, lanes]

    loads = [pltpu.make_async_copy(x_hbm.at[p], xgrid.at[p, pl.ds(1, ROWS)], load_sem.at[p]) for p in range(2)]
    operands = [
        pltpu.make_async_copy(a, b, operand_sem.at[n])
        for n, (a, b) in enumerate(
            (
                (skip_hbm, skip_ref), (wproj_hbm, wproj_ref), (wqkv_hbm, wqkv_ref),
                (wout_hbm, wout_ref), (perm_hbm, perm_ref), (mask_hbm, mask_ref),
            )
        )
    ]
    for copy in loads + operands:
        copy.start()
    barrier = pltpu.get_barrier_semaphore()

    def greet(i):
        pl.semaphore_signal(barrier, inc=1, device_id=tile_id(lax.rem(me + i, TILES)), device_id_type=MESH_ID)

    loop(1, TILES, greet)
    loop(
        0,
        TILES // 2,
        lambda i: pl.semaphore_signal(
            barrier,
            inc=1,
            device_id={"dp": 1 - dp, "row": i // 16, "col": lax.rem(i, 16) * 2 + core},
            device_id_type=MESH_ID,
        ),
    )
    loads[0].wait()
    collect_sides(0, xgrid, sides_out, corners_out)
    pl.semaphore_wait(barrier, TILES - 1 + TILES // 2)

    def rim_of(picture, turn):
        if turn == 0:
            refs = (xgrid, sides_out, sides_in, corners_out, corners_in)
        else:
            refs = (ggrid, gsides_out, gsides_in, gcorners_out, gcorners_in)
        return rim_copies(me, picture, turn, *refs, rim_send, rim_recv)

    for copy in rim_of(0, 0):
        copy.start()
    loads[1].wait()
    collect_sides(1, xgrid, sides_out, corners_out)
    for copy in rim_of(1, 0):
        copy.start()

    def cot_copy(target, slot):
        return pltpu.make_async_remote_copy(
            src_ref=cot_hbm.at[:, times(target, SHARE), :],
            dst_ref=got_cot.at[:, times(slot, SHARE), :],
            send_sem=cot_sem.at[0],
            recv_sem=cot_sem.at[1],
            device_id=tile_id(target),
            device_id_type=MESH_ID,
        )

    def mix_copy(picture, target, slot):
        return pltpu.make_async_remote_copy(
            src_ref=mix.at[picture, times(target, SHARE), :],
            dst_ref=got_mix.at[picture, times(slot, SHARE), :],
            send_sem=mix_sem.at[0, picture],
            recv_sem=mix_sem.at[1, picture],
            device_id=tile_id(target),
            device_id_type=MESH_ID,
        )

    def back_copy(picture, target, slot):
        return pltpu.make_async_remote_copy(
            src_ref=back.at[picture, times(target, SHARE), :],
            dst_ref=gs.at[picture, times(slot, SHARE), :],
            send_sem=back_send.at[picture],
            recv_sem=back_recv.at[picture, slot // BAND_TILES],
            device_id=tile_id(target),
            device_id_type=MESH_ID,
        )

    def passed(view, sem):
        pltpu.make_async_copy(view, view, sem).wait()

    rest = pl.ds(0, CELLS - SHARE)
    own_cot = pltpu.make_async_copy(cot_hbm.at[:, own, :], got_cot.at[:, own, :], own_sem.at[0])
    own_cot.start()
    for copy in operands:
        copy.wait()


    def forward_picture(picture):
        rim = rim_of(picture, 0)
        for copy in rim:
            copy.wait_recv()

        @pl.when(picture == 0)
        def _():
            loop(1, TILES, lambda i: cot_copy(lax.rem(me + i, TILES), me).start())

        clear_outside(me, picture, xgrid, sides_in, corners_in)
        column_stack(picture, sides_in, corners_in, xcols)
        column_terms(picture, xcols, lambda a, c: weight(3 * a + c), terms)

        def do_band(step):
            band = lax.rem(step + tile_row // 2, BANDS)
            cells = times(band, BAND_CELLS)

            def do_block(index):
                strip = band * 2 + index // LANE_BLOCKS
                lanes = times(lax.rem(index, LANE_BLOCKS), LANES)
                rows = xgrid[picture, pl.ds(strip * STRIP, STRIP + 2), :, lanes].astype(F32)
                pre = convolve(
                    rows,
                    [weight(n, lanes) for n in range(9)],
                    terms[0, picture, strip, 0:STRIP, lanes],
                    terms[1, picture, strip, 0:STRIP, lanes],
                )
                square = pre * pre
                tanh = jnp.tanh(pre * (GELU_1 + GELU_3 * square))
                half = 0.5 * pre
                activated = half + half * tanh
                slope = (0.5 + 0.5 * tanh) + half * (1.0 - tanh * tanh) * (GELU_1 + (3.0 * GELU_3) * square)
                here = times(strip, STRIP_CELLS)
                act[picture, here, lanes] = activated.astype(BF16).reshape(STRIP_CELLS, LANES)
                dg[picture, here, lanes] = slope.astype(BF16).reshape(STRIP_CELLS, LANES)

            loop(0, 2 * LANE_BLOCKS, do_block)
            projected = dot(act[picture, cells, :], wproj_ref[...])
            mix[picture, cells, :] = (skip_ref[picture, cells, :].astype(F32) + projected).astype(BF16)

            def send_mix(i):
                mix_copy(picture, band * BAND_TILES + lax.rem(me + i, BAND_TILES), me).start()

            loop(1, BAND_TILES, send_mix)

            @pl.when(band != me // BAND_TILES)
            def _():
                send_mix(0)

        loop(0, BANDS, do_band)

    loop(0, 2, forward_picture)


    gw_ref[...] = jnp.zeros_like(gw_ref)
    go_ref[...] = jnp.zeros_like(go_ref)
    gg_ref[...] = jnp.zeros_like(gg_ref)
    gproj_t[...] = jnp.zeros_like(gproj_t)
    own_cot.wait()
    passed(got_cot.at[:, rest, :], cot_sem.at[1])

    def attend_picture(picture):
        own_mix = pltpu.make_async_copy(mix.at[picture, own, :], got_mix.at[picture, own, :], own_sem.at[1])
        own_mix.start()
        perm = perm_ref[...]
        for b in range(4):
            r = slice(256 * b, 256 * b + 256)
            cot_s[:, 16 * b : 16 * b + 16, :] = dot(perm, got_cot[picture, r, :]).astype(BF16).reshape(16, 16, 256)
        passed(got_mix.at[picture, rest, :], mix_sem.at[1, picture])
        own_mix.wait()
        for b in range(4):
            r = slice(256 * b, 256 * b + 256)
            mix_s[:, 16 * b : 16 * b + 16, :] = dot(perm, got_mix[picture, r, :]).astype(BF16).reshape(16, 16, 256)

        def block(b):
            groups = pl.ds(b * GROUPS, GROUPS)
            out = attend(
                mix_s[groups].reshape(64 * GROUPS, 256), cot_s[groups].reshape(64 * GROUPS, 256), gain_ref[...],
                wqkv_ref, wout_ref, mask_ref, gw_ref, go_ref, gg_ref,
            )
            cot_s[groups] = out.reshape(GROUPS, 64, 256)

        loop(0, 16 // GROUPS, block)
        for b in range(4):
            rows = cot_s[:, 16 * b : 16 * b + 16, :].reshape(256, 256)
            back[picture, 256 * b : 256 * b + 256] = dot(perm, rows).astype(BF16)

        def send_back(i):
            target = lax.rem(tile_row + GRID - i // GRID, GRID) * GRID + lax.rem(
                tile_col + GRID - lax.rem(i, GRID), GRID
            )
            back_copy(picture, target, me).start()

        loop(1, TILES, send_back)
        own_back = pltpu.make_async_copy(back.at[picture, own, :], gs.at[picture, own, :], own_sem.at[2])
        own_back.start()
        own_back.wait()

    loop(0, 2, attend_picture)


    def core_copy(half):
        return pltpu.make_async_remote_copy(
            src_ref=part_out.at[half, :, 1 - core],
            dst_ref=core_in.at[half],
            send_sem=core_send.at[half],
            recv_sem=core_recv.at[half],
            device_id=mate,
            device_id_type=MESH_ID,
        )

    def remote(source, target, send, recv, device):
        return pltpu.make_async_remote_copy(
            src_ref=source, dst_ref=target, send_sem=send, recv_sem=recv, device_id=device, device_id_type=MESH_ID
        )

    def y_id(n):
        return {"dp": n // 2, "row": lax.rem(n, 2)}

    def z_id(n):
        return {"col": n * 2 + core}

    def piece(n):
        return times(n // 2, 16), times(lax.rem(n, 2), LANES)

    def share_id(n):
        return {"dp": n // 32, "row": lax.rem(n // 16, 2), "col": lax.rem(n, 16) * 2 + core}

    mine = q * 16 + chip

    def scatter_copy(half, to):
        source = y_out.at[(half, to // 16, *piece(lax.rem(to, 16)))]
        return remote(source, small_in.at[half, mine], scatter_sem.at[half, 0], scatter_sem.at[half, 1], share_id(to))

    def gather_copy(half, to):
        here = whole.at[(half, q, core, *piece(chip))]
        return remote(here, here, gather_sem.at[half, 0], gather_sem.at[half, 1], share_id(to))

    def mate_copy(half):
        here = whole.at[half, :, core]
        return remote(here, here, core_send.at[2 + half], core_recv.at[2 + half], mate)

    def others(count, mine, action):
        loop(1, count, lambda i: action(lax.rem(mine + i, count)))

    def total_of(ref, count):
        total = ref[0].astype(F32)
        for n in range(1, count):
            total = total + ref[n].astype(F32)
        return total

    def scatter(half):
        core_copy(half).wait_recv()
        for n in range(4):
            y_out[half, n] = (part_out[half, n, core].astype(F32) + core_in[half, n].astype(F32)).astype(BF16)
        others(TILES, mine, lambda n: scatter_copy(half, n).start())

    def gather(half):
        passed(small_in.at[half, pl.ds(0, TILES - 1)], scatter_sem.at[half, 1])
        small_in[half, mine] = y_out[(half, q, *piece(chip))]
        whole[(half, q, core, *piece(chip))] = total_of(small_in.at[half], TILES).astype(BF16)
        others(TILES, mine, lambda n: gather_copy(half, n).start())

    def gather_core(half):
        passed(small_in.at[half, pl.ds(0, TILES - 1)], gather_sem.at[half, 1])
        mate_copy(half).start()

    def reduction_sent(half):
        core_copy(half).wait_send()
        passed(small_in.at[half, pl.ds(0, TILES - 1)], scatter_sem.at[half, 0])
        passed(small_in.at[half, pl.ds(0, TILES - 1)], gather_sem.at[half, 0])

    def ey_copy(to):
        return remote(ex_b.at[q], ex_b.at[q], ey_sem.at[0], ey_sem.at[1], y_id(to))

    def ez_copy(to):
        return remote(ex_c.at[chip], ex_c.at[chip], ez_sem.at[0], ez_sem.at[1], z_id(to))

    for n in range(4):
        block = gw_ref[256 * n : 256 * n + 256] if n < 3 else go_ref[...]
        part_out[1, n] = block.astype(BF16).reshape(2, 128, 256)
    core_copy(1).start()


    spot = lax.broadcasted_iota(jnp.int32, (STRIP, COLS, LANES), 1)
    gkern[...] = jnp.zeros_like(gkern)

    def back_picture(picture):
        def do_band(step):
            band = lax.rem(step + tile_row // 2, BANDS)
            cells = times(band, BAND_CELLS)

            @pl.when(band != me // BAND_TILES)
            def _():
                passed(gs.at[picture, pl.ds(0, BAND_CELLS), :], back_recv.at[picture, band])

            @pl.when(band == me // BAND_TILES)
            def _():
                passed(gs.at[picture, pl.ds(0, BAND_CELLS - SHARE), :], back_recv.at[picture, band])

            flat = gs[picture, cells, :]
            flat_t = flat.T
            for n in range(4):
                lanes = slice(256 * n, 256 * n + 256)
                grad_act = dot_t(flat, wproj_ref[lanes, :])
                grad_pre = (grad_act * dg[picture, cells, lanes].astype(F32)).astype(BF16)
                ggrid[picture, pl.ds(1 + band * BAND, BAND), :, lanes] = grad_pre.reshape(BAND, COLS, 256)
                gproj_t[:, lanes] += dot(flat_t, act[picture, cells, lanes])

        loop(0, BANDS, do_band)
        collect_sides(picture, ggrid, gsides_out, gcorners_out)
        for copy in rim_of(picture, 1):
            copy.start()

        @pl.when(picture == 0)
        def _():
            scatter(1)

        @pl.when(picture == 1)
        def _():
            for n in range(4):
                part_out[0, n] = gproj_t[:, 256 * n : 256 * n + 256].T.astype(BF16).reshape(2, 128, 256)
            core_copy(0).start()
            gather(1)

        def kernel_block(block):
            lanes = times(block, LANES)

            def one(strip, sums):
                grads = ggrid[picture, pl.ds(1 + strip * STRIP, STRIP), :, lanes].astype(F32)
                rows = xgrid[picture, pl.ds(strip * STRIP, STRIP + 2), :, lanes].astype(F32)
                shifted = (
                    jnp.where(spot == COLS - 1, 0.0, pltpu.roll(grads, COLS - 1, 1)),
                    grads,
                    jnp.where(spot == 0, 0.0, pltpu.roll(grads, 1, 1)),
                )
                new = []
                for row_off in range(3):
                    for col_off in range(3):
                        product = shifted[col_off] * rows[row_off : row_off + STRIP]
                        product = product.reshape(STRIP * 4, 8, LANES).sum(axis=0)
                        new.append(sums[3 * row_off + col_off] + product)
                return tuple(new)

            sums = lax.fori_loop(0, STRIPS, one, tuple(jnp.zeros((8, LANES), F32) for _ in range(9)))
            for n in range(9):
                gkern[n : n + 1, lanes] += jnp.sum(sums[n], axis=0, keepdims=True)

        loop(0, LANE_BLOCKS // 4, kernel_block)

        @pl.when(picture == 1)
        def _():
            scatter(0)

        loop(LANE_BLOCKS // 4, LANE_BLOCKS, kernel_block)
        for row_off in range(3):
            for side in range(2):
                n = 3 * row_off + 2 * side
                beside = xcols[side, picture, 7 + row_off : 7 + row_off + ROWS, :]
                gkern[n : n + 1, :] += jnp.sum(
                    gsides_out[side, picture].astype(F32) * beside, axis=0, keepdims=True
                )

    loop(0, 2, back_picture)
    gs_store = pltpu.make_async_copy(gs, gs_hbm, own_sem.at[3])
    gs_store.start()


    extra = [gkern[0:9, 256 * n : 256 * n + 256] for n in range(4)]
    extra = jnp.concatenate(extra + [gg_ref[...], jnp.zeros((11, 256), F32)], axis=0).astype(BF16)
    ex_a[core] = extra
    ex_core = remote(ex_a.at[core], ex_a.at[core], core_send.at[4], core_recv.at[4], mate)
    ex_core.start()

    ex_core.wait_recv()
    ex_b[q] = total_of(ex_a, 2).astype(BF16)
    others(4, q, lambda n: ey_copy(n).start())
    gather_core(1)

    def store_copy(picture, band):
        cells = times(band, BAND_CELLS)
        return pltpu.make_async_copy(dg.at[picture, cells, :], ge_hbm.at[picture, cells, :], store_sem.at[picture, band])

    def last_start(picture):
        for copy in rim_of(picture, 1):
            copy.wait_recv()
        clear_outside(me, picture, ggrid, gsides_in, gcorners_in)
        column_stack(picture, gsides_in, gcorners_in, gcols)
        column_terms(picture, gcols, lambda a, c: weight(8 - 3 * a - c), terms)

    def last_bands(picture, begin, end):
        def do_band(band):
            def do_block(index):
                strip = band * 2 + index // LANE_BLOCKS
                lanes = times(lax.rem(index, LANE_BLOCKS), LANES)
                rows = ggrid[picture, pl.ds(strip * STRIP, STRIP + 2), :, lanes].astype(F32)
                total = convolve(
                    rows,
                    [weight(8 - n, lanes) for n in range(9)],
                    terms[0, picture, strip, 0:STRIP, lanes],
                    terms[1, picture, strip, 0:STRIP, lanes],
                )
                dg[picture, times(strip, STRIP_CELLS), lanes] = total.astype(BF16).reshape(STRIP_CELLS, LANES)

            loop(0, 2 * LANE_BLOCKS, do_block)
            store_copy(picture, band).start()

        loop(begin, end, do_band)

    last_start(0)
    last_bands(0, 0, 2)
    gather(0)
    passed(ex_b.at[pl.ds(0, 3)], ey_sem.at[1])
    ex_c[chip] = total_of(ex_b, 4).astype(BF16)
    others(16, chip, lambda n: ez_copy(n).start())
    last_bands(0, 2, 4)
    last_start(1)
    last_bands(1, 0, 4)
    passed(ex_c.at[pl.ds(0, 15)], ez_sem.at[1])
    extra_out[...] = total_of(ex_c, 16)


    passed(got_cot.at[:, rest, :], cot_sem.at[0])
    for picture in range(2):
        passed(mix.at[picture, rest, :], mix_sem.at[0, picture])
        passed(back.at[picture, rest, :], back_send.at[picture])
    for turn in range(2):
        for picture in range(2):
            for copy in rim_of(picture, turn):
                copy.wait_send()
    ex_core.wait_send()
    passed(ex_b.at[pl.ds(0, 3)], ey_sem.at[0])
    passed(ex_c.at[pl.ds(0, 15)], ez_sem.at[0])
    gs_store.wait()
    for picture in range(2):
        for band in range(BANDS):
            store_copy(picture, band).wait()
    mate_copy(1).wait_recv()
    stores = [pltpu.make_async_copy(whole.at[half], whole_hbm.at[half], own_sem.at[4 + half]) for half in range(2)]
    stores[1].start()
    gather_core(0)
    for half in range(2):
        reduction_sent(half)
    mate_copy(0).wait_recv()
    stores[0].start()
    mate_copy(0).wait_send()
    mate_copy(1).wait_send()
    for copy in stores:
        copy.wait()


def my_tile():
    return lax.axis_index("row") * 32 + lax.axis_index("col")


def constants():
    perm = np.zeros((256, 256), np.float32)
    for a in range(16):
        for b in range(16):
            perm[a * 16 + b, b * 16 + a] = 1
    mask = np.kron(np.eye(4), np.ones((64, 32))).astype(np.float32)
    return jnp.asarray(perm, BF16), jnp.asarray(mask, BF16)


def whole_call(x, skip, cot, kern, wproj, gain, wqkv, wout):
    vmem = pl.BlockSpec(memory_space=pltpu.VMEM)
    anywhere = pl.BlockSpec(memory_space=pl.ANY)
    dma = pltpu.SemaphoreType.DMA

    def bf(*shape):
        return pltpu.VMEM(shape, BF16)

    def fl(*shape):
        return pltpu.VMEM(shape, F32)

    rims = [bf(2, 2, ROWS, EXPAND), bf(2, 2, ROWS, EXPAND), bf(2, 4, 16, EXPAND), bf(2, 4, 16, EXPAND)]
    return pl.pallas_call(
        whole_kernel,
        out_shape=(
            jax.ShapeDtypeStruct((2, CELLS, EXPAND), BF16),
            jax.ShapeDtypeStruct((2, CELLS, WIDTH), BF16),
            jax.ShapeDtypeStruct((2, 4, 2, 128, 256), BF16),
            jax.ShapeDtypeStruct((48, 256), F32),
        ),
        in_specs=[anywhere] * 3 + [vmem, anywhere, vmem] + [anywhere] * 4,
        out_specs=(anywhere, anywhere, anywhere, vmem),
        scratch_shapes=[
            bf(2, ROWS + 2, COLS, EXPAND), bf(2, ROWS + 2, COLS, EXPAND), bf(2, CELLS, EXPAND), bf(2, CELLS, EXPAND),
            bf(2, CELLS, WIDTH), bf(2, CELLS, WIDTH), bf(2, CELLS, WIDTH), bf(16, 64, WIDTH), bf(16, 64, WIDTH),
            bf(2, CELLS, WIDTH), bf(2, CELLS, WIDTH),
        ]
        + rims
        + [fl(2, 2, 48, EXPAND), fl(2, 2, 48, EXPAND), fl(2, 2, STRIPS, 8, EXPAND)]
        + rims
        + [
            fl(WIDTH, EXPAND), fl(16, EXPAND), fl(3 * WIDTH, WIDTH), fl(WIDTH, WIDTH), fl(1, WIDTH),
            bf(2, 4, 2, 128, 256), bf(2, 4, 128, 256), bf(2, 4, 128, 256),
            bf(2, TILES, 16, LANES), bf(2, 4, 2, 128, 256),
            bf(2, 48, 256), bf(4, 48, 256), bf(16, 48, 256),
            bf(2, CELLS, WIDTH), bf(EXPAND, WIDTH), bf(WIDTH, 3 * WIDTH), bf(WIDTH, WIDTH), bf(256, 256), bf(256, LANES),
            dma((2,)), dma((2, 2, 8)), dma((2, 2, 8)), dma((2,)), dma((2, 2)), dma((2,)), dma((2, BANDS)),
            dma((6,)), dma((2, BANDS)),
            dma((5,)), dma((5,)), dma((2, 2)), dma((2, 2)), dma((2,)), dma((2,)), dma((6,)),
        ],
        compiler_params=pltpu.CompilerParams(
            collective_id=0, has_side_effects=True, vmem_limit_bytes=56 * 2**20
        ),
        name="whole",
    )(x, skip, cot, kern, wproj, gain, wqkv, wout, *constants())


def finish_kernel(
    ge_hbm, gs_hbm, whole_hbm, extra_ref, ge_out, gs_out, gkern_out, gproj_out, gwqkv_out, gout_out, ggain_out,
    ge_held, gs_held, whole_ref, gproj, gwqkv, gout, sems, *, scale
):
    ways = [(whole_hbm, whole_ref, None)]
    for picture in range(2):
        for part in range(4):
            here = (picture, pl.ds(256 * part, 256))
            ways.append((ge_hbm.at[here], ge_held.at[here], ge_out.at[here]))
    ways.append((gs_hbm, gs_held, gs_out))
    inward = [pltpu.make_async_copy(a, b, sems.at[0, n]) for n, (a, b, _) in enumerate(ways)]
    outward = [pltpu.make_async_copy(b, c, sems.at[1, n]) for n, (_, b, c) in enumerate(ways) if n]
    results = [
        pltpu.make_async_copy(a, b, sems.at[1, len(ways) + n])
        for n, (a, b) in enumerate(((gproj, gproj_out), (gwqkv, gwqkv_out), (gout, gout_out)))
    ]
    for copy in inward:
        copy.start()
    for first, second in zip(inward[1:5], outward[:4]):
        first.wait()
        second.start()
    inward[0].wait()
    for n in range(8):
        block = whole_ref[n // 4, n % 4].reshape(256, 256).astype(F32) * scale
        if n < 4:
            gproj[256 * n : 256 * n + 256, :] = block
            some = extra_ref[9 * n : 9 * n + 9, :] * scale
            for row in range(3):
                gkern_out[row, :, 256 * n : 256 * n + 256] = some[3 * row : 3 * row + 3]
        elif n < 7:
            gwqkv[:, 256 * (n - 4) : 256 * (n - 4) + 256] = block
        else:
            gout[...] = block
    ggain_out[...] = extra_ref[36:37, :] * scale
    for copy in results:
        copy.start()
    for first, second in zip(inward[5:], outward[4:]):
        first.wait()
        second.start()
    for copy in outward + results:
        copy.wait()


def finish(ge, gs, whole, extra, scale):
    vmem = pl.BlockSpec(memory_space=pltpu.VMEM)
    anywhere = pl.BlockSpec(memory_space=pl.ANY)

    def kernel(*refs):
        finish_kernel(*refs, scale=scale)

    return pl.pallas_call(
        kernel,
        out_shape=(
            jax.ShapeDtypeStruct((2, CELLS, EXPAND), BF16),
            jax.ShapeDtypeStruct((2, CELLS, WIDTH), BF16),
            jax.ShapeDtypeStruct((3, 3, EXPAND), F32),
            jax.ShapeDtypeStruct((EXPAND, WIDTH), F32),
            jax.ShapeDtypeStruct((WIDTH, 3 * WIDTH), F32),
            jax.ShapeDtypeStruct((WIDTH, WIDTH), F32),
            jax.ShapeDtypeStruct((1, WIDTH), F32),
        ),
        in_specs=[anywhere, anywhere, anywhere, vmem],
        out_specs=(anywhere, anywhere, vmem, anywhere, anywhere, anywhere, vmem),
        scratch_shapes=[
            pltpu.VMEM((2, CELLS, EXPAND), BF16),
            pltpu.VMEM((2, CELLS, WIDTH), BF16),
            pltpu.VMEM((2, 4, 2, 128, 256), BF16),
            pltpu.VMEM((EXPAND, WIDTH), F32),
            pltpu.VMEM((WIDTH, 3 * WIDTH), F32),
            pltpu.VMEM((WIDTH, WIDTH), F32),
            pltpu.SemaphoreType.DMA((2, 13)),
        ],
        compiler_params=pltpu.CompilerParams(vmem_limit_bytes=60 * 2**20),
        name="finish",
    )(ge, gs, whole, extra)


def on_device(expanded, skip, cotangent, depth_kernel, w_proj, norm_gain, w_qkv, w_out):
    ge, gs, whole, extra = whole_call(
        expanded[:, 0],
        skip.reshape(2, CELLS, WIDTH),
        cotangent.reshape(2, CELLS, WIDTH),
        depth_kernel,
        w_proj,
        norm_gain.reshape(1, WIDTH),
        w_qkv,
        w_out,
    )
    scale = 1.0 / math.sqrt(2 * lax.axis_size("dp") * TILES * CELLS)
    ge, gs, gkern, gproj, gwqkv, gout, ggain = finish(ge, gs, whole, extra, scale)
    return (
        ge.reshape(2, 1, ROWS, COLS, EXPAND),
        gs.reshape(2, 1, ROWS, COLS, WIDTH),
        gkern,
        gproj,
        gwqkv,
        gout,
        ggain.reshape(WIDTH),
    )


def solution(mesh):
    tiled = P("dp", ("row", "col"), None, None, None)
    return jax.shard_map(
        on_device,
        mesh=mesh,
        in_specs=(tiled, tiled, tiled, P(), P(), P(), P(), P()),
        out_specs=(tiled, tiled, P(), P(), P(), P(), P()),
        check_vma=False,
    )
```

```python
import math

import jax
import jax.numpy as jnp
import numpy as np
from jax import lax
from jax.experimental import pallas as pl
from jax.experimental.pallas import tpu as pltpu
from jax.sharding import PartitionSpec as P

GRID = 8
TILES = 64
ROWS = 32
COLS = 32
CELLS = ROWS * COLS
LANES = 128
WIDTH = 256
EXPAND = 1024
LANE_BLOCKS = EXPAND // LANES
STRIP = 4
STRIPS = ROWS // STRIP
STRIP_CELLS = STRIP * COLS
BAND = 8
BANDS = ROWS // BAND
BAND_CELLS = BAND * COLS
BAND_TILES = TILES // BANDS
GROUPS = 8
SHARE = CELLS // TILES
F32 = jnp.float32
BF16 = jnp.bfloat16
MESH_ID = pl.DeviceIdType.MESH
GELU_1 = math.sqrt(2.0 / math.pi)
GELU_3 = GELU_1 * 0.044715
SIDES = ((0, -1), (0, 1))
ENDS = ((-1, 0), (1, 0))
CORNERS = ((-1, -1), (-1, 1), (1, -1), (1, 1))
AROUND = SIDES + ENDS + CORNERS


def dot(a, b):
    return lax.dot_general(a, b, (((1,), (0,)), ((), ())), preferred_element_type=F32)


def dot_t(a, b):
    return lax.dot_general(a, b, (((1,), (1,)), ((), ())), preferred_element_type=F32)


def dot_tl(a, b):
    return lax.dot_general(a, b, (((0,), (0,)), ((), ())), preferred_element_type=F32)


def tile_id(tile):
    return {"row": tile // 32, "col": lax.rem(tile, 32)}


def times(start, count, size=None):
    return pl.ds(pl.multiple_of(start * count, count), size or count)


def loop(begin, end, body):
    def one(i, carry):
        body(i)
        return carry

    lax.fori_loop(begin, end, one, 0)


def neighbours(me):
    tile_row, tile_col = me // GRID, lax.rem(me, GRID)
    return {
        (down, right): lax.rem(tile_row + down + GRID, GRID) * GRID + lax.rem(tile_col + right + GRID, GRID)
        for down in (-1, 0, 1)
        for right in (-1, 0, 1)
        if (down, right) != (0, 0)
    }


def rim_copies(me, picture, turn, grid_ref, sides_out, sides_in, corners_out, corners_in, send_sem, recv_sem):
    around = neighbours(me)
    copies = []
    for n, (down, right) in enumerate(AROUND):
        if down == 0:
            source = sides_out.at[(right + 1) // 2, picture]
            target = sides_in.at[(1 - right) // 2, picture]
        elif right == 0:
            source = grid_ref.at[picture, 1 if down < 0 else ROWS]
            target = grid_ref.at[picture, ROWS + 1 if down < 0 else 0]
        else:
            place = CORNERS.index((down, right))
            source = corners_out.at[picture, place]
            target = corners_in.at[picture, 3 - place]
        copies.append(
            pltpu.make_async_remote_copy(
                src_ref=source,
                dst_ref=target,
                send_sem=send_sem.at[turn, picture, n],
                recv_sem=recv_sem.at[turn, picture, n],
                device_id=tile_id(around[down, right]),
                device_id_type=MESH_ID,
            )
        )
    return copies


def collect_sides(picture, grid_ref, sides_out, corners_out):
    for side in range(2):
        for start in range(0, ROWS, 16):
            window = grid_ref[picture, 1 + start : 17 + start, 16 * side : 16 * side + 16, :]
            column = window.astype(F32)[:, 15 * side, :]
            sides_out[side, picture, start : start + 16, :] = column.astype(BF16)
    for place, (down, right) in enumerate(CORNERS):
        edge = 0 if down < 0 else 16
        row = 0 if down < 0 else 15
        one = sides_out[(right + 1) // 2, picture, edge : edge + 16, :].astype(F32)[row : row + 1]
        corners_out[picture, place] = jnp.concatenate([one, jnp.zeros((15, EXPAND), F32)], axis=0).astype(BF16)


def clear_outside(me, picture, grid_ref, sides_in, corners_in):
    tile_row, tile_col = me // GRID, lax.rem(me, GRID)
    none = jnp.zeros((16, EXPAND), BF16)
    for side, last in ((0, 0), (1, GRID - 1)):

        @pl.when(tile_col == last)
        def _():
            sides_in[side, picture] = jnp.zeros((ROWS, EXPAND), BF16)
            corners_in[picture, side] = none
            corners_in[picture, 2 + side] = none

    for end, last in ((0, 0), (1, GRID - 1)):

        @pl.when(tile_row == last)
        def _():
            grid_ref[picture, (ROWS + 1) * end] = jnp.zeros((COLS, EXPAND), BF16)
            corners_in[picture, 2 * end] = none
            corners_in[picture, 2 * end + 1] = none


def column_stack(picture, sides_in, corners_in, columns):
    blank = jnp.zeros((7, EXPAND), F32)
    for side in range(2):
        above = corners_in[picture, side].astype(F32)[0:1]
        below = corners_in[picture, 2 + side].astype(F32)[0:1]
        columns[side, picture, 0:8] = jnp.concatenate([blank, above], axis=0)
        columns[side, picture, 8 : 8 + ROWS] = sides_in[side, picture].astype(F32)
        columns[side, picture, 40:48] = jnp.concatenate([below, blank], axis=0)


def column_terms(picture, columns, weights, terms):
    for side in range(2):
        total = None
        for row_off in range(3):
            term = weights(row_off, 2 * side) * columns[side, picture, 7 + row_off : 7 + row_off + ROWS, :]
            total = term if total is None else total + term
        for strip in range(STRIPS):
            terms[side, picture, strip, 0:STRIP] = total[STRIP * strip : STRIP * strip + STRIP]


def convolve(rows, weights, left, right):
    spot = lax.broadcasted_iota(jnp.int32, (STRIP, COLS, LANES), 1)
    parts = []
    for col_off in range(3):
        total = None
        for row_off in range(3):
            term = weights[3 * row_off + col_off][None, :, :] * rows[row_off : row_off + STRIP]
            total = term if total is None else total + term
        parts.append(total)
    from_left = jnp.where(spot == 0, left[:, None, :], pltpu.roll(parts[0], 1, 1))
    from_right = jnp.where(spot == COLS - 1, right[:, None, :], pltpu.roll(parts[2], COLS - 1, 1))
    return parts[1] + from_left + from_right


def pick_heads(full, lane):
    kept = full[0:64]
    for h in range(1, 4):
        kept = jnp.where(lane == h, full[64 * h : 64 * h + 64], kept)
    return kept


def attend(mix, cot, gain, wqkv_ref, wout_ref, mask_ref, gw_ref, go_ref, gg_ref):
    scale = 1.0 / math.sqrt(32.0)
    lane = lax.broadcasted_iota(jnp.int32, (64, 128), 1) // 32
    mix = mix.astype(F32)
    inv = lax.rsqrt(jnp.mean(mix * mix, axis=-1, keepdims=True) + 1e-6)
    mi = mix * inv
    normed = (mi * gain).astype(BF16)
    qkv = dot(normed, wqkv_ref[...]).astype(BF16)
    gatt = dot_t(cot, wout_ref[...]).astype(BF16)
    parts = [(slice(64 * i, 64 * i + 64), 128 * half) for i in range(GROUPS) for half in range(2)]
    q, k, v = ([qkv[r, first + 256 * n : first + 256 * n + 128] for r, first in parts] for n in range(3))
    qexp = [jnp.concatenate([x] * 4, axis=0) * mask_ref[...] for x in q]
    doexp = [jnp.concatenate([gatt[r, first : first + 128]] * 4, axis=0) * mask_ref[...] for r, first in parts]
    st = [dot_t(x, y) * scale for x, y in zip(k, qexp)]
    dp = [dot_t(x, y) for x, y in zip(v, doexp)]
    e = [jnp.exp(x - jnp.max(x, axis=0, keepdims=True)) for x in st]
    p = [x * (1.0 / jnp.sum(x, axis=0, keepdims=True)) for x in e]
    pb = [x.astype(BF16) for x in p]
    ds = [(x * (y - jnp.sum(y * x, axis=0, keepdims=True)) * scale).astype(BF16) for x, y in zip(p, dp)]
    att = [pick_heads(dot_tl(x, y), lane) for x, y in zip(pb, v)]
    gvs = [dot(x, y) for x, y in zip(pb, doexp)]
    gqs = [pick_heads(dot_tl(x, y), lane) for x, y in zip(ds, k)]
    gks = [dot(x, y) for x, y in zip(ds, qexp)]
    att, gqs, gks, gvs = (
        [jnp.concatenate(x[2 * i : 2 * i + 2], axis=1).astype(BF16) for i in range(GROUPS)] for x in (att, gqs, gks, gvs)
    )
    gqkv = [jnp.concatenate(x, axis=0) for x in (gqs, gks, gvs)]
    go_ref[...] += dot_tl(jnp.concatenate(att, axis=0), cot)
    normed_t = normed.T
    gn = jnp.zeros((64 * GROUPS, 256), F32)
    for n in range(3):
        gw_ref[256 * n : 256 * n + 256] += dot(normed_t, gqkv[n])
        gn = gn + dot_t(gqkv[n], wqkv_ref[:, 256 * n : 256 * n + 256])
    gg_ref[...] += jnp.sum(gn * mi, axis=0, keepdims=True)
    scaled = gn * gain
    mean = jnp.mean(scaled * mix, axis=-1, keepdims=True)
    return (cot.astype(F32) + inv * scaled - mi * (inv * inv * mean)).astype(BF16)


def whole_kernel(
    x_hbm, skip_hbm, cot_hbm, kern_ref, wproj_hbm, gain_ref, wqkv_hbm, wout_hbm, perm_hbm, mask_hbm,
    ge_hbm, gs_hbm, whole_hbm, extra_out,
    xgrid, ggrid, act, dg, mix, got_mix, got_cot, mix_s, cot_s, back, gs,
    sides_out, sides_in, corners_out, corners_in, xcols, gcols, terms, gsides_out, gsides_in, gcorners_out, gcorners_in,
    gproj_t, gkern, gw_ref, go_ref, gg_ref, part_out, core_in, y_out, small_in, whole,
    ex_a, ex_b, ex_c, skip_ref, wproj_ref, wqkv_ref, wout_ref, perm_ref, mask_ref,
    load_sem, rim_send, rim_recv, cot_sem, mix_sem, back_send, back_recv, own_sem, store_sem,
    core_send, core_recv, scatter_sem, gather_sem, ey_sem, ez_sem, operand_sem,
):
    me = my_tile()
    tile_row, tile_col = me // GRID, lax.rem(me, GRID)
    dp, row, col = lax.axis_index("dp"), lax.axis_index("row"), lax.axis_index("col")
    core, chip = lax.rem(col, 2), col // 2
    q = dp * 2 + row
    mate = {"col": col + 1 - 2 * core}
    own = times(me, SHARE)

    def weight(n, lanes=slice(None)):
        return kern_ref[n // 3, n % 3 : n % 3 + 1, lanes]

    loads = [pltpu.make_async_copy(x_hbm.at[p], xgrid.at[p, pl.ds(1, ROWS)], load_sem.at[p]) for p in range(2)]
    operands = [
        pltpu.make_async_copy(a, b, operand_sem.at[n])
        for n, (a, b) in enumerate(
            (
                (skip_hbm, skip_ref), (wproj_hbm, wproj_ref), (wqkv_hbm, wqkv_ref),
                (wout_hbm, wout_ref), (perm_hbm, perm_ref), (mask_hbm, mask_ref),
            )
        )
    ]
    for copy in loads + operands:
        copy.start()
    barrier = pltpu.get_barrier_semaphore()

    def greet(i):
        pl.semaphore_signal(barrier, inc=1, device_id=tile_id(lax.rem(me + i, TILES)), device_id_type=MESH_ID)

    loop(1, TILES, greet)
    loop(
        0,
        TILES // 2,
        lambda i: pl.semaphore_signal(
            barrier,
            inc=1,
            device_id={"dp": 1 - dp, "row": i // 16, "col": lax.rem(i, 16) * 2 + core},
            device_id_type=MESH_ID,
        ),
    )
    loads[0].wait()
    collect_sides(0, xgrid, sides_out, corners_out)
    pl.semaphore_wait(barrier, TILES - 1 + TILES // 2)

    def rim_of(picture, turn):
        if turn == 0:
            refs = (xgrid, sides_out, sides_in, corners_out, corners_in)
        else:
            refs = (ggrid, gsides_out, gsides_in, gcorners_out, gcorners_in)
        return rim_copies(me, picture, turn, *refs, rim_send, rim_recv)

    for copy in rim_of(0, 0):
        copy.start()
    loads[1].wait()
    collect_sides(1, xgrid, sides_out, corners_out)
    for copy in rim_of(1, 0):
        copy.start()

    def cot_copy(target, slot):
        return pltpu.make_async_remote_copy(
            src_ref=cot_hbm.at[:, times(target, SHARE), :],
            dst_ref=got_cot.at[:, times(slot, SHARE), :],
            send_sem=cot_sem.at[0],
            recv_sem=cot_sem.at[1],
            device_id=tile_id(target),
            device_id_type=MESH_ID,
        )

    def mix_copy(picture, target, slot):
        return pltpu.make_async_remote_copy(
            src_ref=mix.at[picture, times(target, SHARE), :],
            dst_ref=got_mix.at[picture, times(slot, SHARE), :],
            send_sem=mix_sem.at[0, picture],
            recv_sem=mix_sem.at[1, picture],
            device_id=tile_id(target),
            device_id_type=MESH_ID,
        )

    def back_copy(picture, target, slot):
        return pltpu.make_async_remote_copy(
            src_ref=back.at[picture, times(target, SHARE), :],
            dst_ref=gs.at[picture, times(slot, SHARE), :],
            send_sem=back_send.at[picture],
            recv_sem=back_recv.at[picture, slot // BAND_TILES],
            device_id=tile_id(target),
            device_id_type=MESH_ID,
        )

    def passed(view, sem):
        pltpu.make_async_copy(view, view, sem).wait()

    rest = pl.ds(0, CELLS - SHARE)
    own_cot = pltpu.make_async_copy(cot_hbm.at[:, own, :], got_cot.at[:, own, :], own_sem.at[0])
    own_cot.start()
    for copy in operands:
        copy.wait()


    def forward_picture(picture):
        rim = rim_of(picture, 0)
        for copy in rim:
            copy.wait_recv()

        @pl.when(picture == 0)
        def _():
            loop(1, TILES, lambda i: cot_copy(lax.rem(me + i, TILES), me).start())

        clear_outside(me, picture, xgrid, sides_in, corners_in)
        column_stack(picture, sides_in, corners_in, xcols)
        column_terms(picture, xcols, lambda a, c: weight(3 * a + c), terms)

        def do_band(step):
            band = lax.rem(step + tile_row // 2, BANDS)
            cells = times(band, BAND_CELLS)

            def do_block(index):
                strip = band * 2 + index // LANE_BLOCKS
                lanes = times(lax.rem(index, LANE_BLOCKS), LANES)
                rows = xgrid[picture, pl.ds(strip * STRIP, STRIP + 2), :, lanes].astype(F32)
                pre = convolve(
                    rows,
                    [weight(n, lanes) for n in range(9)],
                    terms[0, picture, strip, 0:STRIP, lanes],
                    terms[1, picture, strip, 0:STRIP, lanes],
                )
                square = pre * pre
                tanh = jnp.tanh(pre * (GELU_1 + GELU_3 * square))
                half = 0.5 * pre
                activated = half + half * tanh
                slope = (0.5 + 0.5 * tanh) + half * (1.0 - tanh * tanh) * (GELU_1 + (3.0 * GELU_3) * square)
                here = times(strip, STRIP_CELLS)
                act[picture, here, lanes] = activated.astype(BF16).reshape(STRIP_CELLS, LANES)
                dg[picture, here, lanes] = slope.astype(BF16).reshape(STRIP_CELLS, LANES)

            loop(0, 2 * LANE_BLOCKS, do_block)
            projected = dot(act[picture, cells, :], wproj_ref[...])
            mix[picture, cells, :] = (skip_ref[picture, cells, :].astype(F32) + projected).astype(BF16)

            def send_mix(i):
                mix_copy(picture, band * BAND_TILES + lax.rem(me + i, BAND_TILES), me).start()

            loop(1, BAND_TILES, send_mix)

            @pl.when(band != me // BAND_TILES)
            def _():
                send_mix(0)

        loop(0, BANDS, do_band)

    loop(0, 2, forward_picture)


    gw_ref[...] = jnp.zeros_like(gw_ref)
    go_ref[...] = jnp.zeros_like(go_ref)
    gg_ref[...] = jnp.zeros_like(gg_ref)
    gproj_t[...] = jnp.zeros_like(gproj_t)
    own_cot.wait()
    passed(got_cot.at[:, rest, :], cot_sem.at[1])

    def attend_picture(picture):
        own_mix = pltpu.make_async_copy(mix.at[picture, own, :], got_mix.at[picture, own, :], own_sem.at[1])
        own_mix.start()
        perm = perm_ref[...]
        for b in range(4):
            r = slice(256 * b, 256 * b + 256)
            cot_s[:, 16 * b : 16 * b + 16, :] = dot(perm, got_cot[picture, r, :]).astype(BF16).reshape(16, 16, 256)
        passed(got_mix.at[picture, rest, :], mix_sem.at[1, picture])
        own_mix.wait()
        for b in range(4):
            r = slice(256 * b, 256 * b + 256)
            mix_s[:, 16 * b : 16 * b + 16, :] = dot(perm, got_mix[picture, r, :]).astype(BF16).reshape(16, 16, 256)

        def block(b):
            groups = pl.ds(b * GROUPS, GROUPS)
            out = attend(
                mix_s[groups].reshape(64 * GROUPS, 256), cot_s[groups].reshape(64 * GROUPS, 256), gain_ref[...],
                wqkv_ref, wout_ref, mask_ref, gw_ref, go_ref, gg_ref,
            )
            cot_s[groups] = out.reshape(GROUPS, 64, 256)

        loop(0, 16 // GROUPS, block)
        for b in range(4):
            rows = cot_s[:, 16 * b : 16 * b + 16, :].reshape(256, 256)
            back[picture, 256 * b : 256 * b + 256] = dot(perm, rows).astype(BF16)

        def send_back(i):
            target = lax.rem(tile_row + GRID - i // GRID, GRID) * GRID + lax.rem(
                tile_col + GRID - lax.rem(i, GRID), GRID
            )
            back_copy(picture, target, me).start()

        own_back = pltpu.make_async_copy(back.at[picture, own, :], gs.at[picture, own, :], own_sem.at[2])
        own_back.start()
        loop(1, TILES, send_back)
        own_back.wait()

    loop(0, 2, attend_picture)


    def core_copy(half):
        return pltpu.make_async_remote_copy(
            src_ref=part_out.at[half, :, 1 - core],
            dst_ref=core_in.at[half],
            send_sem=core_send.at[half],
            recv_sem=core_recv.at[half],
            device_id=mate,
            device_id_type=MESH_ID,
        )

    def remote(source, target, send, recv, device):
        return pltpu.make_async_remote_copy(
            src_ref=source, dst_ref=target, send_sem=send, recv_sem=recv, device_id=device, device_id_type=MESH_ID
        )

    def y_id(n):
        return {"dp": n // 2, "row": lax.rem(n, 2)}

    def z_id(n):
        return {"col": n * 2 + core}

    def piece(n):
        return times(n // 2, 16), times(lax.rem(n, 2), LANES)

    def share_id(n):
        return {"dp": n // 32, "row": lax.rem(n // 16, 2), "col": lax.rem(n, 16) * 2 + core}

    mine = q * 16 + chip

    def scatter_copy(half, to):
        source = y_out.at[(half, to // 16, *piece(lax.rem(to, 16)))]
        return remote(source, small_in.at[half, mine], scatter_sem.at[half, 0], scatter_sem.at[half, 1], share_id(to))

    def gather_copy(half, to):
        here = whole.at[(half, q, core, *piece(chip))]
        return remote(here, here, gather_sem.at[half, 0], gather_sem.at[half, 1], share_id(to))

    def mate_copy(half):
        here = whole.at[half, :, core]
        return remote(here, here, core_send.at[2 + half], core_recv.at[2 + half], mate)

    def others(count, mine, action):
        loop(1, count, lambda i: action(lax.rem(mine + i, count)))

    def total_of(ref, count):
        total = ref[0].astype(F32)
        for n in range(1, count):
            total = total + ref[n].astype(F32)
        return total

    def scatter(half):
        core_copy(half).wait_recv()
        for n in range(4):
            y_out[half, n] = (part_out[half, n, core].astype(F32) + core_in[half, n].astype(F32)).astype(BF16)
        others(TILES, mine, lambda n: scatter_copy(half, n).start())

    def gather(half):
        passed(small_in.at[half, pl.ds(0, TILES - 1)], scatter_sem.at[half, 1])
        small_in[half, mine] = y_out[(half, q, *piece(chip))]
        whole[(half, q, core, *piece(chip))] = total_of(small_in.at[half], TILES).astype(BF16)
        others(TILES, mine, lambda n: gather_copy(half, n).start())

    def gather_core(half):
        passed(small_in.at[half, pl.ds(0, TILES - 1)], gather_sem.at[half, 1])
        mate_copy(half).start()

    def reduction_sent(half):
        core_copy(half).wait_send()
        passed(small_in.at[half, pl.ds(0, TILES - 1)], scatter_sem.at[half, 0])
        passed(small_in.at[half, pl.ds(0, TILES - 1)], gather_sem.at[half, 0])

    def ey_copy(to):
        return remote(ex_b.at[q], ex_b.at[q], ey_sem.at[0], ey_sem.at[1], y_id(to))

    def ez_copy(to):
        return remote(ex_c.at[chip], ex_c.at[chip], ez_sem.at[0], ez_sem.at[1], z_id(to))

    for n in range(4):
        block = gw_ref[256 * n : 256 * n + 256] if n < 3 else go_ref[...]
        part_out[1, n] = block.astype(BF16).reshape(2, 128, 256)
    core_copy(1).start()


    spot = lax.broadcasted_iota(jnp.int32, (STRIP, COLS, LANES), 1)
    gkern[...] = jnp.zeros_like(gkern)

    def back_picture(picture):
        def do_band(step):
            band = lax.rem(step + tile_row // 2, BANDS)
            cells = times(band, BAND_CELLS)

            @pl.when(band != me // BAND_TILES)
            def _():
                passed(gs.at[picture, pl.ds(0, BAND_CELLS), :], back_recv.at[picture, band])

            @pl.when(band == me // BAND_TILES)
            def _():
                passed(gs.at[picture, pl.ds(0, BAND_CELLS - SHARE), :], back_recv.at[picture, band])

            flat = gs[picture, cells, :]
            flat_t = flat.T
            for n in range(4):
                lanes = slice(256 * n, 256 * n + 256)
                grad_act = dot_t(flat, wproj_ref[lanes, :])
                grad_pre = (grad_act * dg[picture, cells, lanes].astype(F32)).astype(BF16)
                ggrid[picture, pl.ds(1 + band * BAND, BAND), :, lanes] = grad_pre.reshape(BAND, COLS, 256)
                gproj_t[:, lanes] += dot(flat_t, act[picture, cells, lanes])

        loop(0, BANDS, do_band)

        @pl.when(picture == 1)
        def _():
            for n in range(4):
                part_out[0, n] = gproj_t[:, 256 * n : 256 * n + 256].T.astype(BF16).reshape(2, 128, 256)
            core_copy(0).start()

        collect_sides(picture, ggrid, gsides_out, gcorners_out)
        for copy in rim_of(picture, 1):
            copy.start()

        @pl.when(picture == 0)
        def _():
            scatter(1)

        @pl.when(picture == 1)
        def _():
            gather(1)

        def kernel_block(block):
            lanes = times(block, LANES)

            def one(strip, sums):
                grads = ggrid[picture, pl.ds(1 + strip * STRIP, STRIP), :, lanes].astype(F32)
                rows = xgrid[picture, pl.ds(strip * STRIP, STRIP + 2), :, lanes].astype(F32)
                shifted = (
                    jnp.where(spot == COLS - 1, 0.0, pltpu.roll(grads, COLS - 1, 1)),
                    grads,
                    jnp.where(spot == 0, 0.0, pltpu.roll(grads, 1, 1)),
                )
                new = []
                for row_off in range(3):
                    for col_off in range(3):
                        product = shifted[col_off] * rows[row_off : row_off + STRIP]
                        product = product.reshape(STRIP * 4, 8, LANES).sum(axis=0)
                        new.append(sums[3 * row_off + col_off] + product)
                return tuple(new)

            sums = lax.fori_loop(0, STRIPS, one, tuple(jnp.zeros((8, LANES), F32) for _ in range(9)))
            for n in range(9):
                gkern[n : n + 1, lanes] += jnp.sum(sums[n], axis=0, keepdims=True)

        loop(0, LANE_BLOCKS // 4, kernel_block)

        @pl.when(picture == 1)
        def _():
            scatter(0)

        loop(LANE_BLOCKS // 4, LANE_BLOCKS, kernel_block)
        for row_off in range(3):
            for side in range(2):
                n = 3 * row_off + 2 * side
                beside = xcols[side, picture, 7 + row_off : 7 + row_off + ROWS, :]
                gkern[n : n + 1, :] += jnp.sum(
                    gsides_out[side, picture].astype(F32) * beside, axis=0, keepdims=True
                )

    loop(0, 2, back_picture)
    gs_store = pltpu.make_async_copy(gs, gs_hbm, own_sem.at[3])
    gs_store.start()


    extra = [gkern[0:9, 256 * n : 256 * n + 256] for n in range(4)]
    extra = jnp.concatenate(extra + [gg_ref[...], jnp.zeros((11, 256), F32)], axis=0).astype(BF16)
    ex_a[core] = extra
    ex_core = remote(ex_a.at[core], ex_a.at[core], core_send.at[4], core_recv.at[4], mate)
    ex_core.start()

    gather_core(1)

    def store_copy(picture, band):
        cells = times(band, BAND_CELLS)
        return pltpu.make_async_copy(dg.at[picture, cells, :], ge_hbm.at[picture, cells, :], store_sem.at[picture, band])

    def last_start(picture):
        for copy in rim_of(picture, 1):
            copy.wait_recv()
        clear_outside(me, picture, ggrid, gsides_in, gcorners_in)
        column_stack(picture, gsides_in, gcorners_in, gcols)
        column_terms(picture, gcols, lambda a, c: weight(8 - 3 * a - c), terms)

    def last_bands(picture, begin, end):
        def do_band(band):
            def do_block(index):
                strip = band * 2 + index // LANE_BLOCKS
                lanes = times(lax.rem(index, LANE_BLOCKS), LANES)
                rows = ggrid[picture, pl.ds(strip * STRIP, STRIP + 2), :, lanes].astype(F32)
                total = convolve(
                    rows,
                    [weight(8 - n, lanes) for n in range(9)],
                    terms[0, picture, strip, 0:STRIP, lanes],
                    terms[1, picture, strip, 0:STRIP, lanes],
                )
                dg[picture, times(strip, STRIP_CELLS), lanes] = total.astype(BF16).reshape(STRIP_CELLS, LANES)

            loop(0, 2 * LANE_BLOCKS, do_block)
            store_copy(picture, band).start()

        loop(begin, end, do_band)

    last_start(0)
    ex_core.wait_recv()
    ex_b[q] = total_of(ex_a, 2).astype(BF16)
    others(4, q, lambda n: ey_copy(n).start())
    last_bands(0, 0, 2)
    gather(0)
    passed(ex_b.at[pl.ds(0, 3)], ey_sem.at[1])
    ex_c[chip] = total_of(ex_b, 4).astype(BF16)
    others(16, chip, lambda n: ez_copy(n).start())
    last_bands(0, 2, 4)
    last_start(1)
    last_bands(1, 0, 4)
    passed(ex_c.at[pl.ds(0, 15)], ez_sem.at[1])
    extra_out[...] = total_of(ex_c, 16)


    passed(got_cot.at[:, rest, :], cot_sem.at[0])
    for picture in range(2):
        passed(mix.at[picture, rest, :], mix_sem.at[0, picture])
        passed(back.at[picture, rest, :], back_send.at[picture])
    for turn in range(2):
        for picture in range(2):
            for copy in rim_of(picture, turn):
                copy.wait_send()
    ex_core.wait_send()
    passed(ex_b.at[pl.ds(0, 3)], ey_sem.at[0])
    passed(ex_c.at[pl.ds(0, 15)], ez_sem.at[0])
    gs_store.wait()
    for picture in range(2):
        for band in range(BANDS):
            store_copy(picture, band).wait()
    mate_copy(1).wait_recv()
    stores = [pltpu.make_async_copy(whole.at[half], whole_hbm.at[half], own_sem.at[4 + half]) for half in range(2)]
    stores[1].start()
    gather_core(0)
    for half in range(2):
        reduction_sent(half)
    mate_copy(0).wait_recv()
    stores[0].start()
    mate_copy(0).wait_send()
    mate_copy(1).wait_send()
    for copy in stores:
        copy.wait()


def my_tile():
    return lax.axis_index("row") * 32 + lax.axis_index("col")


def constants():
    perm = np.zeros((256, 256), np.float32)
    for a in range(16):
        for b in range(16):
            perm[a * 16 + b, b * 16 + a] = 1
    mask = np.kron(np.eye(4), np.ones((64, 32))).astype(np.float32)
    return jnp.asarray(perm, BF16), jnp.asarray(mask, BF16)


def whole_call(x, skip, cot, kern, wproj, gain, wqkv, wout):
    vmem = pl.BlockSpec(memory_space=pltpu.VMEM)
    anywhere = pl.BlockSpec(memory_space=pl.ANY)
    dma = pltpu.SemaphoreType.DMA

    def bf(*shape):
        return pltpu.VMEM(shape, BF16)

    def fl(*shape):
        return pltpu.VMEM(shape, F32)

    rims = [bf(2, 2, ROWS, EXPAND), bf(2, 2, ROWS, EXPAND), bf(2, 4, 16, EXPAND), bf(2, 4, 16, EXPAND)]
    return pl.pallas_call(
        whole_kernel,
        out_shape=(
            jax.ShapeDtypeStruct((2, CELLS, EXPAND), BF16),
            jax.ShapeDtypeStruct((2, CELLS, WIDTH), BF16),
            jax.ShapeDtypeStruct((2, 4, 2, 128, 256), BF16),
            jax.ShapeDtypeStruct((48, 256), F32),
        ),
        in_specs=[anywhere] * 3 + [vmem, anywhere, vmem] + [anywhere] * 4,
        out_specs=(anywhere, anywhere, anywhere, vmem),
        scratch_shapes=[
            bf(2, ROWS + 2, COLS, EXPAND), bf(2, ROWS + 2, COLS, EXPAND), bf(2, CELLS, EXPAND), bf(2, CELLS, EXPAND),
            bf(2, CELLS, WIDTH), bf(2, CELLS, WIDTH), bf(2, CELLS, WIDTH), bf(16, 64, WIDTH), bf(16, 64, WIDTH),
            bf(2, CELLS, WIDTH), bf(2, CELLS, WIDTH),
        ]
        + rims
        + [fl(2, 2, 48, EXPAND), fl(2, 2, 48, EXPAND), fl(2, 2, STRIPS, 8, EXPAND)]
        + rims
        + [
            fl(WIDTH, EXPAND), fl(16, EXPAND), fl(3 * WIDTH, WIDTH), fl(WIDTH, WIDTH), fl(1, WIDTH),
            bf(2, 4, 2, 128, 256), bf(2, 4, 128, 256), bf(2, 4, 128, 256),
            bf(2, TILES, 16, LANES), bf(2, 4, 2, 128, 256),
            bf(2, 48, 256), bf(4, 48, 256), bf(16, 48, 256),
            bf(2, CELLS, WIDTH), bf(EXPAND, WIDTH), bf(WIDTH, 3 * WIDTH), bf(WIDTH, WIDTH), bf(256, 256), bf(256, LANES),
            dma((2,)), dma((2, 2, 8)), dma((2, 2, 8)), dma((2,)), dma((2, 2)), dma((2,)), dma((2, BANDS)),
            dma((6,)), dma((2, BANDS)),
            dma((5,)), dma((5,)), dma((2, 2)), dma((2, 2)), dma((2,)), dma((2,)), dma((6,)),
        ],
        compiler_params=pltpu.CompilerParams(
            collective_id=0, has_side_effects=True, vmem_limit_bytes=56 * 2**20
        ),
        name="whole",
    )(x, skip, cot, kern, wproj, gain, wqkv, wout, *constants())


def finish_kernel(
    ge_hbm, gs_hbm, whole_hbm, extra_ref, ge_out, gs_out, gkern_out, gproj_out, gwqkv_out, gout_out, ggain_out,
    ge_held, gs_held, whole_ref, gproj, gwqkv, gout, sems, *, scale
):
    ways = [(whole_hbm, whole_ref, None)]
    for picture in range(2):
        for part in range(4):
            here = (picture, pl.ds(256 * part, 256))
            ways.append((ge_hbm.at[here], ge_held.at[here], ge_out.at[here]))
    ways.append((gs_hbm, gs_held, gs_out))
    inward = [pltpu.make_async_copy(a, b, sems.at[0, n]) for n, (a, b, _) in enumerate(ways)]
    outward = [pltpu.make_async_copy(b, c, sems.at[1, n]) for n, (_, b, c) in enumerate(ways) if n]
    results = [
        pltpu.make_async_copy(a, b, sems.at[1, len(ways) + n])
        for n, (a, b) in enumerate(((gproj, gproj_out), (gwqkv, gwqkv_out), (gout, gout_out)))
    ]
    for copy in inward:
        copy.start()
    for first, second in zip(inward[1:5], outward[:4]):
        first.wait()
        second.start()
    inward[0].wait()
    for n in range(8):
        block = whole_ref[n // 4, n % 4].reshape(256, 256).astype(F32) * scale
        if n < 4:
            gproj[256 * n : 256 * n + 256, :] = block
            some = extra_ref[9 * n : 9 * n + 9, :] * scale
            for row in range(3):
                gkern_out[row, :, 256 * n : 256 * n + 256] = some[3 * row : 3 * row + 3]
        elif n < 7:
            gwqkv[:, 256 * (n - 4) : 256 * (n - 4) + 256] = block
        else:
            gout[...] = block
    ggain_out[...] = extra_ref[36:37, :] * scale
    for copy in results:
        copy.start()
    for first, second in zip(inward[5:], outward[4:]):
        first.wait()
        second.start()
    for copy in outward + results:
        copy.wait()


def finish(ge, gs, whole, extra, scale):
    vmem = pl.BlockSpec(memory_space=pltpu.VMEM)
    anywhere = pl.BlockSpec(memory_space=pl.ANY)

    def kernel(*refs):
        finish_kernel(*refs, scale=scale)

    return pl.pallas_call(
        kernel,
        out_shape=(
            jax.ShapeDtypeStruct((2, CELLS, EXPAND), BF16),
            jax.ShapeDtypeStruct((2, CELLS, WIDTH), BF16),
            jax.ShapeDtypeStruct((3, 3, EXPAND), F32),
            jax.ShapeDtypeStruct((EXPAND, WIDTH), F32),
            jax.ShapeDtypeStruct((WIDTH, 3 * WIDTH), F32),
            jax.ShapeDtypeStruct((WIDTH, WIDTH), F32),
            jax.ShapeDtypeStruct((1, WIDTH), F32),
        ),
        in_specs=[anywhere, anywhere, anywhere, vmem],
        out_specs=(anywhere, anywhere, vmem, anywhere, anywhere, anywhere, vmem),
        scratch_shapes=[
            pltpu.VMEM((2, CELLS, EXPAND), BF16),
            pltpu.VMEM((2, CELLS, WIDTH), BF16),
            pltpu.VMEM((2, 4, 2, 128, 256), BF16),
            pltpu.VMEM((EXPAND, WIDTH), F32),
            pltpu.VMEM((WIDTH, 3 * WIDTH), F32),
            pltpu.VMEM((WIDTH, WIDTH), F32),
            pltpu.SemaphoreType.DMA((2, 13)),
        ],
        compiler_params=pltpu.CompilerParams(vmem_limit_bytes=60 * 2**20),
        name="finish",
    )(ge, gs, whole, extra)


def on_device(expanded, skip, cotangent, depth_kernel, w_proj, norm_gain, w_qkv, w_out):
    ge, gs, whole, extra = whole_call(
        expanded[:, 0],
        skip.reshape(2, CELLS, WIDTH),
        cotangent.reshape(2, CELLS, WIDTH),
        depth_kernel,
        w_proj,
        norm_gain.reshape(1, WIDTH),
        w_qkv,
        w_out,
    )
    scale = 1.0 / math.sqrt(2 * lax.axis_size("dp") * TILES * CELLS)
    ge, gs, gkern, gproj, gwqkv, gout, ggain = finish(ge, gs, whole, extra, scale)
    return (
        ge.reshape(2, 1, ROWS, COLS, EXPAND),
        gs.reshape(2, 1, ROWS, COLS, WIDTH),
        gkern,
        gproj,
        gwqkv,
        gout,
        ggain.reshape(WIDTH),
    )


def solution(mesh):
    tiled = P("dp", ("row", "col"), None, None, None)
    return jax.shard_map(
        on_device,
        mesh=mesh,
        in_specs=(tiled, tiled, tiled, P(), P(), P(), P(), P()),
        out_specs=(tiled, tiled, P(), P(), P(), P(), P()),
        check_vma=False,
    )
```
